32 devices in a mesh: dp: 4 (over z), tensor: 2 (over x), col: 4 (over y, core).
Axes of the slice: x: 2, y: 2, z: 4, core: 2. Of those that a mesh axis runs over, the one named last changes fastest.
Arguments:
- tokens: bfloat16 [512, 6144], P('dp', 'col'), may hold values from -6 to 6
- routes: int32 [512, 2], P('dp'), may hold values from 0 to 7, all different within a row; in each aligned block of 128 rows (0 to 127, 128 to 255, ...) at most 40 rows name the same one
- route_logits: float32 [512, 2], P('dp'), may hold values from -6 to 6
- kept_experts: int32 [6], replicated, may hold values from 0 to 7, as said below
- gate_weight: bfloat16 [65536, 6144], P(('dp', 'tensor'), 'col'), may hold values from -0.078125 to 0.078125
- up_weight: bfloat16 [65536, 6144], P(('dp', 'tensor'), 'col'), may hold values from -0.078125 to 0.078125
- down_weight: bfloat16 [65536, 3072], P(('dp', 'tensor'), 'col'), as said below
Outputs:
- token_error: float32 [512, 3072], P('dp', 'col')
The draws below stay inside these ranges and needn't reach their ends.
Inputs may be any that keep to these rules, and one draw needn't show every extreme that they name: Each token names two different experts. Among the tokens of one dp index (aligned blocks of 128 tokens) no expert is named by more than 40 routes, and in some block one expert is named by exactly 40. `kept_experts`: 6 different expert numbers. `down_weight`: entries lie between -6 / sqrt(8192) and 6 / sqrt(8192).
All inputs are finite; a program needn't handle non-finite values.
Results may differ from the reference program's by a relative error of at most 0.02.
Values may be sent and summed in bfloat16 or wider, within the bound.
No kernel may reach another device: no remote copies, remote signals or barrier semaphores. Data moves between devices by JAX's collectives and lax.ppermute only.
A program may use at most 192 MiB of HBM per device.

```python
import math
import jax
import jax.numpy as jnp
import numpy as np
from jax import lax

D = 6144
FF = 8192
COLS = 3072
E = 8
K = 6
ITERS = 2
TOK_DEV = 128
CAP = 40
TOKENS = 512
N_DP = 4
N_TENSOR = 2
N_COL = 4


def expert_order(key):
    return jax.random.permutation(jax.random.fold_in(key, 11), E)


def draw_kept_experts(key, part):
    return expert_order(key)[:K].astype(jnp.int32)


def draw_down_weight(key, part):
    order = expert_order(key)
    expert_ids = jnp.arange(E, dtype=jnp.int32)
    pruned = jnp.sum((order[K:][:, None] == expert_ids[None, :]).astype(jnp.float32), axis=0)
    expert_sign = 2.0 * pruned - 1.0
    slopes = jnp.array([-1.0, -1.0 / 3.0, 1.0 / 3.0, 1.0], jnp.float32)
    quarter_slope = jax.random.permutation(jax.random.fold_in(key, 23), slopes)
    levels = jnp.exp(1.2 * (quarter_slope[None, :] * expert_sign[:, None] - 1.0))
    noise_key = jax.random.fold_in(key, 37)
    shape = (E, FF, 4, COLS // 4)
    noise = jnp.clip(jax.random.normal(noise_key, shape, jnp.float32), -6.0, 6.0)
    values = noise * levels[:, None, :, None] * float(FF) ** (-0.5)
    return values.reshape(E * FF, COLS).astype(jnp.bfloat16)


def block_scale(key, dims, shards, least, largest):
    gain = 1.0
    for dim, parts in shards:
        steps = jax.random.uniform(jax.random.fold_in(jax.random.fold_in(key, 6), dim), (parts,), jnp.float32, least / len(shards), largest / len(shards))
        gain = gain * jnp.repeat(jnp.exp(steps), dims[dim] // parts).reshape((-1,) + (1,) * (len(dims) - 1 - dim))
    return gain


def deal_out(own_key, own, number, rows, number_of, top, most, lean):
    ranking = jax.random.permutation(own_key, number_of)
    crowded, ordinary = load_shares(number_of, rows * top, most, lean, True), load_shares(number_of, rows * top, most, lean, False)
    places = jnp.arange(number_of)

    def named(lengths, rotation):
        used = int((lengths > 0).sum())
        fixed = max(1, used // 4)
        moved = fixed + (places - fixed + rotation * (used - fixed)) % max(1, number_of - fixed)
        return jnp.zeros((number_of,), jnp.int32).at[ranking[jnp.where(places < fixed, places, moved)]].set(jnp.asarray(lengths, jnp.int32))

    lengths = jnp.where(number % 4 == 0, named(crowded, number // 4), named(ordinary, number - number // 4 - 1))
    mixed = jax.random.permutation(jax.random.fold_in(own, 3), number_of)
    source_of, sink = mixed[0:number_of // 2 * 2:2], mixed[1:number_of // 2 * 2:2]
    slack = jnp.minimum(lengths[source_of] - 1, most - lengths[sink]) // 2
    slack = jnp.where((source_of == ranking[0]) | (sink == ranking[0]) | (lengths[sink] == 0), 0, jnp.maximum(slack, 0))
    moved = jax.random.randint(jax.random.fold_in(own, 4), (number_of // 2,), 0, 1 << 20) % (slack + 1)
    lengths = lengths.at[source_of].add(-moved).at[sink].add(moved)
    items = jnp.searchsorted(jnp.cumsum(lengths), jnp.arange(rows * top), side="right").astype(jnp.int32)
    table = items.reshape(top, rows).T
    table = table[jax.random.permutation(jax.random.fold_in(own, 1), rows)]
    rotation = jax.random.randint(jax.random.fold_in(own, 2), (rows, 1), 0, top)
    return jnp.take_along_axis(table, (jnp.arange(top)[None, :] + rotation) % top, axis=1)


def load_shares(count, total, limit, slope, full):
    portions = [(1 << 20) // math.isqrt(grade ** slope) + 1 for grade in range(1, count + 1)]
    largest = limit if full else min(limit, max(-(-total // count), total * portions[0] // sum(portions)))
    least = 1 if total - largest >= count - 1 else 0
    counts, surplus = [largest] + [least] * (count - 1), total - largest - least * (count - 1)
    while surplus > 0:
        movable = [i for i in range(1, count) if counts[i] < largest] or [i for i in range(1, count) if counts[i] < limit]
        whole, budget = sum([portions[i] for i in movable]), surplus
        for i in movable:
            extra = min(limit - counts[i], max(1, budget * portions[i] // whole), surplus)
            counts[i] = counts[i] + extra
            surplus = surplus - extra
    return np.array(counts)


def bell_draw(stream_key, extent, deviation, bound, split=(), held_as=jnp.bfloat16):
    loudness = block_scale(stream_key, extent, split, -0.22, 0.18) if split else 1.0
    entries = jax.random.normal(stream_key, extent, jnp.float32) * deviation * loudness
    return jnp.minimum(jnp.maximum(entries, -bound), bound).astype(held_as)


def setup_inputs(seed: int = 0) -> dict:
    keys = jax.random.split(jax.random.key(seed), 8)
    tokens = bell_draw(keys[0], (TOKENS, D), 1.0, 6.0, ((0, 4), (1, 4)))
    routes_keys = jax.random.split(jax.random.fold_in(keys[1], 1), TOKENS // TOK_DEV)
    routes_turns = jax.random.permutation(jax.random.fold_in(keys[1], 3), TOKENS // TOK_DEV)
    routes = jax.vmap(lambda own, number: deal_out(jax.random.fold_in(keys[1], 2), own, number, TOK_DEV, E, 2, CAP, 1))(routes_keys, routes_turns).reshape((TOKENS, 2))
    route_logits = bell_draw(keys[2], (TOKENS, 2), 1.5, 6.0, ((0, 4),), jnp.float32)
    kept_experts = draw_kept_experts(jax.random.fold_in(keys[7], 71), 0)
    gate_weight = bell_draw(keys[4], (E * FF, D), D ** -0.5, 0.078125, ((0, 8), (1, 4)))
    up_weight = bell_draw(keys[5], (E * FF, D), D ** -0.5, 0.078125, ((0, 8), (1, 4)))
    down_weight = draw_down_weight(jax.random.fold_in(keys[7], 71), 0)
    return {"tokens": tokens, "routes": routes, "route_logits": route_logits, "kept_experts": kept_experts, "gate_weight": gate_weight, "up_weight": up_weight, "down_weight": down_weight}


ridge_share = 0.25
top_precision = lax.Precision.HIGHEST


def rounded_sum(terms):
    low = lax.optimization_barrier(terms.astype(jnp.bfloat16))
    return jnp.sum(low.astype(jnp.float32), axis=1)


def reference(tokens, routes, route_logits, kept_experts, gate_weight, up_weight, down_weight):
    slot_count = N_DP * CAP
    piece_rows = E * FF // (N_DP * N_TENSOR)
    pieces = FF // piece_rows
    expert_ids = jnp.arange(E, dtype=jnp.int32)
    kept_table = jnp.any(kept_experts[:, None] == expert_ids[None, :], axis=0).astype(jnp.float32)
    block_routes = routes.reshape(N_DP, TOK_DEV * 2)
    route_onehot = (block_routes[:, :, None] == expert_ids[None, None, :]).astype(jnp.int32)
    route_rank = jnp.sum((jnp.cumsum(route_onehot, axis=1) - route_onehot) * route_onehot, axis=2)
    block_ids = jnp.arange(N_DP, dtype=jnp.int32)[:, None]
    global_slot = (block_routes * slot_count + block_ids * CAP + route_rank).reshape(-1).astype(jnp.int32)
    token_ids = (jnp.arange(TOKENS * 2, dtype=jnp.int32) // 2).astype(jnp.int32)
    gate_probs = jax.nn.softmax(route_logits.astype(jnp.float32), axis=-1).reshape(-1)
    route_kept = kept_table[routes.reshape(-1)]
    total_slots = E * slot_count
    source = jnp.zeros((total_slots,), jnp.int32).at[global_slot].set(token_ids)
    filled = jnp.zeros((total_slots,), jnp.float32).at[global_slot].set(1.0)
    kept_gate = jnp.zeros((total_slots,), jnp.float32).at[global_slot].set(gate_probs * route_kept)
    dropped_gate = jnp.zeros((total_slots,), jnp.float32).at[global_slot].set(gate_probs * (1.0 - route_kept))
    gate_all = gate_weight.reshape(E, FF, D)
    up_all = up_weight.reshape(E, FF, D)
    down_all = down_weight.reshape(E, FF, COLS)

    def expert_forward(expert):
        rows = lax.dynamic_slice_in_dim(source, expert * slot_count, slot_count)
        live = lax.dynamic_slice_in_dim(filled, expert * slot_count, slot_count)
        inputs = jnp.where(live[:, None] > 0, tokens[rows], jnp.zeros((), tokens.dtype))
        blocks = inputs.astype(jnp.float32).reshape(slot_count, N_COL, D // N_COL)
        gate_rows = lax.dynamic_index_in_dim(gate_all, expert, 0, keepdims=False).astype(jnp.float32)
        up_rows = lax.dynamic_index_in_dim(up_all, expert, 0, keepdims=False).astype(jnp.float32)
        gate_terms = jnp.einsum("snd,fnd->snf", blocks, gate_rows.reshape(FF, N_COL, D // N_COL), precision=top_precision)
        gate_sum = rounded_sum(gate_terms)
        up_terms = jnp.einsum("snd,fnd->snf", blocks, up_rows.reshape(FF, N_COL, D // N_COL), precision=top_precision)
        up_sum = rounded_sum(up_terms)
        hidden = (jax.nn.silu(gate_sum) * up_sum).astype(jnp.bfloat16)
        down_rows = lax.dynamic_index_in_dim(down_all, expert, 0, keepdims=False).astype(jnp.float32)
        down_terms = jnp.einsum("snr,nrc->snc", hidden.astype(jnp.float32).reshape(slot_count, pieces, piece_rows), down_rows.reshape(pieces, piece_rows, COLS), precision=top_precision)
        return hidden, rounded_sum(down_terms)

    hidden_all, out_all = lax.map(expert_forward, expert_ids)
    dropped = jnp.zeros((TOKENS, COLS), jnp.float32).at[source].add(dropped_gate[:, None] * out_all.reshape(total_slots, COLS))

    def apply_forward(direction):
        def one_expert(pair):
            return jnp.dot(pair[0].astype(jnp.float32), pair[1], precision=top_precision)

        slot_values = lax.map(one_expert, (hidden_all, direction)).reshape(total_slots, COLS)
        return jnp.zeros((TOKENS, COLS), jnp.float32).at[source].add(kept_gate[:, None] * slot_values)

    def apply_backward(image_tokens):
        slot_values = (kept_gate[:, None] * image_tokens[source]).reshape(E, slot_count, COLS)

        def one_expert(pair):
            return jnp.dot(pair[0].astype(jnp.float32).T, pair[1], precision=top_precision)

        return lax.map(one_expert, (hidden_all, slot_values))

    ridge_weight = ridge_share * 2.0 * TOKENS / E
    base_down = down_all.astype(jnp.float32)
    residual = apply_backward(dropped) - ridge_weight * kept_table[:, None, None] * base_down
    res_norm = jnp.sum(residual * residual)
    direction = residual
    leftover = dropped
    for turn_index in range(ITERS):
        image_tokens = apply_forward(direction)
        curvature = jnp.sum(image_tokens * image_tokens) + ridge_weight * jnp.sum(direction * direction)
        step_size = res_norm / curvature
        leftover = leftover - step_size * image_tokens
        if turn_index + 1 < ITERS:
            curved = apply_backward(image_tokens) + ridge_weight * direction
            residual = residual - step_size * curved
            next_norm = jnp.sum(residual * residual)
            direction = residual + (next_norm / res_norm) * direction
            res_norm = next_norm
    return leftover
```

```python
import functools

import jax
import jax.numpy as jnp
from jax import lax
from jax.experimental import pallas as pl
from jax.experimental.pallas import tpu as pltpu
from jax.sharding import PartitionSpec as P

E = 8
ITERS = 2
CAP = 40
CHUNKS = 4


ridge_share = 0.25
top_precision = lax.Precision.HIGHEST
MIB = 1024 * 1024
f32 = jnp.float32
bf16 = jnp.bfloat16
NT = (((1,), (1,)), ((), ()))
NN = (((1,), (0,)), ((), ()))
TN = (((0,), (0,)), ((), ()))


def whole():
    return pl.BlockSpec(memory_space=pltpu.VMEM)


def scalars():
    return pl.BlockSpec(memory_space=pltpu.SMEM)


def mm(left, right, contract=NN):
    return lax.dot_general(left, right, contract, preferred_element_type=f32)


def split_wide(values):
    high = values.astype(bf16)
    low = (values - high.astype(f32)).astype(bf16)
    return jnp.concatenate([high, low], axis=1)


def mm_wide(left, right, contract=NN):
    lanes = right.shape[1]
    both = mm(left, split_wide(right), contract)
    return both[:, :lanes] + both[:, lanes:]


def params(mib):
    return pltpu.CompilerParams(vmem_limit_bytes=mib * MIB)


def block_slots(first, second):
    count = first.shape[1]
    expert_rows = lax.broadcasted_iota(jnp.int32, (E, count), 0).astype(f32)
    hot_first = (expert_rows == first).astype(f32)
    hot_second = (expert_rows == second).astype(f32)
    before = (
        lax.broadcasted_iota(jnp.int32, (count, count), 0)
        < lax.broadcasted_iota(jnp.int32, (count, count), 1)
    ).astype(bf16)
    place = mm((hot_first + hot_second).astype(bf16), before)
    ranked_first = jnp.sum(hot_first * place, axis=0, keepdims=True)
    ranked_second = jnp.sum(hot_second * place, axis=0, keepdims=True)
    return ranked_first, ranked_second


def pick_kernel(parts, tensor_count, own_ref, info_ref, tokens_ref, out_ref):
    first, second = info_ref[0:1, :], info_ref[1:2, :]
    rank_first, rank_second = block_slots(first, second)
    own = own_ref[0]
    count = first.shape[1]
    rows = lax.broadcasted_iota(jnp.int32, (CAP, count), 0).astype(f32)
    values = tokens_ref[...]
    for part in range(parts):
        expert = (part * tensor_count + own).astype(f32)
        hit = ((first == expert) & (rank_first == rows)) | ((second == expert) & (rank_second == rows))
        out_ref[part] = mm(hit.astype(f32).astype(bf16), values).astype(bf16)


def gate_up_kernel(order_ref, inputs_ref, gate_ref, up_ref, send_ref, keep_ref):
    step = pl.program_id(0)
    values = inputs_ref[...]
    gate = mm(values, gate_ref[...], NT).astype(bf16)
    up = mm(values, up_ref[...], NT).astype(bf16)

    @pl.when(step < 2)
    def _():
        send_ref[0, 0] = gate
        send_ref[0, 1] = up

    @pl.when(step >= 2)
    def _():
        keep_ref[0, 0] = gate
        keep_ref[0, 1] = up


def gate_up(order, inputs, gate_weight, up_weight, chunk, width):
    slots, depth = inputs.shape
    weight_spec = pl.BlockSpec((width, depth), lambda s, order: (order[s] * CHUNKS + chunk, 0))
    shape = jax.ShapeDtypeStruct((2, 2, slots, width), bf16)
    return pl.pallas_call(
        gate_up_kernel,
        grid_spec=pltpu.PrefetchScalarGridSpec(
            num_scalar_prefetch=1,
            grid=(4,),
            in_specs=[
                pl.BlockSpec((slots, depth), lambda s, order: (0, 0)),
                weight_spec,
                weight_spec,
            ],
            out_specs=[
                pl.BlockSpec((1, 2, slots, width), lambda s, order: (jnp.minimum(s, 1), 0, 0, 0)),
                pl.BlockSpec((1, 2, slots, width), lambda s, order: (jnp.maximum(s - 2, 0), 0, 0, 0)),
            ],
        ),
        out_shape=[shape, shape],
        compiler_params=params(20),
        cost_estimate=pl.CostEstimate(
            flops=16 * slots * depth * width, bytes_accessed=16 * width * depth, transcendentals=0
        ),
        name=f"gate_up_{chunk}",
    )(order, inputs, gate_weight, up_weight)


def down_kernel(order_ref, own_ref, across_ref, beside_ref, both_ref, down_ref, *rest):
    refs = (own_ref, across_ref, beside_ref, both_ref)
    if len(rest) == 4:
        old_out_ref, old_gram_ref, out_ref, gram_ref = rest
    else:
        out_ref, gram_ref = rest
    for step, ref in enumerate(refs):

        @pl.when(pl.program_id(0) == step)
        def _(step=step, ref=ref):
            values = ref[...]
            out = mm(values, down_ref[...])
            gram = mm(values, values, NT)
            if step:
                out_ref[...] += out
                gram_ref[...] += gram
            elif len(rest) == 4:
                out_ref[...] = old_out_ref[...] + out
                gram_ref[...] = old_gram_ref[...] + gram
            else:
                out_ref[...] = out
                gram_ref[...] = gram


def down(order, pieces, down_weight, chunk, older):
    slots, width = pieces[0].shape
    columns = down_weight.shape[1]

    def fixed(shape):
        return pl.BlockSpec(shape, lambda s, order: (0,) * len(shape))

    return pl.pallas_call(
        down_kernel,
        grid_spec=pltpu.PrefetchScalarGridSpec(
            num_scalar_prefetch=1,
            grid=(4,),
            in_specs=[fixed((slots, width))] * 4
            + [pl.BlockSpec((width, columns), lambda s, order: (order[s] * CHUNKS + chunk, 0))]
            + [fixed(value.shape) for value in older],
            out_specs=[fixed((slots, columns)), fixed((slots, slots))],
        ),
        out_shape=[
            jax.ShapeDtypeStruct((slots, columns), f32),
            jax.ShapeDtypeStruct((slots, slots), f32),
        ],
        compiler_params=params(20),
        cost_estimate=pl.CostEstimate(
            flops=8 * slots * width * (columns + slots),
            bytes_accessed=8 * width * columns,
            transcendentals=0,
        ),
        name=f"down_{chunk}",
    )(order, *pieces, down_weight, *older)


def pack_kernel(parts, out_ref, gram_ref, packed_ref):
    gram = gram_ref[...]
    wide = out_ref.shape[1] // parts
    for part in range(parts):
        piece = out_ref[:, part * wide : (part + 1) * wide]
        packed_ref[part] = jnp.concatenate([gram, piece], axis=1).astype(bf16)


def route_kernel(blocks, kept_ref, info_ref, hot_ref, gates_ref):
    count = info_ref.shape[2]
    slots = blocks * CAP
    zero = jnp.zeros((CAP, count), f32)
    rows = lax.broadcasted_iota(jnp.int32, (CAP, count), 0).astype(f32)
    for block in range(blocks):
        first, second = info_ref[block, 0:1, :], info_ref[block, 1:2, :]
        delta = info_ref[block, 3:4, :] - info_ref[block, 2:3, :]
        share_first = 1.0 / (1.0 + jnp.exp(delta))
        share_second = 1.0 / (1.0 + jnp.exp(-delta))
        rank_first, rank_second = block_slots(first, second)
        for expert in range(E):
            kept = jnp.zeros((), jnp.bool_)
            for place in range(kept_ref.shape[0]):
                kept = kept | (kept_ref[place] == expert)
            kept = kept.astype(f32)
            hit_first = (first == expert) & (rank_first == rows)
            hit_second = (second == expert) & (rank_second == rows)
            gate = jnp.sum(
                jnp.where(hit_first, share_first, zero) + jnp.where(hit_second, share_second, zero),
                axis=1,
                keepdims=True,
            )
            hot = (hit_first | hit_second).astype(f32)
            row = expert * slots + block * CAP
            for other in range(blocks):
                hot_ref[row : row + CAP, other * count : (other + 1) * count] = hot if other == block else zero
            gates_ref[row : row + CAP, 0:1] = gate * kept
            gates_ref[row : row + CAP, 1:2] = gate * (1.0 - kept)


def solve_kernel(ridge, slots, packed_ref, hot_ref, gates_ref, square_ref, base_ref, zero_ref, one_ref, sums_ref):
    hot = hot_ref[...].astype(bf16)
    kept, dropped = gates_ref[:, 0:1], gates_ref[:, 1:2]
    values = jnp.concatenate([packed_ref[e][:, slots:].astype(f32) for e in range(E)], axis=0)
    base = mm_wide(hot, dropped * values, TN)
    output = mm_wide(hot, kept * values, TN)

    def apply(field):
        spread = kept * mm_wide(hot, field)
        mixed = jnp.concatenate(
            [
                mm_wide(packed_ref[e][:, :slots], spread[e * slots : (e + 1) * slots])
                for e in range(E)
            ],
            axis=0,
        )
        return mm_wide(hot, kept * mixed, TN)

    curved = apply(base)
    zero = curved - ridge * output
    one = apply(zero)
    base_ref[...] = base
    zero_ref[...] = zero
    one_ref[...] = one
    norm = jnp.sum(base * curved) - 2.0 * ridge * jnp.sum(base * output)
    sums_ref[0:1, :] = jnp.full((1, sums_ref.shape[1]), norm, f32) + ridge * ridge * square_ref[0]
    sums_ref[1:2, :] = jnp.full((1, sums_ref.shape[1]), jnp.sum(zero * zero), f32)
    sums_ref[2:3, :] = jnp.full((1, sums_ref.shape[1]), jnp.sum(zero * one), f32)
    sums_ref[3:4, :] = jnp.full((1, sums_ref.shape[1]), jnp.sum(one * one), f32)
    sums_ref[4:8, :] = jnp.zeros((4, sums_ref.shape[1]), f32)


def finish_kernel(ridge, blocks, copies, base_ref, zero_ref, one_ref, sums_ref, out_ref):
    norm = sums_ref[0:1, 0:1]
    zero_zero = sums_ref[1:2, 0:1]
    zero_one = sums_ref[2:3, 0:1]
    one_one = sums_ref[3:4, 0:1]
    step = norm / (zero_zero + ridge * norm)
    left = 1.0 - step * ridge
    new = left * left * norm - 2.0 * left * step * zero_zero + step * step * zero_one
    ratio = new / norm
    grown = left + ratio
    image = grown * grown * zero_zero - 2.0 * grown * step * zero_one + step * step * one_one
    later = new / (image + ridge * (new + ratio * ratio * norm))
    field = base_ref[...] - (step + later * grown) * zero_ref[...] + (later * step) * one_ref[...]
    rows = field.shape[0] // blocks
    for block in range(blocks):
        piece = field[block * rows : (block + 1) * rows].astype(bf16)
        for copy in range(copies):
            out_ref[block * copies + copy] = piece


def join_kernel(pieces_ref, out_ref):
    out_ref[...] = jnp.concatenate(
        [pieces_ref[part].astype(f32) for part in range(pieces_ref.shape[0])], axis=1
    )


def single(kernel, out_shape, in_specs, mib, name):
    many = isinstance(out_shape, list)
    return pl.pallas_call(
        kernel,
        out_shape=out_shape,
        in_specs=in_specs,
        out_specs=[whole()] * len(out_shape) if many else whole(),
        compiler_params=params(mib),
        name=name,
    )


def one_expert_each(tokens, routes, route_logits, kept_experts, gate_weight, up_weight, down_weight):
    dp_count = lax.axis_size("dp")
    tensor_count = lax.axis_size("tensor")
    parts = dp_count * tensor_count
    tok_rows, depth = tokens.shape
    units, columns = down_weight.shape
    slots = dp_count * CAP
    lanes = columns // parts
    width = units // 4 // CHUNKS
    ridge = ridge_share * 2.0 * tok_rows * dp_count / E
    tensor_index = lax.axis_index("tensor")
    col_index = lax.axis_index("col")
    own_expert = lax.axis_index("dp") * tensor_count + tensor_index

    def beside(values):
        return lax.ppermute(values, "col", [(k, k ^ 1) for k in range(4)])

    def across(values):
        return lax.ppermute(values, "col", [(k, k ^ 2) for k in range(4)])

    info = jnp.concatenate([routes.astype(f32).T, route_logits.T], axis=0)
    all_info = lax.all_gather(info, "dp")
    hot, gates = single(
        functools.partial(route_kernel, dp_count),
        [
            jax.ShapeDtypeStruct((E * slots, dp_count * tok_rows), f32),
            jax.ShapeDtypeStruct((E * slots, 2), f32),
        ],
        [scalars(), whole()],
        16,
        "route",
    )(kept_experts, all_info)

    picked = single(
        functools.partial(pick_kernel, dp_count, tensor_count),
        jax.ShapeDtypeStruct((dp_count, CAP, depth), bf16),
        [scalars(), whole(), whole()],
        16,
        "pick",
    )(tensor_index.reshape(1), info, tokens)
    arrived = lax.all_to_all(picked, "dp", split_axis=0, concat_axis=0, tiled=True)
    inputs = arrived.reshape(slots, depth)

    gate_order = col_index ^ jnp.array([3, 1, 2, 0], jnp.int32)
    down_order = col_index ^ jnp.array([0, 2, 1, 3], jnp.int32)
    older = ()
    for chunk in range(CHUNKS):
        send, keep = gate_up(gate_order, inputs, gate_weight, up_weight, chunk, width)
        near = beside(send)
        pair = keep.astype(f32) + near.astype(f32)
        far = across(pair[0].astype(bf16))
        total = pair[1] + far.astype(f32)
        own = (jax.nn.silu(total[0]) * total[1]).astype(bf16)
        other = across(own)
        older = down(down_order, (own, other, beside(own), beside(other)), down_weight, chunk, older)

    is_kept = jnp.any(kept_experts == own_expert).astype(f32)
    wide_down = down_weight.astype(f32)
    square = (is_kept * jnp.sum(wide_down * wide_down)).reshape(1)

    packed = single(
        functools.partial(pack_kernel, parts),
        jax.ShapeDtypeStruct((parts, slots, slots + lanes), bf16),
        [whole(), whole()],
        16,
        "pack",
    )(*older)
    spread = lax.all_to_all(packed, ("dp", "tensor"), split_axis=0, concat_axis=0, tiled=True)

    field = jax.ShapeDtypeStruct((dp_count * tok_rows, lanes), f32)
    base, zero, one, sums = single(
        functools.partial(solve_kernel, ridge, slots),
        [field, field, field, jax.ShapeDtypeStruct((8, 128), f32)],
        [whole(), whole(), whole(), scalars()],
        40,
        "solve",
    )(spread, hot, gates, square)

    for axis, size in (("col", 4), ("tensor", tensor_count), ("dp", dp_count)):
        shifted = [
            lax.ppermute(sums, axis, [(k, (k + step) % size) for k in range(size)])
            for step in range(1, size)
        ]
        for value in shifted:
            sums = sums + value

    home = single(
        functools.partial(finish_kernel, ridge, dp_count, tensor_count),
        jax.ShapeDtypeStruct((parts, tok_rows, lanes), bf16),
        [whole()] * 4,
        16,
        "finish",
    )(base, zero, one, sums)
    pieces = lax.all_to_all(home, ("dp", "tensor"), split_axis=0, concat_axis=0, tiled=True)
    return single(
        join_kernel,
        jax.ShapeDtypeStruct((tok_rows, columns), f32),
        [whole()],
        16,
        "join",
    )(pieces)


def spread_copies(values, experts, held_count, copies):
    old_shape = values.shape
    grouped = values.reshape((experts // held_count, 1, held_count) + old_shape[1:])
    widened = jnp.broadcast_to(grouped, (experts // held_count, copies, held_count) + old_shape[1:])
    return widened.reshape((experts // held_count * copies, held_count) + old_shape[1:])


def expert_major(returned, experts, held_count, copies):
    old_shape = returned.shape
    grouped = returned.reshape((experts // held_count, copies, held_count) + old_shape[2:])
    merged = jnp.sum(grouped, axis=1)
    return merged.reshape((experts * old_shape[2],) + old_shape[3:])


def exact_product(left, right, contract):
    return lax.dot_general(
        left, right, contract, precision=top_precision, preferred_element_type=jnp.float32
    )


def general(tokens, routes, route_logits, kept_experts, gate_weight, up_weight, down_weight):
    dp_count = lax.axis_size("dp")
    tensor_count = lax.axis_size("tensor")
    held_count = max(1, E // dp_count)
    copies = max(1, dp_count // E)
    tok_rows = tokens.shape[0]
    piece_rows = gate_weight.shape[0]
    FF = piece_rows * dp_count * tensor_count // E
    slot_total = E * CAP
    device_rank = lax.axis_index("dp") * tensor_count + lax.axis_index("tensor")
    own_expert = device_rank * piece_rows // FF
    own_group = own_expert % held_count
    expert_ids = jnp.arange(E, dtype=jnp.int32)
    kept_table = jnp.any(kept_experts[:, None] == expert_ids[None, :], axis=0).astype(jnp.float32)
    own_kept = jnp.sum(jnp.where(expert_ids == own_expert, kept_table, 0.0))
    route_experts = routes.reshape(-1)
    route_onehot = (route_experts[:, None] == expert_ids[None, :]).astype(jnp.int32)
    route_rank = jnp.sum((jnp.cumsum(route_onehot, axis=0) - route_onehot) * route_onehot, axis=1)
    route_slot = route_experts * CAP + route_rank
    gate_probs = jax.nn.softmax(route_logits, axis=-1).reshape(-1)
    route_kept = jnp.sum(route_onehot.astype(jnp.float32) * kept_table[None, :], axis=1)
    slot_match = (jnp.arange(slot_total, dtype=jnp.int32)[:, None] == route_slot[None, :]).astype(
        jnp.float32
    )
    pick_tokens = slot_match.reshape(slot_total, tok_rows, 2).sum(axis=2)
    kept_weights = (
        (slot_match * (gate_probs * route_kept)[None, :])
        .reshape(slot_total, tok_rows, 2)
        .sum(axis=2)
    )
    dropped_weights = (
        (slot_match * (gate_probs * (1.0 - route_kept))[None, :])
        .reshape(slot_total, tok_rows, 2)
        .sum(axis=2)
    )
    by_expert = jnp.dot(
        pick_tokens.astype(jnp.bfloat16), tokens, preferred_element_type=jnp.float32
    ).astype(jnp.bfloat16)
    outgoing = spread_copies(by_expert.reshape(E, CAP, -1), E, held_count, copies)
    chosen = lax.dynamic_index_in_dim(
        lax.all_to_all(outgoing, "dp", split_axis=0, concat_axis=0, tiled=True),
        own_group,
        1,
        keepdims=False,
    )
    contract = (((2,), (1,)), ((), ()))
    gate_part = lax.dot_general(chosen, gate_weight, contract, preferred_element_type=jnp.float32)
    up_part = lax.dot_general(chosen, up_weight, contract, preferred_element_type=jnp.float32)
    gate_part, up_part = (gate_part, up_part)
    gate_sum, up_sum = (
        lax.psum(gate_part.astype(jnp.bfloat16), "col").astype(jnp.float32),
        lax.psum(up_part.astype(jnp.bfloat16), "col").astype(jnp.float32),
    )
    hidden = (jax.nn.silu(gate_sum) * up_sum).astype(jnp.bfloat16)
    expert_out = lax.dot_general(
        hidden, down_weight, (((2,), (0,)), ((), ())), preferred_element_type=jnp.float32
    ).astype(jnp.bfloat16)
    hidden_wide = hidden.astype(jnp.float32)
    group_mask = (jnp.arange(held_count) == own_group)[None, :, None, None]
    placed = jnp.where(group_mask, expert_out[:, None], jnp.zeros((), jnp.bfloat16))
    returned = lax.all_to_all(placed, "dp", split_axis=0, concat_axis=0, tiled=True)
    slot_values = expert_major(returned.astype(jnp.float32), E, held_count, copies)
    dropped_part = jnp.dot(dropped_weights.T, slot_values, precision=top_precision)
    dropped = lax.psum(dropped_part, "tensor")
    ridge_weight = ridge_share * 2.0 * tok_rows * dp_count / E

    def apply_backward(image_tokens):
        slot_image = jnp.dot(kept_weights, image_tokens, precision=top_precision)
        outgoing_image = spread_copies(slot_image.reshape(E, CAP, -1), E, held_count, copies)
        arrived = lax.all_to_all(outgoing_image, "dp", split_axis=0, concat_axis=0, tiled=True)
        chosen = lax.dynamic_index_in_dim(arrived, own_group, 1, keepdims=False)
        return exact_product(hidden_wide, chosen, (((0, 1), (0, 1)), ((), ())))

    def total_norm(values):
        return lax.psum(jnp.sum(values * values), ("dp", "tensor", "col"))

    base_down = down_weight.astype(jnp.float32)
    residual = apply_backward(dropped) - ridge_weight * own_kept * base_down
    res_norm = total_norm(residual)
    direction = residual
    leftover = dropped
    for turn_index in range(ITERS):
        slot_part = exact_product(hidden_wide, direction, (((2,), (0,)), ((), ())))
        placed_part = jnp.where(group_mask, slot_part[:, None], 0.0)
        came_back = lax.all_to_all(placed_part, "dp", split_axis=0, concat_axis=0, tiled=True)
        image_part = jnp.dot(
            kept_weights.T, expert_major(came_back, E, held_count, copies), precision=top_precision
        )
        image_tokens = lax.psum(image_part, "tensor")
        first_copy = (lax.axis_index("tensor") == 0).astype(jnp.float32)
        local_term = first_copy * jnp.sum(image_tokens * image_tokens) + ridge_weight * jnp.sum(
            direction * direction
        )
        curvature = lax.psum(local_term, ("dp", "tensor", "col"))
        step_size = res_norm / curvature
        leftover = leftover - step_size * image_tokens
        if turn_index + 1 < ITERS:
            curved = apply_backward(image_tokens) + ridge_weight * direction
            residual = residual - step_size * curved
            next_norm = total_norm(residual)
            direction = residual + next_norm / res_norm * direction
            res_norm = next_norm
    return leftover


def shards(*arrays):
    sizes = [lax.axis_size(axis) for axis in ("dp", "tensor", "col")]
    if sizes[0] * sizes[1] == E and sizes[2] == 4 and ITERS == 2:
        return one_expert_each(*arrays)
    return general(*arrays)


def solution(mesh):
    placed = (
        P("dp", "col"),
        P("dp", None),
        P("dp", None),
        P(),
        P(("dp", "tensor"), "col"),
        P(("dp", "tensor"), "col"),
        P(("dp", "tensor"), "col"),
    )
    return jax.shard_map(
        shards, mesh=mesh, in_specs=placed, out_specs=P("dp", "col"), check_vma=False
    )
```

```python
import functools

import jax
import jax.numpy as jnp
from jax import lax
from jax.experimental import pallas as pl
from jax.experimental.pallas import tpu as pltpu
from jax.sharding import PartitionSpec as P

E = 8
ITERS = 2
CAP = 40


ridge_share = 0.25
top_precision = lax.Precision.HIGHEST
MIB = 1024 * 1024
LIGHT = pl.CostEstimate(flops=1, bytes_accessed=1, transcendentals=0)
f32 = jnp.float32
bf16 = jnp.bfloat16
NT = (((1,), (1,)), ((), ()))
NN = (((1,), (0,)), ((), ()))
TN = (((0,), (0,)), ((), ()))


def whole():
    return pl.BlockSpec(memory_space=pltpu.VMEM)


def scalars():
    return pl.BlockSpec(memory_space=pltpu.SMEM)


def mm(left, right, contract=NN):
    return lax.dot_general(left, right, contract, preferred_element_type=f32)


def split_wide(values):
    high = values.astype(bf16)
    low = (values - high.astype(f32)).astype(bf16)
    return jnp.concatenate([high, low], axis=1)


def mm_wide(left, right, contract=NN):
    lanes = right.shape[1]
    both = mm(left, split_wide(right), contract)
    return both[:, :lanes] + both[:, lanes:]


def params(mib):
    return pltpu.CompilerParams(vmem_limit_bytes=mib * MIB)


def block_slots(first, second):
    count = first.shape[1]
    expert_rows = lax.broadcasted_iota(jnp.int32, (E, count), 0).astype(f32)
    hot_first = (expert_rows == first).astype(f32)
    hot_second = (expert_rows == second).astype(f32)
    before = (
        lax.broadcasted_iota(jnp.int32, (count, count), 0)
        < lax.broadcasted_iota(jnp.int32, (count, count), 1)
    ).astype(bf16)
    place = mm((hot_first + hot_second).astype(bf16), before)
    ranked_first = jnp.sum(hot_first * place, axis=0, keepdims=True)
    ranked_second = jnp.sum(hot_second * place, axis=0, keepdims=True)
    return ranked_first, ranked_second


def pick_kernel(parts, tensor_count, place_ref, info_ref, tokens_ref, *out_refs):
    first, second = info_ref[0:1, :], info_ref[1:2, :]
    rank_first, rank_second = block_slots(first, second)
    count = first.shape[1]
    rows = lax.broadcasted_iota(jnp.int32, (CAP, count), 0).astype(f32)
    values = tokens_ref[...]
    for shift, out_ref in enumerate(out_refs):
        expert = (lax.rem(place_ref[0] + shift, parts) * tensor_count + place_ref[1]).astype(f32)
        hit = ((first == expert) & (rank_first == rows)) | ((second == expert) & (rank_second == rows))
        out_ref[...] = mm(hit.astype(f32).astype(bf16), values).astype(bf16)


def turn_kernel(*refs):
    pieces = refs[: (len(refs) - 1) // 2]
    rows = jnp.concatenate([ref[...].astype(f32) for ref in pieces], axis=0)
    refs[-1][...] = rows.T.astype(bf16)


def gate_up_kernel(order_ref, inputs_ref, gate_ref, up_ref, *rest):
    send_ref, keep_ref = rest[-2:]
    step = pl.program_id(0)
    values = inputs_ref[...]
    gate = mm(gate_ref[...], values).T.astype(bf16)
    up = mm(up_ref[...], values).T.astype(bf16)

    @pl.when(step < 2)
    def _():
        send_ref[0, 0] = gate
        send_ref[0, 1] = up

    @pl.when(step >= 2)
    def _():
        keep_ref[0, 0] = gate
        keep_ref[0, 1] = up


def gate_up(order, inputs, gate_weight, up_weight, width, at, after):
    depth, slots = inputs.shape
    quarter = gate_weight.shape[0] // 4
    gate_weight = gate_weight.reshape(4, quarter, depth)
    up_weight = up_weight.reshape(4, quarter, depth)
    weight_spec = pl.BlockSpec((None, width, depth), lambda s, order: (order[s], at // width, 0))
    shape = jax.ShapeDtypeStruct((2, 2, slots, width), bf16)
    return pl.pallas_call(
        gate_up_kernel,
        grid_spec=pltpu.PrefetchScalarGridSpec(
            num_scalar_prefetch=1,
            grid=(4,),
            in_specs=[
                pl.BlockSpec((depth, slots), lambda s, order: (0, 0)),
                weight_spec,
                weight_spec,
            ]
            + [pl.BlockSpec(memory_space=pl.ANY)] * len(after),
            out_specs=[
                pl.BlockSpec((1, 2, slots, width), lambda s, order: (jnp.minimum(s, 1), 0, 0, 0)),
                pl.BlockSpec((1, 2, slots, width), lambda s, order: (jnp.maximum(s - 2, 0), 0, 0, 0)),
            ],
        ),
        out_shape=[shape, shape],
        compiler_params=params(41),
        cost_estimate=LIGHT,
        name=f"gate_up_{at}",
    )(order, inputs, gate_weight, up_weight, *after)


def down_kernel(order_ref, own_ref, across_ref, beside_ref, both_ref, down_ref, *rest):
    pieces = (own_ref, across_ref, beside_ref, both_ref)
    old, new = rest[:-3], rest[-3:]
    step = pl.program_id(0)

    @pl.when(step == 0)
    def _():
        for index, ref in enumerate(new):
            ref[...] = old[index][...] if old else jnp.zeros_like(ref)

    out_ref, gram_ref, square_ref = new
    weight = down_ref[...]
    wide = weight.astype(f32)
    square_ref[...] += jnp.sum((wide * wide).reshape(-1, 8, wide.shape[1]), axis=0)
    for index, ref in enumerate(pieces):

        @pl.when(step == index)
        def _(ref=ref):
            values = ref[...]
            out_ref[...] += mm(values, weight)
            gram_ref[...] += mm(values, values, NT)


def down(order, pieces, down_weight, at, older):
    slots, width = pieces[0].shape
    columns = down_weight.shape[1]
    down_weight = down_weight.reshape(4, -1, columns)

    def fixed(shape):
        return pl.BlockSpec(shape, lambda s, order: (0,) * len(shape))

    shapes = [(slots, columns), (slots, slots), (8, columns)]
    return pl.pallas_call(
        down_kernel,
        grid_spec=pltpu.PrefetchScalarGridSpec(
            num_scalar_prefetch=1,
            grid=(4,),
            in_specs=[fixed((slots, width))] * 4
            + [
                pl.BlockSpec((None, width, columns), lambda s, order: (order[s], at // width, 0))
            ]
            + [fixed(value.shape) for value in older],
            out_specs=[fixed(shape) for shape in shapes],
        ),
        out_shape=[jax.ShapeDtypeStruct(shape, f32) for shape in shapes],
        compiler_params=params(20),
        cost_estimate=LIGHT,
        name=f"down_{at}",
    )(order, *pieces, down_weight, *older)


def pack_kernel(parts, out_ref, gram_ref, packed_ref):
    gram = gram_ref[...]
    wide = out_ref.shape[1] // parts
    for part in range(parts):
        piece = out_ref[:, part * wide : (part + 1) * wide]
        packed_ref[part] = jnp.concatenate([gram, piece], axis=1).astype(bf16)


def route_kernel(blocks, tensor_count, kept_ref, place_ref, *refs):
    infos = refs[:blocks]
    hot_ref, turned_ref, gates_ref, info_ref, wide_ref = refs[blocks:]
    for shift in range(blocks):
        info_ref[lax.rem(place_ref[0] + blocks - shift, blocks)] = infos[shift][...]
    count = info_ref.shape[2]
    slots = blocks * CAP
    zero = jnp.zeros((CAP, count), f32)
    rows = lax.broadcasted_iota(jnp.int32, (CAP, count), 0).astype(f32)
    for block in range(blocks):
        first, second = info_ref[block, 0:1, :], info_ref[block, 1:2, :]
        delta = info_ref[block, 3:4, :] - info_ref[block, 2:3, :]
        share_first = 1.0 / (1.0 + jnp.exp(delta))
        share_second = 1.0 / (1.0 + jnp.exp(-delta))
        rank_first, rank_second = block_slots(first, second)
        for expert in range(E):
            kept = jnp.zeros((), jnp.int32)
            for index in range(kept_ref.shape[0]):
                kept = kept | (kept_ref[index] == expert).astype(jnp.int32)
            kept = kept.astype(f32)
            hit_first = (first == expert) & (rank_first == rows)
            hit_second = (second == expert) & (rank_second == rows)
            gate = jnp.sum(
                jnp.where(hit_first, share_first, zero) + jnp.where(hit_second, share_second, zero),
                axis=1,
                keepdims=True,
            )
            row = expert * slots + (expert // tensor_count - block) % blocks * CAP
            for other in range(blocks):
                wide_ref[row : row + CAP, other * count : (other + 1) * count] = (
                    (hit_first | hit_second).astype(f32) if other == block else zero
                )
            gates_ref[row : row + CAP, 0:1] = gate * kept
            gates_ref[row : row + CAP, 1:2] = gate * (1.0 - kept)
    hot_ref[...] = wide_ref[...].astype(bf16)
    turned_ref[...] = wide_ref[...].T.astype(bf16)


def solve_kernel(ridge, slots, own_ref, packed_ref, hot_ref, turned_ref, gates_ref, square_ref, base_ref, zero_ref, one_ref, sums_ref):
    hot, turned = hot_ref[...], turned_ref[...]
    kept, dropped = gates_ref[:, 0:1], gates_ref[:, 1:2]
    values = jnp.concatenate([packed_ref[e][:, slots:].astype(f32) for e in range(E)], axis=0)
    base = mm_wide(turned, dropped * values)
    output = mm_wide(turned, kept * values)

    def apply(field):
        spread = kept * mm_wide(hot, field)
        mixed = jnp.concatenate(
            [
                mm_wide(packed_ref[e][:, :slots], spread[e * slots : (e + 1) * slots])
                for e in range(E)
            ],
            axis=0,
        )
        return mm_wide(turned, kept * mixed)

    curved = apply(base)
    zero = curved - ridge * output
    one = apply(zero)
    base_ref[...] = base
    zero_ref[...] = zero
    one_ref[...] = one
    norm = jnp.sum(base * (curved - 2.0 * ridge * output))
    square = jnp.sum(square_ref[...]) * own_ref[0]
    lane = lax.broadcasted_iota(jnp.int32, sums_ref.shape[1:], 1)
    sums = jnp.where(lane == 0, norm + ridge * ridge * square, 0.0)
    for index, value in enumerate((jnp.sum(zero * zero), jnp.sum(zero * one), jnp.sum(one * one))):
        sums = jnp.where(lane == index + 1, value, sums)
    for part in range(sums_ref.shape[0]):
        sums_ref[part] = sums


def finish_kernel(ridge, blocks, copies, base_ref, zero_ref, one_ref, sums_ref, out_ref):
    sums = jnp.sum(sums_ref[...], axis=0)[0:1, :]
    norm, zero_zero = sums[:, 0:1], sums[:, 1:2]
    zero_one, one_one = sums[:, 2:3], sums[:, 3:4]
    step = norm / (zero_zero + ridge * norm)
    left = 1.0 - step * ridge
    new = left * left * norm - 2.0 * left * step * zero_zero + step * step * zero_one
    ratio = new / norm
    grown = left + ratio
    image = grown * grown * zero_zero - 2.0 * grown * step * zero_one + step * step * one_one
    later = new / (image + ridge * (new + ratio * ratio * norm))
    field = base_ref[...] - (step + later * grown) * zero_ref[...] + (later * step) * one_ref[...]
    rows = field.shape[0] // blocks
    turned = field.T.astype(bf16)
    for block in range(blocks):
        for copy in range(copies):
            out_ref[block * copies + copy] = turned[:, block * rows : (block + 1) * rows]


def join_kernel(pieces_ref, out_ref):
    rows = jnp.concatenate([pieces_ref[part].astype(f32) for part in range(pieces_ref.shape[0])], axis=0)
    out_ref[...] = rows.T


def single(kernel, out_shape, in_specs, mib, name, scratch=()):
    many = isinstance(out_shape, list)
    return pl.pallas_call(
        kernel,
        out_shape=out_shape,
        in_specs=in_specs,
        out_specs=[whole()] * len(out_shape) if many else whole(),
        scratch_shapes=list(scratch),
        compiler_params=params(mib),
        cost_estimate=LIGHT,
        name=name,
    )


def one_expert_each(tokens, routes, route_logits, kept_experts, gate_weight, up_weight, down_weight):
    dp_count = lax.axis_size("dp")
    tensor_count = lax.axis_size("tensor")
    parts = dp_count * tensor_count
    tok_rows, depth = tokens.shape
    units, columns = down_weight.shape
    slots = dp_count * CAP
    lanes = columns // parts
    eighth = units // 32
    ridge = ridge_share * 2.0 * tok_rows * dp_count / E
    dp_index = lax.axis_index("dp")
    tensor_index = lax.axis_index("tensor")
    col_index = lax.axis_index("col")
    own_expert = dp_index * tensor_count + tensor_index
    place = jnp.stack([dp_index, tensor_index])

    def beside(values):
        return lax.ppermute(values, "col", [(k, k ^ 1) for k in range(4)])

    def across(values):
        return lax.ppermute(values, "col", [(k, k ^ 2) for k in range(4)])

    def ahead(values, shift):
        if shift == 0:
            return values
        return lax.ppermute(values, "dp", [(k, (k + shift) % dp_count) for k in range(dp_count)])

    info = jnp.concatenate([routes.astype(f32).T, route_logits.T], axis=0)
    picked = single(
        functools.partial(pick_kernel, dp_count, tensor_count),
        [jax.ShapeDtypeStruct((CAP, depth), bf16)] * dp_count,
        [scalars(), whole(), whole()],
        16,
        "pick",
    )(place, info, tokens)
    arrived = [ahead(value, shift) for shift, value in enumerate(picked)]
    infos = [ahead(info, shift) for shift in range(dp_count)]
    inputs = single(
        turn_kernel,
        jax.ShapeDtypeStruct((depth, slots), bf16),
        [whole()] * dp_count + [pl.BlockSpec(memory_space=pl.ANY)] * dp_count,
        16,
        "turn",
    )(*arrived, *infos)
    total_slots, total_tokens = E * slots, dp_count * tok_rows
    hot, turned, gates = single(
        functools.partial(route_kernel, dp_count, tensor_count),
        [
            jax.ShapeDtypeStruct((total_slots, total_tokens), bf16),
            jax.ShapeDtypeStruct((total_tokens, total_slots), bf16),
            jax.ShapeDtypeStruct((total_slots, 2), f32),
        ],
        [scalars(), scalars()] + [whole()] * dp_count,
        24,
        "route",
        [pltpu.VMEM((dp_count,) + info.shape, f32), pltpu.VMEM((total_slots, total_tokens), f32)],
    )(kept_experts, place, *infos)

    gate_order = col_index ^ jnp.array([3, 1, 2, 0], jnp.int32)
    down_order = col_index ^ jnp.array([0, 2, 1, 3], jnp.int32)
    plan = [(width * eighth, at * eighth) for width, at in ((1, 6), (2, 0), (2, 2), (2, 4), (1, 7))]
    last = len(plan) - 1
    keeps, pairs, sent = [], [], []
    for chunk, (width, at) in enumerate(plan):
        after = [pairs[chunk - 2], keeps[chunk - 1][0]] if chunk >= 2 else []
        send, keep = gate_up(gate_order, inputs, gate_weight, up_weight, width, at, after)
        near = beside(send)
        pairs.append((keep[0].astype(f32) + near[0].astype(f32)).astype(bf16))
        sent.append(across(pairs[-1]))
        keeps.append((keep, near))
    older, olders = (), []
    for chunk, (width, at) in enumerate(plan):
        first = [pairs[last]]
        if chunk == 1:
            first.append(gates)
        if chunk >= 2:
            first.append(olders[chunk - 2][2])
        far = lax.optimization_barrier((sent[chunk], *first))[0]
        keep, near = keeps[chunk]
        total = keep[1].astype(f32) + near[1].astype(f32) + far.astype(f32)
        own = (jax.nn.silu(total[0]) * total[1]).astype(bf16)
        other = across(own)
        older = down(down_order, (own, other, beside(own), beside(other)), down_weight, at, older)
        olders.append(older)

    packed = single(
        functools.partial(pack_kernel, parts),
        jax.ShapeDtypeStruct((parts, slots, slots + lanes), bf16),
        [whole(), whole()],
        16,
        "pack",
    )(*older[:2])
    spread = lax.all_to_all(packed, ("dp", "tensor"), split_axis=0, concat_axis=0, tiled=True)

    everyone = parts * lax.axis_size("col")
    is_kept = jnp.any(kept_experts == own_expert).astype(f32).reshape(1)
    field = jax.ShapeDtypeStruct((total_tokens, lanes), f32)
    base, zero, one, sums = single(
        functools.partial(solve_kernel, ridge, slots),
        [field, field, field, jax.ShapeDtypeStruct((everyone, 1, 128), f32)],
        [scalars()] + [whole()] * 5,
        40,
        "solve",
    )(is_kept, spread, hot, turned, gates, older[2])
    sums = lax.all_to_all(sums, ("dp", "tensor", "col"), split_axis=0, concat_axis=0, tiled=True)

    home = single(
        functools.partial(finish_kernel, ridge, dp_count, tensor_count),
        jax.ShapeDtypeStruct((parts, lanes, tok_rows), bf16),
        [whole()] * 4,
        16,
        "finish",
    )(base, zero, one, sums)
    pieces = lax.all_to_all(home, ("dp", "tensor"), split_axis=0, concat_axis=0, tiled=True)
    return single(
        join_kernel,
        jax.ShapeDtypeStruct((tok_rows, columns), f32),
        [whole()],
        16,
        "join",
    )(pieces)


def spread_copies(values, experts, held_count, copies):
    old_shape = values.shape
    grouped = values.reshape((experts // held_count, 1, held_count) + old_shape[1:])
    widened = jnp.broadcast_to(grouped, (experts // held_count, copies, held_count) + old_shape[1:])
    return widened.reshape((experts // held_count * copies, held_count) + old_shape[1:])


def expert_major(returned, experts, held_count, copies):
    old_shape = returned.shape
    grouped = returned.reshape((experts // held_count, copies, held_count) + old_shape[2:])
    merged = jnp.sum(grouped, axis=1)
    return merged.reshape((experts * old_shape[2],) + old_shape[3:])


def exact_product(left, right, contract):
    return lax.dot_general(
        left, right, contract, precision=top_precision, preferred_element_type=jnp.float32
    )


def general(tokens, routes, route_logits, kept_experts, gate_weight, up_weight, down_weight):
    dp_count = lax.axis_size("dp")
    tensor_count = lax.axis_size("tensor")
    held_count = max(1, E // dp_count)
    copies = max(1, dp_count // E)
    tok_rows = tokens.shape[0]
    piece_rows = gate_weight.shape[0]
    FF = piece_rows * dp_count * tensor_count // E
    slot_total = E * CAP
    device_rank = lax.axis_index("dp") * tensor_count + lax.axis_index("tensor")
    own_expert = device_rank * piece_rows // FF
    own_group = own_expert % held_count
    expert_ids = jnp.arange(E, dtype=jnp.int32)
    kept_table = jnp.any(kept_experts[:, None] == expert_ids[None, :], axis=0).astype(jnp.float32)
    own_kept = jnp.sum(jnp.where(expert_ids == own_expert, kept_table, 0.0))
    route_experts = routes.reshape(-1)
    route_onehot = (route_experts[:, None] == expert_ids[None, :]).astype(jnp.int32)
    route_rank = jnp.sum((jnp.cumsum(route_onehot, axis=0) - route_onehot) * route_onehot, axis=1)
    route_slot = route_experts * CAP + route_rank
    gate_probs = jax.nn.softmax(route_logits, axis=-1).reshape(-1)
    route_kept = jnp.sum(route_onehot.astype(jnp.float32) * kept_table[None, :], axis=1)
    slot_match = (jnp.arange(slot_total, dtype=jnp.int32)[:, None] == route_slot[None, :]).astype(
        jnp.float32
    )
    pick_tokens = slot_match.reshape(slot_total, tok_rows, 2).sum(axis=2)
    kept_weights = (
        (slot_match * (gate_probs * route_kept)[None, :])
        .reshape(slot_total, tok_rows, 2)
        .sum(axis=2)
    )
    dropped_weights = (
        (slot_match * (gate_probs * (1.0 - route_kept))[None, :])
        .reshape(slot_total, tok_rows, 2)
        .sum(axis=2)
    )
    by_expert = jnp.dot(
        pick_tokens.astype(jnp.bfloat16), tokens, preferred_element_type=jnp.float32
    ).astype(jnp.bfloat16)
    outgoing = spread_copies(by_expert.reshape(E, CAP, -1), E, held_count, copies)
    chosen = lax.dynamic_index_in_dim(
        lax.all_to_all(outgoing, "dp", split_axis=0, concat_axis=0, tiled=True),
        own_group,
        1,
        keepdims=False,
    )
    contract = (((2,), (1,)), ((), ()))
    gate_part = lax.dot_general(chosen, gate_weight, contract, preferred_element_type=jnp.float32)
    up_part = lax.dot_general(chosen, up_weight, contract, preferred_element_type=jnp.float32)
    gate_part, up_part = (gate_part, up_part)
    gate_sum, up_sum = (
        lax.psum(gate_part.astype(jnp.bfloat16), "col").astype(jnp.float32),
        lax.psum(up_part.astype(jnp.bfloat16), "col").astype(jnp.float32),
    )
    hidden = (jax.nn.silu(gate_sum) * up_sum).astype(jnp.bfloat16)
    expert_out = lax.dot_general(
        hidden, down_weight, (((2,), (0,)), ((), ())), preferred_element_type=jnp.float32
    ).astype(jnp.bfloat16)
    hidden_wide = hidden.astype(jnp.float32)
    group_mask = (jnp.arange(held_count) == own_group)[None, :, None, None]
    placed = jnp.where(group_mask, expert_out[:, None], jnp.zeros((), jnp.bfloat16))
    returned = lax.all_to_all(placed, "dp", split_axis=0, concat_axis=0, tiled=True)
    slot_values = expert_major(returned.astype(jnp.float32), E, held_count, copies)
    dropped_part = jnp.dot(dropped_weights.T, slot_values, precision=top_precision)
    dropped = lax.psum(dropped_part, "tensor")
    ridge_weight = ridge_share * 2.0 * tok_rows * dp_count / E

    def apply_backward(image_tokens):
        slot_image = jnp.dot(kept_weights, image_tokens, precision=top_precision)
        outgoing_image = spread_copies(slot_image.reshape(E, CAP, -1), E, held_count, copies)
        arrived = lax.all_to_all(outgoing_image, "dp", split_axis=0, concat_axis=0, tiled=True)
        chosen = lax.dynamic_index_in_dim(arrived, own_group, 1, keepdims=False)
        return exact_product(hidden_wide, chosen, (((0, 1), (0, 1)), ((), ())))

    def total_norm(values):
        return lax.psum(jnp.sum(values * values), ("dp", "tensor", "col"))

    base_down = down_weight.astype(jnp.float32)
    residual = apply_backward(dropped) - ridge_weight * own_kept * base_down
    res_norm = total_norm(residual)
    direction = residual
    leftover = dropped
    for turn_index in range(ITERS):
        slot_part = exact_product(hidden_wide, direction, (((2,), (0,)), ((), ())))
        placed_part = jnp.where(group_mask, slot_part[:, None], 0.0)
        came_back = lax.all_to_all(placed_part, "dp", split_axis=0, concat_axis=0, tiled=True)
        image_part = jnp.dot(
            kept_weights.T, expert_major(came_back, E, held_count, copies), precision=top_precision
        )
        image_tokens = lax.psum(image_part, "tensor")
        first_copy = (lax.axis_index("tensor") == 0).astype(jnp.float32)
        local_term = first_copy * jnp.sum(image_tokens * image_tokens) + ridge_weight * jnp.sum(
            direction * direction
        )
        curvature = lax.psum(local_term, ("dp", "tensor", "col"))
        step_size = res_norm / curvature
        leftover = leftover - step_size * image_tokens
        if turn_index + 1 < ITERS:
            curved = apply_backward(image_tokens) + ridge_weight * direction
            residual = residual - step_size * curved
            next_norm = total_norm(residual)
            direction = residual + next_norm / res_norm * direction
            res_norm = next_norm
    return leftover


def shards(*arrays):
    sizes = [lax.axis_size(axis) for axis in ("dp", "tensor", "col")]
    if sizes[0] * sizes[1] == E and sizes[2] == 4 and ITERS == 2:
        return one_expert_each(*arrays)
    return general(*arrays)


def solution(mesh):
    placed = (
        P("dp", "col"),
        P("dp", None),
        P("dp", None),
        P(),
        P(("dp", "tensor"), "col"),
        P(("dp", "tensor"), "col"),
        P(("dp", "tensor"), "col"),
    )
    return jax.shard_map(
        shards, mesh=mesh, in_specs=placed, out_specs=P("dp", "col"), check_vma=False
    )
```

```python
import functools

import jax
import jax.numpy as jnp
from jax import lax
from jax.experimental import pallas as pl
from jax.experimental.pallas import tpu as pltpu
from jax.sharding import PartitionSpec as P

E = 8
ITERS = 2
CAP = 40
CHUNKS = 4


ridge_share = 0.25
top_precision = lax.Precision.HIGHEST
MIB = 1024 * 1024
LIGHT = pl.CostEstimate(flops=1, bytes_accessed=1, transcendentals=0)
f32 = jnp.float32
bf16 = jnp.bfloat16
NT = (((1,), (1,)), ((), ()))
NN = (((1,), (0,)), ((), ()))
TN = (((0,), (0,)), ((), ()))


def whole():
    return pl.BlockSpec(memory_space=pltpu.VMEM)


def scalars():
    return pl.BlockSpec(memory_space=pltpu.SMEM)


def mm(left, right, contract=NN):
    return lax.dot_general(left, right, contract, preferred_element_type=f32)


def split_wide(values):
    high = values.astype(bf16)
    low = (values - high.astype(f32)).astype(bf16)
    return jnp.concatenate([high, low], axis=1)


def mm_wide(left, right, contract=NN):
    lanes = right.shape[1]
    both = mm(left, split_wide(right), contract)
    return both[:, :lanes] + both[:, lanes:]


def params(mib):
    return pltpu.CompilerParams(vmem_limit_bytes=mib * MIB)


def block_slots(first, second):
    count = first.shape[1]
    expert_rows = lax.broadcasted_iota(jnp.int32, (E, count), 0).astype(f32)
    hot_first = (expert_rows == first).astype(f32)
    hot_second = (expert_rows == second).astype(f32)
    before = (
        lax.broadcasted_iota(jnp.int32, (count, count), 0)
        < lax.broadcasted_iota(jnp.int32, (count, count), 1)
    ).astype(bf16)
    place = mm((hot_first + hot_second).astype(bf16), before)
    ranked_first = jnp.sum(hot_first * place, axis=0, keepdims=True)
    ranked_second = jnp.sum(hot_second * place, axis=0, keepdims=True)
    return ranked_first, ranked_second


def pick_kernel(parts, tensor_count, place_ref, routes_ref, logits_ref, tokens_ref, info_ref, *out_refs):
    info_ref[0:2, :] = routes_ref[...].astype(f32)
    info_ref[2:4, :] = logits_ref[...]
    first, second = info_ref[0:1, :], info_ref[1:2, :]
    rank_first, rank_second = block_slots(first, second)
    count = first.shape[1]
    rows = lax.broadcasted_iota(jnp.int32, (CAP, count), 0).astype(f32)
    values = tokens_ref[...]
    for shift, out_ref in enumerate(out_refs):
        expert = (lax.rem(place_ref[0] + shift, parts) * tensor_count + place_ref[1]).astype(f32)
        hit = ((first == expert) & (rank_first == rows)) | ((second == expert) & (rank_second == rows))
        out_ref[...] = mm(hit.astype(f32).astype(bf16), values).astype(bf16)


def turn_kernel(*refs):
    rows = jnp.concatenate([ref[...].astype(f32) for ref in refs[:-1]], axis=0)
    refs[-1][...] = rows.T.astype(bf16)


def turned(values):
    rows, slots = values.shape
    main = slots // 128 * 128
    rest = slots - main
    if main == 0 or rest == 0 or 128 % rest or rows % (128 // rest):
        return values.T
    groups = 128 // rest
    tall = rows // groups
    folded = jnp.concatenate(
        [values[group * tall : (group + 1) * tall, main:] for group in range(groups)], axis=1
    ).T
    tail = jnp.concatenate(
        [folded[group * rest : (group + 1) * rest] for group in range(groups)], axis=1
    )
    return jnp.concatenate([values[:, :main].T, tail], axis=0)


def gate_up_kernel(has_keep, order_ref, inputs_ref, gate_ref, up_ref, *rest):
    values = inputs_ref[...]
    gate = turned(mm(gate_ref[...], values).astype(bf16))
    up = turned(mm(up_ref[...], values).astype(bf16))
    step = pl.program_id(0)
    outs = rest[-(1 + (has_keep == 2)) :]
    for index, ref in enumerate(outs):

        @pl.when(step // 2 == index)
        def _(ref=ref):
            ref[0, 0] = gate
            ref[0, 1] = up


def gate_up(order, inputs, gate_weight, up_weight, width, keep, send, after):
    depth, slots = inputs.shape
    quarter = gate_weight.shape[0] // 4
    gate_weight = gate_weight.reshape(4, quarter, depth)
    up_weight = up_weight.reshape(4, quarter, depth)
    base = 0 if keep is not None else 2
    chunks = [chunk for chunk in (keep, send) if chunk is not None]
    count = len(chunks)

    def place(s, order):
        return (order[base + s], chunks[0] if count == 1 else jnp.where(s < 2, chunks[0], chunks[1]), 0)

    weight_spec = pl.BlockSpec((None, width, depth), place)
    out_specs = [
        pl.BlockSpec(
            (1, 2, slots, width),
            lambda s, order, index=index: (jnp.clip(s - 2 * index, 0, 1), 0, 0, 0),
        )
        for index in range(count)
    ]
    return pl.pallas_call(
        functools.partial(gate_up_kernel, count),
        grid_spec=pltpu.PrefetchScalarGridSpec(
            num_scalar_prefetch=1,
            grid=(2 * count,),
            in_specs=[
                pl.BlockSpec((depth, slots), lambda s, order: (0, 0)),
                weight_spec,
                weight_spec,
            ]
            + [pl.BlockSpec(memory_space=pl.ANY)] * len(after),
            out_specs=out_specs,
        ),
        out_shape=[jax.ShapeDtypeStruct((2, 2, slots, width), bf16)] * count,
        compiler_params=params(41),
        cost_estimate=LIGHT,
        name=f"gate_up_{chunks[-1] + (send is None)}",
    )(order, inputs, gate_weight, up_weight, *after)


def down_kernel(pack, has_old, order_ref, place_ref, own_ref, across_ref, beside_ref, both_ref, down_ref, *rest):
    pieces = (own_ref, across_ref, beside_ref, both_ref)
    old, new = rest[:3] if has_old else (), rest[3 * has_old :]
    packed_refs = ()
    if pack:
        packed_refs, new = new[:-3], new[-3:]
    step = pl.program_id(0)

    @pl.when(step == 0)
    def _():
        for index, ref in enumerate(new):
            ref[...] = old[index][...] if old else jnp.zeros_like(ref)

    out_ref, gram_ref, square_ref = new
    weight = down_ref[...]
    wide = weight.astype(f32)
    square_ref[...] += jnp.sum((wide * wide).reshape(-1, 8, wide.shape[1]), axis=0)
    for index, ref in enumerate(pieces):

        @pl.when(step == index)
        def _(ref=ref, index=index):
            values = ref[...]
            out_ref[...] += mm(values, weight)
            gram_ref[...] += mm(values, values, NT)
            if pack and index == len(pieces) - 1:
                dp_count, tensor_count = pack
                columns = out_ref.shape[1]
                lanes = columns // (dp_count * tensor_count)
                group = columns // dp_count
                gram = gram_ref[...]
                rolled = pltpu.roll(out_ref[...], lax.rem(columns - place_ref[0] * group, columns), 1)
                for ahead in range(dp_count):
                    parts = [
                        rolled[:, ahead * group + part * lanes : ahead * group + (part + 1) * lanes]
                        for part in range(tensor_count)
                    ]
                    for aside in range(tensor_count):
                        target = lax.rem(place_ref[1] + aside, tensor_count)
                        piece = parts[0]
                        for part in range(1, tensor_count):
                            piece = jnp.where(target == part, parts[part], piece)
                        packed_refs[ahead * tensor_count + aside][...] = jnp.concatenate(
                            [gram, piece], axis=1
                        ).astype(bf16)


def down(order, place, pieces, down_weight, chunk, older, pack=None):
    slots, width = pieces[0].shape
    columns = down_weight.shape[1]
    down_weight = down_weight.reshape(4, -1, columns)

    def fixed(shape):
        return pl.BlockSpec(shape, lambda s, order, place: (0,) * len(shape))

    shapes = [(slots, columns), (slots, slots), (8, columns)]
    out_shape = [jax.ShapeDtypeStruct(shape, f32) for shape in shapes]
    if pack:
        parts = pack[0] * pack[1]
        packed = (slots, slots + columns // parts)
        out_shape = [jax.ShapeDtypeStruct(packed, bf16)] * parts + out_shape
    return pl.pallas_call(
        functools.partial(down_kernel, pack, bool(older)),
        grid_spec=pltpu.PrefetchScalarGridSpec(
            num_scalar_prefetch=2,
            grid=(4,),
            in_specs=[fixed((slots, width))] * 4
            + [pl.BlockSpec((None, width, columns), lambda s, order, place: (order[s], chunk, 0))]
            + [fixed(value.shape) for value in older],
            out_specs=[fixed(value.shape) for value in out_shape],
        ),
        out_shape=out_shape,
        compiler_params=params(20),
        cost_estimate=LIGHT,
        name=f"down_{chunk}",
    )(order, place, *pieces, down_weight, *older)


def route_kernel(blocks, tensor_count, kept_ref, place_ref, *refs):
    infos = refs[:blocks]
    hot_ref, turned_ref, gates_ref, wide_ref = refs[-4:]
    count = infos[0].shape[1]
    slots = blocks * CAP
    zero = jnp.zeros((CAP, count), f32)
    rows = lax.broadcasted_iota(jnp.int32, (CAP, count), 0).astype(f32)
    routed = []
    for block in range(blocks):
        first, second = infos[block][0:1, :], infos[block][1:2, :]
        delta = infos[block][3:4, :] - infos[block][2:3, :]
        share_first = 1.0 / (1.0 + jnp.exp(delta))
        share_second = 1.0 / (1.0 + jnp.exp(-delta))
        routed.append((first, second, share_first, share_second) + block_slots(first, second))
    for back in range(blocks):
        for aside in range(tensor_count):
            expert = lax.rem(place_ref[0] + blocks - back, blocks) * tensor_count
            expert = expert + lax.rem(place_ref[1] + tensor_count - aside, tensor_count)
            kept = jnp.zeros((), jnp.int32)
            for index in range(kept_ref.shape[0]):
                kept = kept | (kept_ref[index] == expert).astype(jnp.int32)
            kept, expert = kept.astype(f32), expert.astype(f32)
            for shift in range(blocks):
                block = (back + shift) % blocks
                first, second, share_first, share_second, rank_first, rank_second = routed[block]
                hit_first = (first == expert) & (rank_first == rows)
                hit_second = (second == expert) & (rank_second == rows)
                gate = jnp.sum(
                    jnp.where(hit_first, share_first, zero) + jnp.where(hit_second, share_second, zero),
                    axis=1,
                    keepdims=True,
                )
                row = (back * tensor_count + aside) * slots + shift * CAP
                for other in range(blocks):
                    wide_ref[row : row + CAP, other * count : (other + 1) * count] = (
                        (hit_first | hit_second).astype(f32) if other == block else zero
                    )
                gates_ref[row : row + CAP, 0:1] = gate * kept
                gates_ref[row : row + CAP, 1:2] = gate * (1.0 - kept)
    hot_ref[...] = wide_ref[...].astype(bf16)
    turned_ref[...] = wide_ref[...].T.astype(bf16)


def solve_kernel(ridge, slots, own_ref, hot_ref, turned_ref, gates_ref, square_ref, *refs):
    packed_refs, (base_ref, zero_ref, one_ref, sums_ref) = refs[:E], refs[E:]
    hot, turned = hot_ref[...], turned_ref[...]
    kept, dropped = gates_ref[:, 0:1], gates_ref[:, 1:2]
    values = jnp.concatenate([packed_refs[e][:, slots:].astype(f32) for e in range(E)], axis=0)
    base = mm_wide(turned, dropped * values)
    output = mm_wide(turned, kept * values)

    def apply(field):
        spread = kept * mm_wide(hot, field)
        mixed = jnp.concatenate(
            [
                mm_wide(packed_refs[e][:, :slots], spread[e * slots : (e + 1) * slots])
                for e in range(E)
            ],
            axis=0,
        )
        return mm_wide(turned, kept * mixed)

    curved = apply(base)
    zero = curved - ridge * output
    one = apply(zero)
    base_ref[...] = base
    zero_ref[...] = zero
    one_ref[...] = one
    norm = jnp.sum(base * (curved - 2.0 * ridge * output))
    square = jnp.sum(square_ref[...]) * own_ref[0]
    lane = lax.broadcasted_iota(jnp.int32, sums_ref.shape[1:], 1)
    sums = jnp.where(lane == 0, norm + ridge * ridge * square, 0.0)
    for index, value in enumerate((jnp.sum(zero * zero), jnp.sum(zero * one), jnp.sum(one * one))):
        sums = jnp.where(lane == index + 1, value, sums)
    for part in range(sums_ref.shape[0]):
        sums_ref[part] = sums


def finish_kernel(ridge, base_ref, zero_ref, one_ref, sums_ref, *out_refs):
    sums = jnp.sum(sums_ref[...], axis=0)[0:1, :]
    norm, zero_zero = sums[:, 0:1], sums[:, 1:2]
    zero_one, one_one = sums[:, 2:3], sums[:, 3:4]
    step = norm / (zero_zero + ridge * norm)
    left = 1.0 - step * ridge
    new = left * left * norm - 2.0 * left * step * zero_zero + step * step * zero_one
    ratio = new / norm
    grown = left + ratio
    image = grown * grown * zero_zero - 2.0 * grown * step * zero_one + step * step * one_one
    later = new / (image + ridge * (new + ratio * ratio * norm))
    field = base_ref[...] - (step + later * grown) * zero_ref[...] + (later * step) * one_ref[...]
    rows = field.shape[0] // len(out_refs)
    sideways = field.T.astype(bf16)
    for block, ref in enumerate(out_refs):
        ref[...] = sideways[:, block * rows : (block + 1) * rows]


def join_kernel(blocks, tensor_count, place_ref, *refs):
    pieces, (out_ref, rows_ref) = refs[:-2], refs[-2:]
    lanes = pieces[0].shape[0]
    for back in range(blocks):
        for aside in range(tensor_count):
            part = lax.rem(place_ref[0] + blocks - back, blocks) * tensor_count
            part = part + lax.rem(place_ref[1] + tensor_count - aside, tensor_count)
            start = pl.multiple_of(part * lanes, 8)
            rows_ref[pl.ds(start, lanes), :] = pieces[back * tensor_count + aside][...].astype(f32)
    out_ref[...] = rows_ref[...].T


def single(kernel, out_shape, in_specs, mib, name, scratch=()):
    many = isinstance(out_shape, list)
    return pl.pallas_call(
        kernel,
        out_shape=out_shape,
        in_specs=in_specs,
        out_specs=[whole()] * len(out_shape) if many else whole(),
        scratch_shapes=list(scratch),
        compiler_params=params(mib),
        cost_estimate=LIGHT,
        name=name,
    )


def one_expert_each(tokens, routes, route_logits, kept_experts, gate_weight, up_weight, down_weight):
    dp_count = lax.axis_size("dp")
    tensor_count = lax.axis_size("tensor")
    parts = dp_count * tensor_count
    tok_rows, depth = tokens.shape
    units, columns = down_weight.shape
    slots = dp_count * CAP
    lanes = columns // parts
    width = units // 4 // CHUNKS
    ridge = ridge_share * 2.0 * tok_rows * dp_count / E
    dp_index = lax.axis_index("dp")
    tensor_index = lax.axis_index("tensor")
    col_index = lax.axis_index("col")
    own_expert = dp_index * tensor_count + tensor_index
    place = jnp.stack([dp_index, tensor_index])

    def beside(values):
        return lax.ppermute(values, "col", [(k, k ^ 1) for k in range(4)])

    def across(values):
        return lax.ppermute(values, "col", [(k, k ^ 2) for k in range(4)])

    def shifted(values, ahead, aside=0):
        if ahead == 0 and aside == 0:
            return values
        pairs = [
            (i * tensor_count + j, (i + ahead) % dp_count * tensor_count + (j + aside) % tensor_count)
            for i in range(dp_count)
            for j in range(tensor_count)
        ]
        return lax.ppermute(values, ("dp", "tensor"), pairs)

    shifts = [(ahead, aside) for ahead in range(dp_count) for aside in range(tensor_count)]
    info, *picked = single(
        functools.partial(pick_kernel, dp_count, tensor_count),
        [jax.ShapeDtypeStruct((4, tok_rows), f32)] + [jax.ShapeDtypeStruct((CAP, depth), bf16)] * dp_count,
        [scalars(), whole(), whole(), whole()],
        16,
        "pick",
    )(place, routes.T, route_logits.T, tokens)
    arrived = [shifted(value, ahead) for ahead, value in enumerate(picked)]
    inputs = single(
        turn_kernel,
        jax.ShapeDtypeStruct((depth, slots), bf16),
        [whole()] * dp_count,
        16,
        "turn",
    )(*arrived)

    gate_order = col_index ^ jnp.array([2, 0, 3, 1], jnp.int32)
    down_order = col_index ^ jnp.array([0, 2, 1, 3], jnp.int32)

    def products(keep, send, after=()):
        return gate_up(gate_order, inputs, gate_weight, up_weight, width, keep, send, after)

    last = CHUNKS - 1
    keeps, nears, pairs, fars, owns = [], [], [], [], []

    def activate(chunk, after):
        far = lax.optimization_barrier((fars[chunk], *after))[0] if after else fars[chunk]
        total = keeps[chunk][1].astype(f32) + nears[chunk][1].astype(f32) + far.astype(f32)
        owns.append((jax.nn.silu(total[0]) * total[1]).astype(bf16))

    nears.append(beside(products(None, 0)[0]))
    for chunk in range(CHUNKS):
        after = []
        if chunk >= 2:
            after = after + [fars[chunk - 2]]
        if chunk >= 3:
            activate(chunk - 3, [])
            after = after + [owns[chunk - 3]]
        if chunk < last:
            keep, send = products(chunk, chunk + 1, after)
            nears.append(beside(send))
        else:
            (keep,) = products(chunk, None, after)
        keeps.append(keep)
        pairs.append((keep[0].astype(f32) + nears[chunk][0].astype(f32)).astype(bf16))
        fars.append(across(pairs[-1]))
    info = lax.optimization_barrier((info, owns[0]))[0]
    infos = [shifted(info, ahead) for ahead in range(dp_count)]
    older, olders = (), []
    for chunk in range(CHUNKS):
        if chunk >= len(owns):
            after = [pairs[last]]
            if chunk >= 2:
                after.append(olders[chunk - 2][2])
                after.extend(infos[1:])
            activate(chunk, after)
        own = owns[chunk]
        other = across(own)
        older = down(
            down_order,
            place,
            (own, other, beside(own), beside(other)),
            down_weight,
            chunk,
            older,
            (dp_count, tensor_count) if chunk == last else None,
        )
        olders.append(older)
    packed, (_, _, square) = older[:parts], older[parts:]
    spread = [shifted(value, *shift) for value, shift in zip(packed, shifts)]

    total_slots, total_tokens = E * slots, dp_count * tok_rows
    hot, turned_hot, gates = single(
        functools.partial(route_kernel, dp_count, tensor_count),
        [
            jax.ShapeDtypeStruct((total_slots, total_tokens), bf16),
            jax.ShapeDtypeStruct((total_tokens, total_slots), bf16),
            jax.ShapeDtypeStruct((total_slots, 2), f32),
        ],
        [scalars(), scalars()] + [whole()] * dp_count + [pl.BlockSpec(memory_space=pl.ANY)],
        24,
        "route",
        [pltpu.VMEM((total_slots, total_tokens), f32)],
    )(kept_experts, place, *infos, square)
    is_kept = jnp.any(kept_experts == own_expert).astype(f32).reshape(1)
    field = jax.ShapeDtypeStruct((total_tokens, lanes), f32)
    everyone = parts * lax.axis_size("col")
    base, zero, one, sums = single(
        functools.partial(solve_kernel, ridge, slots),
        [field, field, field, jax.ShapeDtypeStruct((everyone, 1, 128), f32)],
        [scalars()] + [whole()] * (4 + E),
        40,
        "solve",
    )(is_kept, hot, turned_hot, gates, square, *spread)
    sums = lax.all_to_all(sums, ("dp", "tensor", "col"), split_axis=0, concat_axis=0, tiled=True)

    home = single(
        functools.partial(finish_kernel, ridge),
        [jax.ShapeDtypeStruct((lanes, tok_rows), bf16)] * dp_count,
        [whole()] * 4,
        16,
        "finish",
    )(base, zero, one, sums)
    pieces = [shifted(home[-ahead % dp_count], ahead, aside) for ahead, aside in shifts]
    return single(
        functools.partial(join_kernel, dp_count, tensor_count),
        jax.ShapeDtypeStruct((tok_rows, columns), f32),
        [scalars()] + [whole()] * parts,
        16,
        "join",
        [pltpu.VMEM((columns, tok_rows), f32)],
    )(place, *pieces)


def spread_copies(values, experts, held_count, copies):
    old_shape = values.shape
    grouped = values.reshape((experts // held_count, 1, held_count) + old_shape[1:])
    widened = jnp.broadcast_to(grouped, (experts // held_count, copies, held_count) + old_shape[1:])
    return widened.reshape((experts // held_count * copies, held_count) + old_shape[1:])


def expert_major(returned, experts, held_count, copies):
    old_shape = returned.shape
    grouped = returned.reshape((experts // held_count, copies, held_count) + old_shape[2:])
    merged = jnp.sum(grouped, axis=1)
    return merged.reshape((experts * old_shape[2],) + old_shape[3:])


def exact_product(left, right, contract):
    return lax.dot_general(
        left, right, contract, precision=top_precision, preferred_element_type=jnp.float32
    )


def general(tokens, routes, route_logits, kept_experts, gate_weight, up_weight, down_weight):
    dp_count = lax.axis_size("dp")
    tensor_count = lax.axis_size("tensor")
    held_count = max(1, E // dp_count)
    copies = max(1, dp_count // E)
    tok_rows = tokens.shape[0]
    piece_rows = gate_weight.shape[0]
    FF = piece_rows * dp_count * tensor_count // E
    slot_total = E * CAP
    device_rank = lax.axis_index("dp") * tensor_count + lax.axis_index("tensor")
    own_expert = device_rank * piece_rows // FF
    own_group = own_expert % held_count
    expert_ids = jnp.arange(E, dtype=jnp.int32)
    kept_table = jnp.any(kept_experts[:, None] == expert_ids[None, :], axis=0).astype(jnp.float32)
    own_kept = jnp.sum(jnp.where(expert_ids == own_expert, kept_table, 0.0))
    route_experts = routes.reshape(-1)
    route_onehot = (route_experts[:, None] == expert_ids[None, :]).astype(jnp.int32)
    route_rank = jnp.sum((jnp.cumsum(route_onehot, axis=0) - route_onehot) * route_onehot, axis=1)
    route_slot = route_experts * CAP + route_rank
    gate_probs = jax.nn.softmax(route_logits, axis=-1).reshape(-1)
    route_kept = jnp.sum(route_onehot.astype(jnp.float32) * kept_table[None, :], axis=1)
    slot_match = (jnp.arange(slot_total, dtype=jnp.int32)[:, None] == route_slot[None, :]).astype(
        jnp.float32
    )
    pick_tokens = slot_match.reshape(slot_total, tok_rows, 2).sum(axis=2)
    kept_weights = (
        (slot_match * (gate_probs * route_kept)[None, :])
        .reshape(slot_total, tok_rows, 2)
        .sum(axis=2)
    )
    dropped_weights = (
        (slot_match * (gate_probs * (1.0 - route_kept))[None, :])
        .reshape(slot_total, tok_rows, 2)
        .sum(axis=2)
    )
    by_expert = jnp.dot(
        pick_tokens.astype(jnp.bfloat16), tokens, preferred_element_type=jnp.float32
    ).astype(jnp.bfloat16)
    outgoing = spread_copies(by_expert.reshape(E, CAP, -1), E, held_count, copies)
    chosen = lax.dynamic_index_in_dim(
        lax.all_to_all(outgoing, "dp", split_axis=0, concat_axis=0, tiled=True),
        own_group,
        1,
        keepdims=False,
    )
    contract = (((2,), (1,)), ((), ()))
    gate_part = lax.dot_general(chosen, gate_weight, contract, preferred_element_type=jnp.float32)
    up_part = lax.dot_general(chosen, up_weight, contract, preferred_element_type=jnp.float32)
    gate_part, up_part = (gate_part, up_part)
    gate_sum, up_sum = (
        lax.psum(gate_part.astype(jnp.bfloat16), "col").astype(jnp.float32),
        lax.psum(up_part.astype(jnp.bfloat16), "col").astype(jnp.float32),
    )
    hidden = (jax.nn.silu(gate_sum) * up_sum).astype(jnp.bfloat16)
    expert_out = lax.dot_general(
        hidden, down_weight, (((2,), (0,)), ((), ())), preferred_element_type=jnp.float32
    ).astype(jnp.bfloat16)
    hidden_wide = hidden.astype(jnp.float32)
    group_mask = (jnp.arange(held_count) == own_group)[None, :, None, None]
    placed = jnp.where(group_mask, expert_out[:, None], jnp.zeros((), jnp.bfloat16))
    returned = lax.all_to_all(placed, "dp", split_axis=0, concat_axis=0, tiled=True)
    slot_values = expert_major(returned.astype(jnp.float32), E, held_count, copies)
    dropped_part = jnp.dot(dropped_weights.T, slot_values, precision=top_precision)
    dropped = lax.psum(dropped_part, "tensor")
    ridge_weight = ridge_share * 2.0 * tok_rows * dp_count / E

    def apply_backward(image_tokens):
        slot_image = jnp.dot(kept_weights, image_tokens, precision=top_precision)
        outgoing_image = spread_copies(slot_image.reshape(E, CAP, -1), E, held_count, copies)
        arrived = lax.all_to_all(outgoing_image, "dp", split_axis=0, concat_axis=0, tiled=True)
        chosen = lax.dynamic_index_in_dim(arrived, own_group, 1, keepdims=False)
        return exact_product(hidden_wide, chosen, (((0, 1), (0, 1)), ((), ())))

    def total_norm(values):
        return lax.psum(jnp.sum(values * values), ("dp", "tensor", "col"))

    base_down = down_weight.astype(jnp.float32)
    residual = apply_backward(dropped) - ridge_weight * own_kept * base_down
    res_norm = total_norm(residual)
    direction = residual
    leftover = dropped
    for turn_index in range(ITERS):
        slot_part = exact_product(hidden_wide, direction, (((2,), (0,)), ((), ())))
        placed_part = jnp.where(group_mask, slot_part[:, None], 0.0)
        came_back = lax.all_to_all(placed_part, "dp", split_axis=0, concat_axis=0, tiled=True)
        image_part = jnp.dot(
            kept_weights.T, expert_major(came_back, E, held_count, copies), precision=top_precision
        )
        image_tokens = lax.psum(image_part, "tensor")
        first_copy = (lax.axis_index("tensor") == 0).astype(jnp.float32)
        local_term = first_copy * jnp.sum(image_tokens * image_tokens) + ridge_weight * jnp.sum(
            direction * direction
        )
        curvature = lax.psum(local_term, ("dp", "tensor", "col"))
        step_size = res_norm / curvature
        leftover = leftover - step_size * image_tokens
        if turn_index + 1 < ITERS:
            curved = apply_backward(image_tokens) + ridge_weight * direction
            residual = residual - step_size * curved
            next_norm = total_norm(residual)
            direction = residual + next_norm / res_norm * direction
            res_norm = next_norm
    return leftover


def shards(*arrays):
    sizes = [lax.axis_size(axis) for axis in ("dp", "tensor", "col")]
    if sizes[0] * sizes[1] == E and sizes[2] == 4 and ITERS == 2:
        return one_expert_each(*arrays)
    return general(*arrays)


def solution(mesh):
    placed = (
        P("dp", "col"),
        P("dp", None),
        P("dp", None),
        P(),
        P(("dp", "tensor"), "col"),
        P(("dp", "tensor"), "col"),
        P(("dp", "tensor"), "col"),
    )
    return jax.shard_map(
        shards, mesh=mesh, in_specs=placed, out_specs=P("dp", "col"), check_vma=False
    )
```

```python
import functools

import jax
import jax.numpy as jnp
from jax import lax
from jax.experimental import pallas as pl
from jax.experimental.pallas import tpu as pltpu
from jax.sharding import PartitionSpec as P

E = 8
ITERS = 2
CAP = 40
CHUNKS = 4


ridge_share = 0.25
top_precision = lax.Precision.HIGHEST
MIB = 1024 * 1024
LIGHT = pl.CostEstimate(flops=1, bytes_accessed=1, transcendentals=0)
f32 = jnp.float32
bf16 = jnp.bfloat16
NT = (((1,), (1,)), ((), ()))
NN = (((1,), (0,)), ((), ()))
TN = (((0,), (0,)), ((), ()))


def whole():
    return pl.BlockSpec(memory_space=pltpu.VMEM)


def scalars():
    return pl.BlockSpec(memory_space=pltpu.SMEM)


def mm(left, right, contract=NN):
    return lax.dot_general(left, right, contract, preferred_element_type=f32)


def split_wide(values):
    high = values.astype(bf16)
    low = (values - high.astype(f32)).astype(bf16)
    return jnp.concatenate([high, low], axis=1)


def mm_wide(left, right, contract=NN):
    lanes = right.shape[1]
    both = mm(left, split_wide(right), contract)
    return both[:, :lanes] + both[:, lanes:]


def params(mib):
    return pltpu.CompilerParams(vmem_limit_bytes=mib * MIB)


def block_slots(first, second):
    count = first.shape[1]
    expert_rows = lax.broadcasted_iota(jnp.int32, (E, count), 0).astype(f32)
    hot_first = (expert_rows == first).astype(f32)
    hot_second = (expert_rows == second).astype(f32)
    before = (
        lax.broadcasted_iota(jnp.int32, (count, count), 0)
        < lax.broadcasted_iota(jnp.int32, (count, count), 1)
    ).astype(bf16)
    place = mm((hot_first + hot_second).astype(bf16), before)
    ranked_first = jnp.sum(hot_first * place, axis=0, keepdims=True)
    ranked_second = jnp.sum(hot_second * place, axis=0, keepdims=True)
    return ranked_first, ranked_second


def pick_kernel(parts, tensor_count, place_ref, routes_ref, logits_ref, tokens_ref, info_ref, *out_refs):
    info_ref[0:2, :] = routes_ref[...].astype(f32)
    info_ref[2:4, :] = logits_ref[...]
    first, second = info_ref[0:1, :], info_ref[1:2, :]
    rank_first, rank_second = block_slots(first, second)
    count = first.shape[1]
    rows = lax.broadcasted_iota(jnp.int32, (CAP, count), 0).astype(f32)
    values = tokens_ref[...]
    for shift, out_ref in enumerate(out_refs):
        expert = (lax.rem(place_ref[0] + shift, parts) * tensor_count + place_ref[1]).astype(f32)
        hit = ((first == expert) & (rank_first == rows)) | ((second == expert) & (rank_second == rows))
        out_ref[...] = mm(hit.astype(f32).astype(bf16), values).astype(bf16)


def turn_kernel(*refs):
    rows = jnp.concatenate([ref[...].astype(f32) for ref in refs[:-1]], axis=0)
    refs[-1][...] = rows.T.astype(bf16)


def turned(values):
    rows, slots = values.shape
    main = slots // 128 * 128
    rest = slots - main
    if main == 0 or rest == 0 or 128 % rest or rows % (128 // rest):
        return values.T
    groups = 128 // rest
    tall = rows // groups
    folded = jnp.concatenate(
        [values[group * tall : (group + 1) * tall, main:] for group in range(groups)], axis=1
    ).T
    tail = jnp.concatenate(
        [folded[group * rest : (group + 1) * rest] for group in range(groups)], axis=1
    )
    return jnp.concatenate([values[:, :main].T, tail], axis=0)


def gate_up_kernel(plan, order_ref, inputs_ref, gate_ref, up_ref, *rest):
    outs, (weights, sems) = rest[-2 - len(plan) // 2 : -2], rest[-2:]
    width = weights.shape[2]
    copies = []
    for step, (slot, chunk) in enumerate(plan):
        rows = pl.ds(chunk * width, width)
        for kind, ref in enumerate((gate_ref, up_ref)):
            copy = pltpu.make_async_copy(
                ref.at[order_ref[slot], rows], weights.at[step, kind], sems.at[step, kind]
            )
            copy.start()
            copies.append(copy)
    values = inputs_ref[...]
    for step in range(len(plan)):
        for kind in range(2):
            copies[2 * step + kind].wait()
            outs[step // 2][step % 2, kind] = turned(mm(weights[step, kind], values).astype(bf16))


def gate_up(order, inputs, gate_weight, up_weight, width, keep, send, after):
    depth, slots = inputs.shape
    quarter = gate_weight.shape[0] // 4
    plan = [(0, keep), (1, keep)] if keep is not None else []
    plan = plan + ([(2, send), (3, send)] if send is not None else [])
    anywhere = pl.BlockSpec(memory_space=pl.ANY)
    return pl.pallas_call(
        functools.partial(gate_up_kernel, plan),
        in_specs=[scalars(), whole(), anywhere, anywhere] + [anywhere] * len(after),
        out_specs=[whole()] * (len(plan) // 2),
        out_shape=[jax.ShapeDtypeStruct((2, 2, slots, width), bf16)] * (len(plan) // 2),
        scratch_shapes=[
            pltpu.VMEM((len(plan), 2, width, depth), bf16),
            pltpu.SemaphoreType.DMA((len(plan), 2)),
        ],
        compiler_params=params(41),
        cost_estimate=LIGHT,
        name=f"gate_up_{plan[-1][1] + (send is None)}",
    )(
        order,
        inputs,
        gate_weight.reshape(4, quarter, depth),
        up_weight.reshape(4, quarter, depth),
        *after,
    )


def down_kernel(pack, has_old, order_ref, place_ref, own_ref, across_ref, beside_ref, both_ref, down_ref, *rest):
    pieces = (own_ref, across_ref, beside_ref, both_ref)
    old, new = rest[:3] if has_old else (), rest[3 * has_old :]
    packed_refs = ()
    if pack:
        packed_refs, new = new[:-3], new[-3:]
    step = pl.program_id(0)

    @pl.when(step == 0)
    def _():
        for index, ref in enumerate(new):
            ref[...] = old[index][...] if old else jnp.zeros_like(ref)

    out_ref, gram_ref, square_ref = new
    weight = down_ref[...]
    wide = weight.astype(f32)
    square_ref[...] += jnp.sum((wide * wide).reshape(-1, 8, wide.shape[1]), axis=0)
    for index, ref in enumerate(pieces):

        @pl.when(step == index)
        def _(ref=ref, index=index):
            values = ref[...]
            out_ref[...] += mm(values, weight)
            gram_ref[...] += mm(values, values, NT)
            if pack and index == len(pieces) - 1:
                dp_count, tensor_count = pack
                columns = out_ref.shape[1]
                lanes = columns // (dp_count * tensor_count)
                group = columns // dp_count
                gram = gram_ref[...]
                rolled = pltpu.roll(out_ref[...], lax.rem(columns - place_ref[0] * group, columns), 1)
                for ahead in range(dp_count):
                    parts = [
                        rolled[:, ahead * group + part * lanes : ahead * group + (part + 1) * lanes]
                        for part in range(tensor_count)
                    ]
                    for aside in range(tensor_count):
                        target = lax.rem(place_ref[1] + aside, tensor_count)
                        piece = parts[0]
                        for part in range(1, tensor_count):
                            piece = jnp.where(target == part, parts[part], piece)
                        packed_refs[ahead * tensor_count + aside][...] = jnp.concatenate(
                            [gram, piece], axis=1
                        ).astype(bf16)


def down(order, place, pieces, down_weight, chunk, older, pack=None):
    slots, width = pieces[0].shape
    columns = down_weight.shape[1]
    down_weight = down_weight.reshape(4, -1, columns)

    def fixed(shape):
        return pl.BlockSpec(shape, lambda s, order, place: (0,) * len(shape))

    shapes = [(slots, columns), (slots, slots), (8, columns)]
    out_shape = [jax.ShapeDtypeStruct(shape, f32) for shape in shapes]
    if pack:
        parts = pack[0] * pack[1]
        packed = (slots, slots + columns // parts)
        out_shape = [jax.ShapeDtypeStruct(packed, bf16)] * parts + out_shape
    return pl.pallas_call(
        functools.partial(down_kernel, pack, bool(older)),
        grid_spec=pltpu.PrefetchScalarGridSpec(
            num_scalar_prefetch=2,
            grid=(4,),
            in_specs=[fixed((slots, width))] * 4
            + [pl.BlockSpec((None, width, columns), lambda s, order, place: (order[s], chunk, 0))]
            + [fixed(value.shape) for value in older],
            out_specs=[fixed(value.shape) for value in out_shape],
        ),
        out_shape=out_shape,
        compiler_params=params(20),
        cost_estimate=LIGHT,
        name=f"down_{chunk}",
    )(order, place, *pieces, down_weight, *older)


def route_kernel(blocks, tensor_count, kept_ref, place_ref, *refs):
    infos = refs[:blocks]
    hot_ref, turned_ref, gates_ref, wide_ref = refs[-4:]
    count = infos[0].shape[1]
    slots = blocks * CAP
    zero = jnp.zeros((CAP, count), f32)
    rows = lax.broadcasted_iota(jnp.int32, (CAP, count), 0).astype(f32)
    routed = []
    for block in range(blocks):
        first, second = infos[block][0:1, :], infos[block][1:2, :]
        delta = infos[block][3:4, :] - infos[block][2:3, :]
        share_first = 1.0 / (1.0 + jnp.exp(delta))
        share_second = 1.0 / (1.0 + jnp.exp(-delta))
        routed.append((first, second, share_first, share_second) + block_slots(first, second))
    for back in range(blocks):
        for aside in range(tensor_count):
            expert = lax.rem(place_ref[0] + blocks - back, blocks) * tensor_count
            expert = expert + lax.rem(place_ref[1] + tensor_count - aside, tensor_count)
            kept = jnp.zeros((), jnp.int32)
            for index in range(kept_ref.shape[0]):
                kept = kept | (kept_ref[index] == expert).astype(jnp.int32)
            kept, expert = kept.astype(f32), expert.astype(f32)
            for shift in range(blocks):
                block = (back + shift) % blocks
                first, second, share_first, share_second, rank_first, rank_second = routed[block]
                hit_first = (first == expert) & (rank_first == rows)
                hit_second = (second == expert) & (rank_second == rows)
                gate = jnp.sum(
                    jnp.where(hit_first, share_first, zero) + jnp.where(hit_second, share_second, zero),
                    axis=1,
                    keepdims=True,
                )
                row = (back * tensor_count + aside) * slots + shift * CAP
                for other in range(blocks):
                    wide_ref[row : row + CAP, other * count : (other + 1) * count] = (
                        (hit_first | hit_second).astype(f32) if other == block else zero
                    )
                gates_ref[row : row + CAP, 0:1] = gate * kept
                gates_ref[row : row + CAP, 1:2] = gate * (1.0 - kept)
    hot_ref[...] = wide_ref[...].astype(bf16)
    turned_ref[...] = wide_ref[...].T.astype(bf16)


def solve_kernel(ridge, slots, own_ref, hot_ref, turned_ref, gates_ref, square_ref, *refs):
    packed_refs, (base_ref, zero_ref, one_ref, sums_ref) = refs[:E], refs[E:]
    hot, turned = hot_ref[...], turned_ref[...]
    kept, dropped = gates_ref[:, 0:1], gates_ref[:, 1:2]
    values = jnp.concatenate([packed_refs[e][:, slots:].astype(f32) for e in range(E)], axis=0)
    base = mm_wide(turned, dropped * values)
    output = mm_wide(turned, kept * values)

    def apply(field):
        spread = kept * mm_wide(hot, field)
        mixed = jnp.concatenate(
            [
                mm_wide(packed_refs[e][:, :slots], spread[e * slots : (e + 1) * slots])
                for e in range(E)
            ],
            axis=0,
        )
        return mm_wide(turned, kept * mixed)

    curved = apply(base)
    zero = curved - ridge * output
    one = apply(zero)
    base_ref[...] = base
    zero_ref[...] = zero
    one_ref[...] = one
    norm = jnp.sum(base * (curved - 2.0 * ridge * output))
    square = jnp.sum(square_ref[...]) * own_ref[0]
    lane = lax.broadcasted_iota(jnp.int32, sums_ref.shape[1:], 1)
    sums = jnp.where(lane == 0, norm + ridge * ridge * square, 0.0)
    for index, value in enumerate((jnp.sum(zero * zero), jnp.sum(zero * one), jnp.sum(one * one))):
        sums = jnp.where(lane == index + 1, value, sums)
    for part in range(sums_ref.shape[0]):
        sums_ref[part] = sums


def finish_kernel(ridge, base_ref, zero_ref, one_ref, sums_ref, *out_refs):
    sums = jnp.sum(sums_ref[...], axis=0)[0:1, :]
    norm, zero_zero = sums[:, 0:1], sums[:, 1:2]
    zero_one, one_one = sums[:, 2:3], sums[:, 3:4]
    step = norm / (zero_zero + ridge * norm)
    left = 1.0 - step * ridge
    new = left * left * norm - 2.0 * left * step * zero_zero + step * step * zero_one
    ratio = new / norm
    grown = left + ratio
    image = grown * grown * zero_zero - 2.0 * grown * step * zero_one + step * step * one_one
    later = new / (image + ridge * (new + ratio * ratio * norm))
    field = base_ref[...] - (step + later * grown) * zero_ref[...] + (later * step) * one_ref[...]
    rows = field.shape[0] // len(out_refs)
    sideways = field.T.astype(bf16)
    for block, ref in enumerate(out_refs):
        ref[...] = sideways[:, block * rows : (block + 1) * rows]


def join_kernel(blocks, tensor_count, place_ref, *refs):
    pieces, (out_ref, rows_ref) = refs[:-2], refs[-2:]
    lanes = pieces[0].shape[0]
    for back in range(blocks):
        for aside in range(tensor_count):
            part = lax.rem(place_ref[0] + blocks - back, blocks) * tensor_count
            part = part + lax.rem(place_ref[1] + tensor_count - aside, tensor_count)
            start = pl.multiple_of(part * lanes, 8)
            rows_ref[pl.ds(start, lanes), :] = pieces[back * tensor_count + aside][...].astype(f32)
    out_ref[...] = rows_ref[...].T


def single(kernel, out_shape, in_specs, mib, name, scratch=()):
    many = isinstance(out_shape, list)
    return pl.pallas_call(
        kernel,
        out_shape=out_shape,
        in_specs=in_specs,
        out_specs=[whole()] * len(out_shape) if many else whole(),
        scratch_shapes=list(scratch),
        compiler_params=params(mib),
        cost_estimate=LIGHT,
        name=name,
    )


def one_expert_each(tokens, routes, route_logits, kept_experts, gate_weight, up_weight, down_weight):
    dp_count = lax.axis_size("dp")
    tensor_count = lax.axis_size("tensor")
    parts = dp_count * tensor_count
    tok_rows, depth = tokens.shape
    units, columns = down_weight.shape
    slots = dp_count * CAP
    lanes = columns // parts
    width = units // 4 // CHUNKS
    ridge = ridge_share * 2.0 * tok_rows * dp_count / E
    dp_index = lax.axis_index("dp")
    tensor_index = lax.axis_index("tensor")
    col_index = lax.axis_index("col")
    own_expert = dp_index * tensor_count + tensor_index
    place = jnp.stack([dp_index, tensor_index])

    def beside(values):
        return lax.ppermute(values, "col", [(k, k ^ 1) for k in range(4)])

    def across(values):
        return lax.ppermute(values, "col", [(k, k ^ 2) for k in range(4)])

    def shifted(values, ahead, aside=0):
        if ahead == 0 and aside == 0:
            return values
        pairs = [
            (i * tensor_count + j, (i + ahead) % dp_count * tensor_count + (j + aside) % tensor_count)
            for i in range(dp_count)
            for j in range(tensor_count)
        ]
        return lax.ppermute(values, ("dp", "tensor"), pairs)

    shifts = [(ahead, aside) for ahead in range(dp_count) for aside in range(tensor_count)]
    info, *picked = single(
        functools.partial(pick_kernel, dp_count, tensor_count),
        [jax.ShapeDtypeStruct((4, tok_rows), f32)] + [jax.ShapeDtypeStruct((CAP, depth), bf16)] * dp_count,
        [scalars(), whole(), whole(), whole()],
        16,
        "pick",
    )(place, routes.T, route_logits.T, tokens)
    arrived = [shifted(value, ahead) for ahead, value in enumerate(picked)]
    inputs = single(
        turn_kernel,
        jax.ShapeDtypeStruct((depth, slots), bf16),
        [whole()] * dp_count,
        16,
        "turn",
    )(*arrived)

    gate_order = col_index ^ jnp.array([2, 0, 3, 1], jnp.int32)
    down_order = col_index ^ jnp.array([0, 2, 1, 3], jnp.int32)

    def products(keep, send, after=()):
        return gate_up(gate_order, inputs, gate_weight, up_weight, width, keep, send, after)

    last = CHUNKS - 1
    keeps, nears, pairs, fars, owns = [], [], [], [], []

    def activate(chunk, after):
        far = lax.optimization_barrier((fars[chunk], *after))[0] if after else fars[chunk]
        total = keeps[chunk][1].astype(f32) + nears[chunk][1].astype(f32) + far.astype(f32)
        owns.append((jax.nn.silu(total[0]) * total[1]).astype(bf16))

    nears.append(beside(products(None, 0)[0]))
    for chunk in range(CHUNKS):
        after = []
        if chunk >= 2:
            after = after + [fars[chunk - 2]]
        if chunk >= 3:
            activate(chunk - 3, [])
            after = after + [owns[chunk - 3]]
        if chunk < last:
            keep, send = products(chunk, chunk + 1, after)
            nears.append(beside(send))
        else:
            (keep,) = products(chunk, None, after)
        keeps.append(keep)
        pairs.append((keep[0].astype(f32) + nears[chunk][0].astype(f32)).astype(bf16))
        fars.append(across(pairs[-1]))
    older, olders = (), []
    for chunk in range(CHUNKS):
        if chunk >= len(owns):
            after = [pairs[last]]
            if chunk >= 2:
                after.append(olders[chunk - 2][2])
            if chunk == last:
                info = lax.optimization_barrier((info, owns[chunk - 1]))[0]
                infos = [shifted(info, ahead) for ahead in range(dp_count)]
                after.extend(infos[1:])
            activate(chunk, after)
        own = owns[chunk]
        other = across(own)
        older = down(
            down_order,
            place,
            (own, other, beside(own), beside(other)),
            down_weight,
            chunk,
            older,
            (dp_count, tensor_count) if chunk == last else None,
        )
        olders.append(older)
    packed, (_, _, square) = older[:parts], older[parts:]
    spread = [shifted(value, *shift) for value, shift in zip(packed, shifts)]

    total_slots, total_tokens = E * slots, dp_count * tok_rows
    hot, turned_hot, gates = single(
        functools.partial(route_kernel, dp_count, tensor_count),
        [
            jax.ShapeDtypeStruct((total_slots, total_tokens), bf16),
            jax.ShapeDtypeStruct((total_tokens, total_slots), bf16),
            jax.ShapeDtypeStruct((total_slots, 2), f32),
        ],
        [scalars(), scalars()] + [whole()] * dp_count + [pl.BlockSpec(memory_space=pl.ANY)],
        24,
        "route",
        [pltpu.VMEM((total_slots, total_tokens), f32)],
    )(kept_experts, place, *infos, square)
    is_kept = jnp.any(kept_experts == own_expert).astype(f32).reshape(1)
    field = jax.ShapeDtypeStruct((total_tokens, lanes), f32)
    everyone = parts * lax.axis_size("col")
    base, zero, one, sums = single(
        functools.partial(solve_kernel, ridge, slots),
        [field, field, field, jax.ShapeDtypeStruct((everyone, 1, 128), f32)],
        [scalars()] + [whole()] * (4 + E),
        40,
        "solve",
    )(is_kept, hot, turned_hot, gates, square, *spread)
    sums = lax.all_to_all(sums, ("dp", "tensor", "col"), split_axis=0, concat_axis=0, tiled=True)

    home = single(
        functools.partial(finish_kernel, ridge),
        [jax.ShapeDtypeStruct((lanes, tok_rows), bf16)] * dp_count,
        [whole()] * 4,
        16,
        "finish",
    )(base, zero, one, sums)
    pieces = [shifted(home[-ahead % dp_count], ahead, aside) for ahead, aside in shifts]
    return single(
        functools.partial(join_kernel, dp_count, tensor_count),
        jax.ShapeDtypeStruct((tok_rows, columns), f32),
        [scalars()] + [whole()] * parts,
        16,
        "join",
        [pltpu.VMEM((columns, tok_rows), f32)],
    )(place, *pieces)


def spread_copies(values, experts, held_count, copies):
    old_shape = values.shape
    grouped = values.reshape((experts // held_count, 1, held_count) + old_shape[1:])
    widened = jnp.broadcast_to(grouped, (experts // held_count, copies, held_count) + old_shape[1:])
    return widened.reshape((experts // held_count * copies, held_count) + old_shape[1:])


def expert_major(returned, experts, held_count, copies):
    old_shape = returned.shape
    grouped = returned.reshape((experts // held_count, copies, held_count) + old_shape[2:])
    merged = jnp.sum(grouped, axis=1)
    return merged.reshape((experts * old_shape[2],) + old_shape[3:])


def exact_product(left, right, contract):
    return lax.dot_general(
        left, right, contract, precision=top_precision, preferred_element_type=jnp.float32
    )


def general(tokens, routes, route_logits, kept_experts, gate_weight, up_weight, down_weight):
    dp_count = lax.axis_size("dp")
    tensor_count = lax.axis_size("tensor")
    held_count = max(1, E // dp_count)
    copies = max(1, dp_count // E)
    tok_rows = tokens.shape[0]
    piece_rows = gate_weight.shape[0]
    FF = piece_rows * dp_count * tensor_count // E
    slot_total = E * CAP
    device_rank = lax.axis_index("dp") * tensor_count + lax.axis_index("tensor")
    own_expert = device_rank * piece_rows // FF
    own_group = own_expert % held_count
    expert_ids = jnp.arange(E, dtype=jnp.int32)
    kept_table = jnp.any(kept_experts[:, None] == expert_ids[None, :], axis=0).astype(jnp.float32)
    own_kept = jnp.sum(jnp.where(expert_ids == own_expert, kept_table, 0.0))
    route_experts = routes.reshape(-1)
    route_onehot = (route_experts[:, None] == expert_ids[None, :]).astype(jnp.int32)
    route_rank = jnp.sum((jnp.cumsum(route_onehot, axis=0) - route_onehot) * route_onehot, axis=1)
    route_slot = route_experts * CAP + route_rank
    gate_probs = jax.nn.softmax(route_logits, axis=-1).reshape(-1)
    route_kept = jnp.sum(route_onehot.astype(jnp.float32) * kept_table[None, :], axis=1)
    slot_match = (jnp.arange(slot_total, dtype=jnp.int32)[:, None] == route_slot[None, :]).astype(
        jnp.float32
    )
    pick_tokens = slot_match.reshape(slot_total, tok_rows, 2).sum(axis=2)
    kept_weights = (
        (slot_match * (gate_probs * route_kept)[None, :])
        .reshape(slot_total, tok_rows, 2)
        .sum(axis=2)
    )
    dropped_weights = (
        (slot_match * (gate_probs * (1.0 - route_kept))[None, :])
        .reshape(slot_total, tok_rows, 2)
        .sum(axis=2)
    )
    by_expert = jnp.dot(
        pick_tokens.astype(jnp.bfloat16), tokens, preferred_element_type=jnp.float32
    ).astype(jnp.bfloat16)
    outgoing = spread_copies(by_expert.reshape(E, CAP, -1), E, held_count, copies)
    chosen = lax.dynamic_index_in_dim(
        lax.all_to_all(outgoing, "dp", split_axis=0, concat_axis=0, tiled=True),
        own_group,
        1,
        keepdims=False,
    )
    contract = (((2,), (1,)), ((), ()))
    gate_part = lax.dot_general(chosen, gate_weight, contract, preferred_element_type=jnp.float32)
    up_part = lax.dot_general(chosen, up_weight, contract, preferred_element_type=jnp.float32)
    gate_part, up_part = (gate_part, up_part)
    gate_sum, up_sum = (
        lax.psum(gate_part.astype(jnp.bfloat16), "col").astype(jnp.float32),
        lax.psum(up_part.astype(jnp.bfloat16), "col").astype(jnp.float32),
    )
    hidden = (jax.nn.silu(gate_sum) * up_sum).astype(jnp.bfloat16)
    expert_out = lax.dot_general(
        hidden, down_weight, (((2,), (0,)), ((), ())), preferred_element_type=jnp.float32
    ).astype(jnp.bfloat16)
    hidden_wide = hidden.astype(jnp.float32)
    group_mask = (jnp.arange(held_count) == own_group)[None, :, None, None]
    placed = jnp.where(group_mask, expert_out[:, None], jnp.zeros((), jnp.bfloat16))
    returned = lax.all_to_all(placed, "dp", split_axis=0, concat_axis=0, tiled=True)
    slot_values = expert_major(returned.astype(jnp.float32), E, held_count, copies)
    dropped_part = jnp.dot(dropped_weights.T, slot_values, precision=top_precision)
    dropped = lax.psum(dropped_part, "tensor")
    ridge_weight = ridge_share * 2.0 * tok_rows * dp_count / E

    def apply_backward(image_tokens):
        slot_image = jnp.dot(kept_weights, image_tokens, precision=top_precision)
        outgoing_image = spread_copies(slot_image.reshape(E, CAP, -1), E, held_count, copies)
        arrived = lax.all_to_all(outgoing_image, "dp", split_axis=0, concat_axis=0, tiled=True)
        chosen = lax.dynamic_index_in_dim(arrived, own_group, 1, keepdims=False)
        return exact_product(hidden_wide, chosen, (((0, 1), (0, 1)), ((), ())))

    def total_norm(values):
        return lax.psum(jnp.sum(values * values), ("dp", "tensor", "col"))

    base_down = down_weight.astype(jnp.float32)
    residual = apply_backward(dropped) - ridge_weight * own_kept * base_down
    res_norm = total_norm(residual)
    direction = residual
    leftover = dropped
    for turn_index in range(ITERS):
        slot_part = exact_product(hidden_wide, direction, (((2,), (0,)), ((), ())))
        placed_part = jnp.where(group_mask, slot_part[:, None], 0.0)
        came_back = lax.all_to_all(placed_part, "dp", split_axis=0, concat_axis=0, tiled=True)
        image_part = jnp.dot(
            kept_weights.T, expert_major(came_back, E, held_count, copies), precision=top_precision
        )
        image_tokens = lax.psum(image_part, "tensor")
        first_copy = (lax.axis_index("tensor") == 0).astype(jnp.float32)
        local_term = first_copy * jnp.sum(image_tokens * image_tokens) + ridge_weight * jnp.sum(
            direction * direction
        )
        curvature = lax.psum(local_term, ("dp", "tensor", "col"))
        step_size = res_norm / curvature
        leftover = leftover - step_size * image_tokens
        if turn_index + 1 < ITERS:
            curved = apply_backward(image_tokens) + ridge_weight * direction
            residual = residual - step_size * curved
            next_norm = total_norm(residual)
            direction = residual + next_norm / res_norm * direction
            res_norm = next_norm
    return leftover


def shards(*arrays):
    sizes = [lax.axis_size(axis) for axis in ("dp", "tensor", "col")]
    if sizes[0] * sizes[1] == E and sizes[2] == 4 and ITERS == 2:
        return one_expert_each(*arrays)
    return general(*arrays)


def solution(mesh):
    placed = (
        P("dp", "col"),
        P("dp", None),
        P("dp", None),
        P(),
        P(("dp", "tensor"), "col"),
        P(("dp", "tensor"), "col"),
        P(("dp", "tensor"), "col"),
    )
    return jax.shard_map(
        shards, mesh=mesh, in_specs=placed, out_specs=P("dp", "col"), check_vma=False
    )
```

```python
import functools

import jax
import jax.numpy as jnp
from jax import lax
from jax.experimental import pallas as pl
from jax.experimental.pallas import tpu as pltpu
from jax.sharding import PartitionSpec as P

E = 8
ITERS = 2
CAP = 40
CHUNKS = 4


ridge_share = 0.25
top_precision = lax.Precision.HIGHEST
MIB = 1024 * 1024
LIGHT = pl.CostEstimate(flops=1, bytes_accessed=1, transcendentals=0)
f32 = jnp.float32
bf16 = jnp.bfloat16
NT = (((1,), (1,)), ((), ()))
NN = (((1,), (0,)), ((), ()))
TN = (((0,), (0,)), ((), ()))


def whole():
    return pl.BlockSpec(memory_space=pltpu.VMEM)


def scalars():
    return pl.BlockSpec(memory_space=pltpu.SMEM)


def mm(left, right, contract=NN):
    return lax.dot_general(left, right, contract, preferred_element_type=f32)


def split_wide(values):
    high = values.astype(bf16)
    low = (values - high.astype(f32)).astype(bf16)
    return jnp.concatenate([high, low], axis=1)


def mm_wide(left, right, contract=NN):
    lanes = right.shape[1]
    both = mm(left, split_wide(right), contract)
    return both[:, :lanes] + both[:, lanes:]


def params(mib):
    return pltpu.CompilerParams(vmem_limit_bytes=mib * MIB)


def block_slots(first, second):
    count = first.shape[1]
    expert_rows = lax.broadcasted_iota(jnp.int32, (E, count), 0).astype(f32)
    hot_first = (expert_rows == first).astype(f32)
    hot_second = (expert_rows == second).astype(f32)
    before = (
        lax.broadcasted_iota(jnp.int32, (count, count), 0)
        < lax.broadcasted_iota(jnp.int32, (count, count), 1)
    ).astype(bf16)
    place = mm((hot_first + hot_second).astype(bf16), before)
    ranked_first = jnp.sum(hot_first * place, axis=0, keepdims=True)
    ranked_second = jnp.sum(hot_second * place, axis=0, keepdims=True)
    return ranked_first, ranked_second


def pick_kernel(parts, tensor_count, place_ref, info_ref, tokens_ref, *out_refs):
    first, second = info_ref[0:1, :], info_ref[1:2, :]
    rank_first, rank_second = block_slots(first, second)
    count = first.shape[1]
    rows = lax.broadcasted_iota(jnp.int32, (CAP, count), 0).astype(f32)
    values = tokens_ref[...]
    for shift, out_ref in enumerate(out_refs):
        expert = (lax.rem(place_ref[0] + shift, parts) * tensor_count + place_ref[1]).astype(f32)
        hit = ((first == expert) & (rank_first == rows)) | ((second == expert) & (rank_second == rows))
        out_ref[...] = mm(hit.astype(f32).astype(bf16), values).astype(bf16)


def stack_kernel(*refs):
    pieces = refs[: (len(refs) - 1) // 2]
    refs[-1][...] = jnp.concatenate([ref[...].astype(f32) for ref in pieces], axis=0).astype(bf16)


def gate_up_kernel(has_keep, order_ref, inputs_ref, gate_ref, up_ref, *rest):
    values = inputs_ref[...]
    gate = mm(values, gate_ref[...], NT).astype(bf16)
    up = mm(values, up_ref[...], NT).astype(bf16)
    step = pl.program_id(0)
    outs = rest[-(1 + (has_keep == 2)) :]
    for index, ref in enumerate(outs):

        @pl.when(step // 2 == index)
        def _(ref=ref):
            ref[0, 0] = gate
            ref[0, 1] = up


def gate_up(order, inputs, gate_weight, up_weight, width, keep, send, after):
    slots, depth = inputs.shape
    quarter = gate_weight.shape[0] // 4
    gate_weight = gate_weight.reshape(4, quarter, depth)
    up_weight = up_weight.reshape(4, quarter, depth)
    base = 0 if keep is not None else 2
    chunks = [chunk for chunk in (keep, send) if chunk is not None]
    count = len(chunks)

    def place(s, order):
        return (order[base + s], chunks[0] if count == 1 else jnp.where(s < 2, chunks[0], chunks[1]), 0)

    weight_spec = pl.BlockSpec((None, width, depth), place)
    out_specs = [
        pl.BlockSpec(
            (1, 2, slots, width),
            lambda s, order, index=index: (jnp.clip(s - 2 * index, 0, 1), 0, 0, 0),
        )
        for index in range(count)
    ]
    return pl.pallas_call(
        functools.partial(gate_up_kernel, count),
        grid_spec=pltpu.PrefetchScalarGridSpec(
            num_scalar_prefetch=1,
            grid=(2 * count,),
            in_specs=[
                pl.BlockSpec((slots, depth), lambda s, order: (0, 0)),
                weight_spec,
                weight_spec,
            ]
            + [pl.BlockSpec(memory_space=pl.ANY)] * len(after),
            out_specs=out_specs,
        ),
        out_shape=[jax.ShapeDtypeStruct((2, 2, slots, width), bf16)] * count,
        compiler_params=params(41),
        cost_estimate=pl.CostEstimate(
            flops=32 * count * slots * depth * width,
            bytes_accessed=32 * count * width * depth,
            transcendentals=0,
        ),
        name=f"gate_up_{chunks[-1] + (send is None)}",
    )(order, inputs, gate_weight, up_weight, *after)


def down_kernel(count, pack, has_old, order_ref, place_ref, *refs):
    pieces, down_ref, rest = refs[:count], refs[count], refs[count + 1 :]
    old, new = rest[:3] if has_old else (), rest[3 * has_old :]
    packed_refs = ()
    if pack:
        packed_refs, new = new[:-3], new[-3:]
    step = pl.program_id(0)

    @pl.when(step == 0)
    def _():
        for index, ref in enumerate(new):
            ref[...] = old[index][...] if old else jnp.zeros_like(ref)

    out_ref, gram_ref, square_ref = new
    weight = down_ref[...]
    wide = weight.astype(f32)
    square_ref[...] += jnp.sum((wide * wide).reshape(-1, 8, wide.shape[1]), axis=0)
    for index, ref in enumerate(pieces):

        @pl.when(step == index)
        def _(ref=ref, index=index):
            values = ref[...]
            out_ref[...] += mm(values, weight)
            gram_ref[...] += mm(values, values, NT)
            if pack and index == len(pieces) - 1:
                dp_count, tensor_count = pack
                columns = out_ref.shape[1]
                lanes = columns // (dp_count * tensor_count)
                group = columns // dp_count
                gram = gram_ref[...]
                rolled = pltpu.roll(out_ref[...], lax.rem(columns - place_ref[0] * group, columns), 1)
                for ahead in range(dp_count):
                    parts = [
                        rolled[:, ahead * group + part * lanes : ahead * group + (part + 1) * lanes]
                        for part in range(tensor_count)
                    ]
                    for aside in range(tensor_count):
                        target = lax.rem(place_ref[1] + aside, tensor_count)
                        piece = parts[0]
                        for part in range(1, tensor_count):
                            piece = jnp.where(target == part, parts[part], piece)
                        packed_refs[ahead * tensor_count + aside][...] = jnp.concatenate(
                            [gram, piece], axis=1
                        ).astype(bf16)


def down(order, place, pieces, down_weight, chunk, older, first=0, pack=None):
    slots, width = pieces[0].shape
    columns = down_weight.shape[1]
    down_weight = down_weight.reshape(4, -1, columns)

    def fixed(shape):
        return pl.BlockSpec(shape, lambda s, order, place: (0,) * len(shape))

    shapes = [(slots, columns), (slots, slots), (8, columns)]
    out_shape = [jax.ShapeDtypeStruct(shape, f32) for shape in shapes]
    if pack:
        parts = pack[0] * pack[1]
        packed = (slots, slots + columns // parts)
        out_shape = [jax.ShapeDtypeStruct(packed, bf16)] * parts + out_shape
    return pl.pallas_call(
        functools.partial(down_kernel, len(pieces), pack, bool(older)),
        grid_spec=pltpu.PrefetchScalarGridSpec(
            num_scalar_prefetch=2,
            grid=(len(pieces),),
            in_specs=[fixed((slots, width))] * len(pieces)
            + [pl.BlockSpec((None, width, columns), lambda s, order, place: (order[first + s], chunk, 0))]
            + [fixed(value.shape) for value in older],
            out_specs=[fixed(value.shape) for value in out_shape],
        ),
        out_shape=out_shape,
        compiler_params=params(20),
        cost_estimate=LIGHT,
        name=f"down_{chunk}_{first}",
    )(order, place, *pieces, down_weight, *older)


def route_kernel(blocks, tensor_count, kept_ref, place_ref, *refs):
    infos = refs[:blocks]
    hot_ref, turned_ref, gates_ref, wide_ref = refs[-4:]
    count = infos[0].shape[1]
    slots = blocks * CAP
    zero = jnp.zeros((CAP, count), f32)
    rows = lax.broadcasted_iota(jnp.int32, (CAP, count), 0).astype(f32)
    routed = []
    for block in range(blocks):
        first, second = infos[block][0:1, :], infos[block][1:2, :]
        delta = infos[block][3:4, :] - infos[block][2:3, :]
        share_first = 1.0 / (1.0 + jnp.exp(delta))
        share_second = 1.0 / (1.0 + jnp.exp(-delta))
        routed.append((first, second, share_first, share_second) + block_slots(first, second))
    for back in range(blocks):
        for aside in range(tensor_count):
            expert = lax.rem(place_ref[0] + blocks - back, blocks) * tensor_count
            expert = expert + lax.rem(place_ref[1] + tensor_count - aside, tensor_count)
            kept = jnp.zeros((), jnp.int32)
            for index in range(kept_ref.shape[0]):
                kept = kept | (kept_ref[index] == expert).astype(jnp.int32)
            kept, expert = kept.astype(f32), expert.astype(f32)
            for shift in range(blocks):
                block = (back + shift) % blocks
                first, second, share_first, share_second, rank_first, rank_second = routed[block]
                hit_first = (first == expert) & (rank_first == rows)
                hit_second = (second == expert) & (rank_second == rows)
                gate = jnp.sum(
                    jnp.where(hit_first, share_first, zero) + jnp.where(hit_second, share_second, zero),
                    axis=1,
                    keepdims=True,
                )
                row = (back * tensor_count + aside) * slots + shift * CAP
                for other in range(blocks):
                    wide_ref[row : row + CAP, other * count : (other + 1) * count] = (
                        (hit_first | hit_second).astype(f32) if other == block else zero
                    )
                gates_ref[row : row + CAP, 0:1] = gate * kept
                gates_ref[row : row + CAP, 1:2] = gate * (1.0 - kept)
    hot_ref[...] = wide_ref[...].astype(bf16)
    turned_ref[...] = wide_ref[...].T.astype(bf16)


def solve_kernel(ridge, slots, own_ref, hot_ref, turned_ref, gates_ref, square_ref, *refs):
    packed_refs, (base_ref, zero_ref, one_ref, sums_ref) = refs[:E], refs[E:]
    hot, turned = hot_ref[...], turned_ref[...]
    kept, dropped = gates_ref[:, 0:1], gates_ref[:, 1:2]
    values = jnp.concatenate([packed_refs[e][:, slots:].astype(f32) for e in range(E)], axis=0)
    base = mm_wide(turned, dropped * values)
    output = mm_wide(turned, kept * values)

    def apply(field):
        spread = kept * mm_wide(hot, field)
        mixed = jnp.concatenate(
            [
                mm_wide(packed_refs[e][:, :slots], spread[e * slots : (e + 1) * slots])
                for e in range(E)
            ],
            axis=0,
        )
        return mm_wide(turned, kept * mixed)

    curved = apply(base)
    zero = curved - ridge * output
    one = apply(zero)
    base_ref[...] = base
    zero_ref[...] = zero
    one_ref[...] = one
    norm = jnp.sum(base * (curved - 2.0 * ridge * output))
    square = jnp.sum(square_ref[...]) * own_ref[0]
    lane = lax.broadcasted_iota(jnp.int32, sums_ref.shape[1:], 1)
    sums = jnp.where(lane == 0, norm + ridge * ridge * square, 0.0)
    for index, value in enumerate((jnp.sum(zero * zero), jnp.sum(zero * one), jnp.sum(one * one))):
        sums = jnp.where(lane == index + 1, value, sums)
    for part in range(sums_ref.shape[0]):
        sums_ref[part] = sums


def finish_kernel(ridge, blocks, copies, place_ref, base_ref, zero_ref, one_ref, sums_ref, out_ref):
    sums = jnp.sum(sums_ref[...], axis=0)[0:1, :]
    norm, zero_zero = sums[:, 0:1], sums[:, 1:2]
    zero_one, one_one = sums[:, 2:3], sums[:, 3:4]
    step = norm / (zero_zero + ridge * norm)
    left = 1.0 - step * ridge
    new = left * left * norm - 2.0 * left * step * zero_zero + step * step * zero_one
    ratio = new / norm
    grown = left + ratio
    image = grown * grown * zero_zero - 2.0 * grown * step * zero_one + step * step * one_one
    later = new / (image + ridge * (new + ratio * ratio * norm))
    field = base_ref[...] - (step + later * grown) * zero_ref[...] + (later * step) * one_ref[...]
    rows = field.shape[0] // blocks
    sideways = field.T.astype(bf16)
    for back in range(blocks):
        target = lax.rem(place_ref[0] + blocks - back, blocks) * copies
        for copy in range(copies):
            out_ref[target + copy] = sideways[:, back * rows : (back + 1) * rows]


def join_kernel(pieces_ref, out_ref):
    rows = jnp.concatenate([pieces_ref[part].astype(f32) for part in range(pieces_ref.shape[0])], axis=0)
    out_ref[...] = rows.T


def single(kernel, out_shape, in_specs, mib, name, scratch=()):
    many = isinstance(out_shape, list)
    return pl.pallas_call(
        kernel,
        out_shape=out_shape,
        in_specs=in_specs,
        out_specs=[whole()] * len(out_shape) if many else whole(),
        scratch_shapes=list(scratch),
        compiler_params=params(mib),
        cost_estimate=LIGHT,
        name=name,
    )


def one_expert_each(tokens, routes, route_logits, kept_experts, gate_weight, up_weight, down_weight):
    dp_count = lax.axis_size("dp")
    tensor_count = lax.axis_size("tensor")
    parts = dp_count * tensor_count
    tok_rows, depth = tokens.shape
    units, columns = down_weight.shape
    slots = dp_count * CAP
    lanes = columns // parts
    width = units // 4 // CHUNKS
    ridge = ridge_share * 2.0 * tok_rows * dp_count / E
    dp_index = lax.axis_index("dp")
    tensor_index = lax.axis_index("tensor")
    col_index = lax.axis_index("col")
    own_expert = dp_index * tensor_count + tensor_index
    place = jnp.stack([dp_index, tensor_index])

    def beside(values):
        return lax.ppermute(values, "col", [(k, k ^ 1) for k in range(4)])

    def across(values):
        return lax.ppermute(values, "col", [(k, k ^ 2) for k in range(4)])

    def shifted(values, ahead, aside=0):
        if ahead == 0 and aside == 0:
            return values
        pairs = [
            (i * tensor_count + j, (i + ahead) % dp_count * tensor_count + (j + aside) % tensor_count)
            for i in range(dp_count)
            for j in range(tensor_count)
        ]
        return lax.ppermute(values, ("dp", "tensor"), pairs)

    shifts = [(ahead, aside) for ahead in range(dp_count) for aside in range(tensor_count)]
    upper = lax.pad(routes.T, jnp.int32(0), ((0, 2, 0), (0, 0, 0))).astype(f32)
    info = upper + lax.pad(route_logits.T, f32(0), ((2, 0, 0), (0, 0, 0)))
    picked = single(
        functools.partial(pick_kernel, dp_count, tensor_count),
        [jax.ShapeDtypeStruct((CAP, depth), bf16)] * dp_count,
        [scalars(), whole(), whole()],
        16,
        "pick",
    )(place, info, tokens)
    arrived = [shifted(value, ahead) for ahead, value in enumerate(picked)]
    info = lax.optimization_barrier((info, arrived[1]))[0]
    infos = [shifted(info, ahead) for ahead in range(dp_count)]
    inputs = single(
        stack_kernel,
        jax.ShapeDtypeStruct((slots, depth), bf16),
        [whole()] * dp_count + [pl.BlockSpec(memory_space=pl.ANY)] * dp_count,
        16,
        "stack",
    )(*arrived, *infos)

    gate_order = col_index ^ jnp.array([2, 0, 3, 1], jnp.int32)
    down_order = col_index ^ jnp.array([0, 2, 1, 3], jnp.int32)

    def products(keep, send, after=()):
        return gate_up(gate_order, inputs, gate_weight, up_weight, width, keep, send, after)

    last = CHUNKS - 1
    keeps, nears, pairs, fars, owns = [], [], [], [], []

    def activate(chunk, after):
        far = lax.optimization_barrier((fars[chunk], *after))[0] if after else fars[chunk]
        total = keeps[chunk][1].astype(f32) + nears[chunk][1].astype(f32) + far.astype(f32)
        owns.append((jax.nn.silu(total[0]) * total[1]).astype(bf16))

    nears.append(beside(products(None, 0)[0]))
    for chunk in range(CHUNKS):
        after = [keeps[-1]] if chunk else []
        if chunk >= 2:
            after.extend([fars[chunk - 2], pairs[chunk - 1]])
        if chunk < last:
            keep, send = products(chunk, chunk + 1, after)
            nears.append(beside(send))
        else:
            (keep,) = products(chunk, None, after)
        keeps.append(keep)
        pairs.append((keep[0].astype(f32) + nears[chunk][0].astype(f32)).astype(bf16))
        fars.append(across(pairs[-1]))
    older, olders = (), []
    for chunk in range(CHUNKS):
        if chunk >= len(owns):
            after = [pairs[last]]
            if chunk >= 2:
                after.append(olders[chunk - 2][2])
            activate(chunk, after)
        own = owns[chunk]
        other = across(own)
        pieces = (own, other, beside(own), beside(other))
        if chunk < last:
            older = down(down_order, place, pieces, down_weight, chunk, older)
        else:
            older = down(down_order, place, pieces[:3], down_weight, chunk, older)
            older = down(
                down_order, place, pieces[3:], down_weight, chunk, older, 3, (dp_count, tensor_count)
            )
        olders.append(older)
    packed, (_, _, square) = older[:parts], older[parts:]
    spread = [shifted(value, *shift) for value, shift in zip(packed, shifts)]

    total_slots, total_tokens = E * slots, dp_count * tok_rows
    hot, turned_hot, gates = single(
        functools.partial(route_kernel, dp_count, tensor_count),
        [
            jax.ShapeDtypeStruct((total_slots, total_tokens), bf16),
            jax.ShapeDtypeStruct((total_tokens, total_slots), bf16),
            jax.ShapeDtypeStruct((total_slots, 2), f32),
        ],
        [scalars(), scalars()] + [whole()] * dp_count + [pl.BlockSpec(memory_space=pl.ANY)],
        24,
        "route",
        [pltpu.VMEM((total_slots, total_tokens), f32)],
    )(kept_experts, place, *infos, square)
    is_kept = jnp.any(kept_experts == own_expert).astype(f32).reshape(1)
    field = jax.ShapeDtypeStruct((total_tokens, lanes), f32)
    everyone = parts * lax.axis_size("col")
    base, zero, one, sums = single(
        functools.partial(solve_kernel, ridge, slots),
        [field, field, field, jax.ShapeDtypeStruct((everyone, 1, 128), f32)],
        [scalars()] + [whole()] * (4 + E),
        40,
        "solve",
    )(is_kept, hot, turned_hot, gates, square, *spread)
    sums = lax.all_to_all(sums, ("dp", "tensor", "col"), split_axis=0, concat_axis=0, tiled=True)

    home = single(
        functools.partial(finish_kernel, ridge, dp_count, tensor_count),
        jax.ShapeDtypeStruct((parts, lanes, tok_rows), bf16),
        [scalars()] + [whole()] * 4,
        16,
        "finish",
    )(place, base, zero, one, sums)
    home = lax.all_to_all(home, ("dp", "tensor"), split_axis=0, concat_axis=0, tiled=True)
    return single(
        join_kernel,
        jax.ShapeDtypeStruct((tok_rows, columns), f32),
        [whole()],
        16,
        "join",
    )(home)


def spread_copies(values, experts, held_count, copies):
    old_shape = values.shape
    grouped = values.reshape((experts // held_count, 1, held_count) + old_shape[1:])
    widened = jnp.broadcast_to(grouped, (experts // held_count, copies, held_count) + old_shape[1:])
    return widened.reshape((experts // held_count * copies, held_count) + old_shape[1:])


def expert_major(returned, experts, held_count, copies):
    old_shape = returned.shape
    grouped = returned.reshape((experts // held_count, copies, held_count) + old_shape[2:])
    merged = jnp.sum(grouped, axis=1)
    return merged.reshape((experts * old_shape[2],) + old_shape[3:])


def exact_product(left, right, contract):
    return lax.dot_general(
        left, right, contract, precision=top_precision, preferred_element_type=jnp.float32
    )


def general(tokens, routes, route_logits, kept_experts, gate_weight, up_weight, down_weight):
    dp_count = lax.axis_size("dp")
    tensor_count = lax.axis_size("tensor")
    held_count = max(1, E // dp_count)
    copies = max(1, dp_count // E)
    tok_rows = tokens.shape[0]
    piece_rows = gate_weight.shape[0]
    FF = piece_rows * dp_count * tensor_count // E
    slot_total = E * CAP
    device_rank = lax.axis_index("dp") * tensor_count + lax.axis_index("tensor")
    own_expert = device_rank * piece_rows // FF
    own_group = own_expert % held_count
    expert_ids = jnp.arange(E, dtype=jnp.int32)
    kept_table = jnp.any(kept_experts[:, None] == expert_ids[None, :], axis=0).astype(jnp.float32)
    own_kept = jnp.sum(jnp.where(expert_ids == own_expert, kept_table, 0.0))
    route_experts = routes.reshape(-1)
    route_onehot = (route_experts[:, None] == expert_ids[None, :]).astype(jnp.int32)
    route_rank = jnp.sum((jnp.cumsum(route_onehot, axis=0) - route_onehot) * route_onehot, axis=1)
    route_slot = route_experts * CAP + route_rank
    gate_probs = jax.nn.softmax(route_logits, axis=-1).reshape(-1)
    route_kept = jnp.sum(route_onehot.astype(jnp.float32) * kept_table[None, :], axis=1)
    slot_match = (jnp.arange(slot_total, dtype=jnp.int32)[:, None] == route_slot[None, :]).astype(
        jnp.float32
    )
    pick_tokens = slot_match.reshape(slot_total, tok_rows, 2).sum(axis=2)
    kept_weights = (
        (slot_match * (gate_probs * route_kept)[None, :])
        .reshape(slot_total, tok_rows, 2)
        .sum(axis=2)
    )
    dropped_weights = (
        (slot_match * (gate_probs * (1.0 - route_kept))[None, :])
        .reshape(slot_total, tok_rows, 2)
        .sum(axis=2)
    )
    by_expert = jnp.dot(
        pick_tokens.astype(jnp.bfloat16), tokens, preferred_element_type=jnp.float32
    ).astype(jnp.bfloat16)
    outgoing = spread_copies(by_expert.reshape(E, CAP, -1), E, held_count, copies)
    chosen = lax.dynamic_index_in_dim(
        lax.all_to_all(outgoing, "dp", split_axis=0, concat_axis=0, tiled=True),
        own_group,
        1,
        keepdims=False,
    )
    contract = (((2,), (1,)), ((), ()))
    gate_part = lax.dot_general(chosen, gate_weight, contract, preferred_element_type=jnp.float32)
    up_part = lax.dot_general(chosen, up_weight, contract, preferred_element_type=jnp.float32)
    gate_part, up_part = (gate_part, up_part)
    gate_sum, up_sum = (
        lax.psum(gate_part.astype(jnp.bfloat16), "col").astype(jnp.float32),
        lax.psum(up_part.astype(jnp.bfloat16), "col").astype(jnp.float32),
    )
    hidden = (jax.nn.silu(gate_sum) * up_sum).astype(jnp.bfloat16)
    expert_out = lax.dot_general(
        hidden, down_weight, (((2,), (0,)), ((), ())), preferred_element_type=jnp.float32
    ).astype(jnp.bfloat16)
    hidden_wide = hidden.astype(jnp.float32)
    group_mask = (jnp.arange(held_count) == own_group)[None, :, None, None]
    placed = jnp.where(group_mask, expert_out[:, None], jnp.zeros((), jnp.bfloat16))
    returned = lax.all_to_all(placed, "dp", split_axis=0, concat_axis=0, tiled=True)
    slot_values = expert_major(returned.astype(jnp.float32), E, held_count, copies)
    dropped_part = jnp.dot(dropped_weights.T, slot_values, precision=top_precision)
    dropped = lax.psum(dropped_part, "tensor")
    ridge_weight = ridge_share * 2.0 * tok_rows * dp_count / E

    def apply_backward(image_tokens):
        slot_image = jnp.dot(kept_weights, image_tokens, precision=top_precision)
        outgoing_image = spread_copies(slot_image.reshape(E, CAP, -1), E, held_count, copies)
        arrived = lax.all_to_all(outgoing_image, "dp", split_axis=0, concat_axis=0, tiled=True)
        chosen = lax.dynamic_index_in_dim(arrived, own_group, 1, keepdims=False)
        return exact_product(hidden_wide, chosen, (((0, 1), (0, 1)), ((), ())))

    def total_norm(values):
        return lax.psum(jnp.sum(values * values), ("dp", "tensor", "col"))

    base_down = down_weight.astype(jnp.float32)
    residual = apply_backward(dropped) - ridge_weight * own_kept * base_down
    res_norm = total_norm(residual)
    direction = residual
    leftover = dropped
    for turn_index in range(ITERS):
        slot_part = exact_product(hidden_wide, direction, (((2,), (0,)), ((), ())))
        placed_part = jnp.where(group_mask, slot_part[:, None], 0.0)
        came_back = lax.all_to_all(placed_part, "dp", split_axis=0, concat_axis=0, tiled=True)
        image_part = jnp.dot(
            kept_weights.T, expert_major(came_back, E, held_count, copies), precision=top_precision
        )
        image_tokens = lax.psum(image_part, "tensor")
        first_copy = (lax.axis_index("tensor") == 0).astype(jnp.float32)
        local_term = first_copy * jnp.sum(image_tokens * image_tokens) + ridge_weight * jnp.sum(
            direction * direction
        )
        curvature = lax.psum(local_term, ("dp", "tensor", "col"))
        step_size = res_norm / curvature
        leftover = leftover - step_size * image_tokens
        if turn_index + 1 < ITERS:
            curved = apply_backward(image_tokens) + ridge_weight * direction
            residual = residual - step_size * curved
            next_norm = total_norm(residual)
            direction = residual + next_norm / res_norm * direction
            res_norm = next_norm
    return leftover


def shards(*arrays):
    sizes = [lax.axis_size(axis) for axis in ("dp", "tensor", "col")]
    if sizes[0] * sizes[1] == E and sizes[2] == 4 and ITERS == 2:
        return one_expert_each(*arrays)
    return general(*arrays)


def solution(mesh):
    placed = (
        P("dp", "col"),
        P("dp", None),
        P("dp", None),
        P(),
        P(("dp", "tensor"), "col"),
        P(("dp", "tensor"), "col"),
        P(("dp", "tensor"), "col"),
    )
    return jax.shard_map(
        shards, mesh=mesh, in_specs=placed, out_specs=P("dp", "col"), check_vma=False
    )
```

```python
import functools

import jax
import jax.numpy as jnp
from jax import lax
from jax.experimental import pallas as pl
from jax.experimental.pallas import tpu as pltpu
from jax.sharding import PartitionSpec as P

E = 8
ITERS = 2
CAP = 40
CHUNKS = 4


ridge_share = 0.25
top_precision = lax.Precision.HIGHEST
MIB = 1024 * 1024
LIGHT = pl.CostEstimate(flops=1, bytes_accessed=1, transcendentals=0)
f32 = jnp.float32
bf16 = jnp.bfloat16
NT = (((1,), (1,)), ((), ()))
NN = (((1,), (0,)), ((), ()))
TN = (((0,), (0,)), ((), ()))


def whole():
    return pl.BlockSpec(memory_space=pltpu.VMEM)


def scalars():
    return pl.BlockSpec(memory_space=pltpu.SMEM)


def mm(left, right, contract=NN):
    return lax.dot_general(left, right, contract, preferred_element_type=f32)


def split_wide(values):
    high = values.astype(bf16)
    low = (values - high.astype(f32)).astype(bf16)
    return jnp.concatenate([high, low], axis=1)


def mm_wide(left, right, contract=NN):
    lanes = right.shape[1]
    both = mm(left, split_wide(right), contract)
    return both[:, :lanes] + both[:, lanes:]


def params(mib):
    return pltpu.CompilerParams(vmem_limit_bytes=mib * MIB)


def block_slots(first, second):
    count = first.shape[1]
    expert_rows = lax.broadcasted_iota(jnp.int32, (E, count), 0).astype(f32)
    hot_first = (expert_rows == first).astype(f32)
    hot_second = (expert_rows == second).astype(f32)
    before = (
        lax.broadcasted_iota(jnp.int32, (count, count), 0)
        < lax.broadcasted_iota(jnp.int32, (count, count), 1)
    ).astype(bf16)
    place = mm((hot_first + hot_second).astype(bf16), before)
    ranked_first = jnp.sum(hot_first * place, axis=0, keepdims=True)
    ranked_second = jnp.sum(hot_second * place, axis=0, keepdims=True)
    return ranked_first, ranked_second


def pick_kernel(parts, tensor_count, place_ref, info_ref, tokens_ref, *out_refs):
    first, second = info_ref[0:1, :], info_ref[1:2, :]
    rank_first, rank_second = block_slots(first, second)
    count = first.shape[1]
    rows = lax.broadcasted_iota(jnp.int32, (CAP, count), 0).astype(f32)
    values = tokens_ref[...]
    logits = info_ref[2:4, :]
    high = logits.astype(bf16).astype(f32)
    middle = (logits - high).astype(bf16).astype(f32)
    extra = jnp.concatenate([info_ref[0:2, :], high, middle, logits - high - middle], axis=0)
    extra = jnp.concatenate([extra, jnp.zeros((8, values.shape[1] - count), f32)], axis=1)
    for shift, out_ref in enumerate(out_refs):
        expert = (lax.rem(place_ref[0] + shift, parts) * tensor_count + place_ref[1]).astype(f32)
        hit = ((first == expert) & (rank_first == rows)) | ((second == expert) & (rank_second == rows))
        rows_picked = mm(hit.astype(f32).astype(bf16), values)
        out_ref[...] = jnp.concatenate([rows_picked, extra], axis=0).astype(bf16)


def stack_kernel(*refs):
    pieces, (rows_ref, info_ref) = refs[:-2], refs[-2:]
    wide = [ref[...].astype(f32) for ref in pieces]
    rows_ref[...] = jnp.concatenate([value[:CAP] for value in wide], axis=0).astype(bf16)
    for index, value in enumerate(wide):
        extra = value[CAP : CAP + 8, : info_ref.shape[2]]
        info_ref[index, 0:2, :] = extra[0:2]
        info_ref[index, 2:4, :] = extra[2:4] + extra[4:6] + extra[6:8]


def gate_up_kernel(has_keep, order_ref, inputs_ref, gate_ref, up_ref, *rest):
    values = inputs_ref[...]
    gate = mm(values, gate_ref[...], NT).astype(bf16)
    up = mm(values, up_ref[...], NT).astype(bf16)
    step = pl.program_id(0)
    outs = rest[-(1 + (has_keep == 2)) :]
    for index, ref in enumerate(outs):

        @pl.when(step // 2 == index)
        def _(ref=ref):
            ref[0, 0] = gate
            ref[0, 1] = up


def gate_up(order, inputs, gate_weight, up_weight, width, keep, send, after):
    slots, depth = inputs.shape
    quarter = gate_weight.shape[0] // 4
    gate_weight = gate_weight.reshape(4, quarter, depth)
    up_weight = up_weight.reshape(4, quarter, depth)
    base = 0 if keep is not None else 2
    chunks = [chunk for chunk in (keep, send) if chunk is not None]
    count = len(chunks)

    def place(s, order):
        return (order[base + s], chunks[0] if count == 1 else jnp.where(s < 2, chunks[0], chunks[1]), 0)

    weight_spec = pl.BlockSpec((None, width, depth), place)
    out_specs = [
        pl.BlockSpec(
            (1, 2, slots, width),
            lambda s, order, index=index: (jnp.clip(s - 2 * index, 0, 1), 0, 0, 0),
        )
        for index in range(count)
    ]
    return pl.pallas_call(
        functools.partial(gate_up_kernel, count),
        grid_spec=pltpu.PrefetchScalarGridSpec(
            num_scalar_prefetch=1,
            grid=(2 * count,),
            in_specs=[
                pl.BlockSpec((slots, depth), lambda s, order: (0, 0)),
                weight_spec,
                weight_spec,
            ]
            + [pl.BlockSpec(memory_space=pl.ANY)] * len(after),
            out_specs=out_specs,
        ),
        out_shape=[jax.ShapeDtypeStruct((2, 2, slots, width), bf16)] * count,
        compiler_params=params(41),
        cost_estimate=pl.CostEstimate(
            flops=32 * count * slots * depth * width,
            bytes_accessed=32 * count * width * depth,
            transcendentals=0,
        ),
        name=f"gate_up_{chunks[-1] + (send is None)}",
    )(order, inputs, gate_weight, up_weight, *after)


def down_kernel(count, pack, has_old, order_ref, place_ref, *refs):
    pieces, down_ref, rest = refs[:count], refs[count], refs[count + 1 :]
    old, new = rest[:3] if has_old else (), rest[3 * has_old :]
    packed_refs = ()
    if pack:
        packed_refs, new = new[:-3], new[-3:]
    step = pl.program_id(0)

    @pl.when(step == 0)
    def _():
        for index, ref in enumerate(new):
            ref[...] = old[index][...] if old else jnp.zeros_like(ref)

    out_ref, gram_ref, square_ref = new
    weight = down_ref[...]
    wide = weight.astype(f32)
    square_ref[...] += jnp.sum((wide * wide).reshape(-1, 8, wide.shape[1]), axis=0)
    for index, ref in enumerate(pieces):

        @pl.when(step == index)
        def _(ref=ref, index=index):
            values = ref[...]
            out_ref[...] += mm(values, weight)
            gram_ref[...] += mm(values, values, NT)
            if pack and index == len(pieces) - 1:
                dp_count, tensor_count = pack
                columns = out_ref.shape[1]
                lanes = columns // (dp_count * tensor_count)
                group = columns // dp_count
                gram = gram_ref[...]
                rolled = pltpu.roll(out_ref[...], lax.rem(columns - place_ref[0] * group, columns), 1)
                for ahead in range(dp_count):
                    parts = [
                        rolled[:, ahead * group + part * lanes : ahead * group + (part + 1) * lanes]
                        for part in range(tensor_count)
                    ]
                    for aside in range(tensor_count):
                        target = lax.rem(place_ref[1] + aside, tensor_count)
                        piece = parts[0]
                        for part in range(1, tensor_count):
                            piece = jnp.where(target == part, parts[part], piece)
                        packed_refs[ahead * tensor_count + aside][...] = jnp.concatenate(
                            [gram, piece], axis=1
                        ).astype(bf16)


def down(order, place, pieces, down_weight, chunk, older, first=0, pack=None):
    slots, width = pieces[0].shape
    columns = down_weight.shape[1]
    down_weight = down_weight.reshape(4, -1, columns)

    def fixed(shape):
        return pl.BlockSpec(shape, lambda s, order, place: (0,) * len(shape))

    shapes = [(slots, columns), (slots, slots), (8, columns)]
    out_shape = [jax.ShapeDtypeStruct(shape, f32) for shape in shapes]
    if pack:
        parts = pack[0] * pack[1]
        packed = (slots, slots + columns // parts)
        out_shape = [jax.ShapeDtypeStruct(packed, bf16)] * parts + out_shape
    return pl.pallas_call(
        functools.partial(down_kernel, len(pieces), pack, bool(older)),
        grid_spec=pltpu.PrefetchScalarGridSpec(
            num_scalar_prefetch=2,
            grid=(len(pieces),),
            in_specs=[fixed((slots, width))] * len(pieces)
            + [pl.BlockSpec((None, width, columns), lambda s, order, place: (order[first + s], chunk, 0))]
            + [fixed(value.shape) for value in older],
            out_specs=[fixed(value.shape) for value in out_shape],
        ),
        out_shape=out_shape,
        compiler_params=params(20),
        cost_estimate=LIGHT,
        name=f"down_{chunk}_{first}",
    )(order, place, *pieces, down_weight, *older)


def route_kernel(blocks, tensor_count, kept_ref, place_ref, *refs):
    infos = [refs[0][block] for block in range(blocks)]
    hot_ref, turned_ref, gates_ref, wide_ref = refs[-4:]
    count = infos[0].shape[1]
    slots = blocks * CAP
    zero = jnp.zeros((CAP, count), f32)
    rows = lax.broadcasted_iota(jnp.int32, (CAP, count), 0).astype(f32)
    routed = []
    for block in range(blocks):
        first, second = infos[block][0:1, :], infos[block][1:2, :]
        delta = infos[block][3:4, :] - infos[block][2:3, :]
        share_first = 1.0 / (1.0 + jnp.exp(delta))
        share_second = 1.0 / (1.0 + jnp.exp(-delta))
        routed.append((first, second, share_first, share_second) + block_slots(first, second))
    for back in range(blocks):
        for aside in range(tensor_count):
            expert = lax.rem(place_ref[0] + blocks - back, blocks) * tensor_count
            expert = expert + lax.rem(place_ref[1] + tensor_count - aside, tensor_count)
            kept = jnp.zeros((), jnp.int32)
            for index in range(kept_ref.shape[0]):
                kept = kept | (kept_ref[index] == expert).astype(jnp.int32)
            kept, expert = kept.astype(f32), expert.astype(f32)
            for shift in range(blocks):
                block = (back + shift) % blocks
                first, second, share_first, share_second, rank_first, rank_second = routed[block]
                hit_first = (first == expert) & (rank_first == rows)
                hit_second = (second == expert) & (rank_second == rows)
                gate = jnp.sum(
                    jnp.where(hit_first, share_first, zero) + jnp.where(hit_second, share_second, zero),
                    axis=1,
                    keepdims=True,
                )
                row = (back * tensor_count + aside) * slots + shift * CAP
                for other in range(blocks):
                    wide_ref[row : row + CAP, other * count : (other + 1) * count] = (
                        (hit_first | hit_second).astype(f32) if other == block else zero
                    )
                gates_ref[row : row + CAP, 0:1] = gate * kept
                gates_ref[row : row + CAP, 1:2] = gate * (1.0 - kept)
    hot_ref[...] = wide_ref[...].astype(bf16)
    turned_ref[...] = wide_ref[...].T.astype(bf16)


def solve_kernel(ridge, slots, own_ref, hot_ref, turned_ref, gates_ref, square_ref, *refs):
    packed_refs, (base_ref, zero_ref, one_ref, sums_ref) = refs[:E], refs[E:]
    hot, turned = hot_ref[...], turned_ref[...]
    kept, dropped = gates_ref[:, 0:1], gates_ref[:, 1:2]
    values = jnp.concatenate([packed_refs[e][:, slots:].astype(f32) for e in range(E)], axis=0)
    base = mm_wide(turned, dropped * values)
    output = mm_wide(turned, kept * values)

    def apply(field):
        spread = kept * mm_wide(hot, field)
        mixed = jnp.concatenate(
            [
                mm_wide(packed_refs[e][:, :slots], spread[e * slots : (e + 1) * slots])
                for e in range(E)
            ],
            axis=0,
        )
        return mm_wide(turned, kept * mixed)

    curved = apply(base)
    zero = curved - ridge * output
    one = apply(zero)
    base_ref[...] = base
    zero_ref[...] = zero
    one_ref[...] = one
    norm = jnp.sum(base * (curved - 2.0 * ridge * output))
    square = jnp.sum(square_ref[...]) * own_ref[0]
    lane = lax.broadcasted_iota(jnp.int32, sums_ref.shape[1:], 1)
    sums = jnp.where(lane == 0, norm + ridge * ridge * square, 0.0)
    for index, value in enumerate((jnp.sum(zero * zero), jnp.sum(zero * one), jnp.sum(one * one))):
        sums = jnp.where(lane == index + 1, value, sums)
    for part in range(sums_ref.shape[0]):
        sums_ref[part] = sums


def finish_kernel(ridge, blocks, copies, place_ref, base_ref, zero_ref, one_ref, sums_ref, out_ref):
    sums = jnp.sum(sums_ref[...], axis=0)[0:1, :]
    norm, zero_zero = sums[:, 0:1], sums[:, 1:2]
    zero_one, one_one = sums[:, 2:3], sums[:, 3:4]
    step = norm / (zero_zero + ridge * norm)
    left = 1.0 - step * ridge
    new = left * left * norm - 2.0 * left * step * zero_zero + step * step * zero_one
    ratio = new / norm
    grown = left + ratio
    image = grown * grown * zero_zero - 2.0 * grown * step * zero_one + step * step * one_one
    later = new / (image + ridge * (new + ratio * ratio * norm))
    field = base_ref[...] - (step + later * grown) * zero_ref[...] + (later * step) * one_ref[...]
    rows = field.shape[0] // blocks
    sideways = field.T.astype(bf16)
    for back in range(blocks):
        target = lax.rem(place_ref[0] + blocks - back, blocks) * copies
        for copy in range(copies):
            out_ref[target + copy] = sideways[:, back * rows : (back + 1) * rows]


def join_kernel(pieces_ref, out_ref):
    rows = jnp.concatenate([pieces_ref[part].astype(f32) for part in range(pieces_ref.shape[0])], axis=0)
    out_ref[...] = rows.T


def single(kernel, out_shape, in_specs, mib, name, scratch=()):
    many = isinstance(out_shape, list)
    return pl.pallas_call(
        kernel,
        out_shape=out_shape,
        in_specs=in_specs,
        out_specs=[whole()] * len(out_shape) if many else whole(),
        scratch_shapes=list(scratch),
        compiler_params=params(mib),
        cost_estimate=LIGHT,
        name=name,
    )


def one_expert_each(tokens, routes, route_logits, kept_experts, gate_weight, up_weight, down_weight):
    dp_count = lax.axis_size("dp")
    tensor_count = lax.axis_size("tensor")
    parts = dp_count * tensor_count
    tok_rows, depth = tokens.shape
    units, columns = down_weight.shape
    slots = dp_count * CAP
    lanes = columns // parts
    width = units // 4 // CHUNKS
    ridge = ridge_share * 2.0 * tok_rows * dp_count / E
    dp_index = lax.axis_index("dp")
    tensor_index = lax.axis_index("tensor")
    col_index = lax.axis_index("col")
    own_expert = dp_index * tensor_count + tensor_index
    place = jnp.stack([dp_index, tensor_index])

    def beside(values):
        return lax.ppermute(values, "col", [(k, k ^ 1) for k in range(4)])

    def across(values):
        return lax.ppermute(values, "col", [(k, k ^ 2) for k in range(4)])

    def shifted(values, ahead, aside=0):
        if ahead == 0 and aside == 0:
            return values
        pairs = [
            (i * tensor_count + j, (i + ahead) % dp_count * tensor_count + (j + aside) % tensor_count)
            for i in range(dp_count)
            for j in range(tensor_count)
        ]
        return lax.ppermute(values, ("dp", "tensor"), pairs)

    shifts = [(ahead, aside) for ahead in range(dp_count) for aside in range(tensor_count)]
    upper = lax.pad(routes.T, jnp.int32(0), ((0, 2, 0), (0, 0, 0))).astype(f32)
    info = upper + lax.pad(route_logits.T, f32(0), ((2, 0, 0), (0, 0, 0)))
    picked = single(
        functools.partial(pick_kernel, dp_count, tensor_count),
        [jax.ShapeDtypeStruct((CAP + 8, depth), bf16)] * dp_count,
        [scalars(), whole(), whole()],
        16,
        "pick",
    )(place, info, tokens)
    arrived = [shifted(value, ahead) for ahead, value in enumerate(picked)]
    inputs, infos = single(
        stack_kernel,
        [jax.ShapeDtypeStruct((slots, depth), bf16), jax.ShapeDtypeStruct((dp_count, 4, tok_rows), f32)],
        [whole()] * dp_count,
        16,
        "stack",
    )(*arrived)

    gate_order = col_index ^ jnp.array([2, 0, 3, 1], jnp.int32)
    down_order = col_index ^ jnp.array([0, 2, 1, 3], jnp.int32)

    def products(keep, send, after=()):
        return gate_up(gate_order, inputs, gate_weight, up_weight, width, keep, send, after)

    last = CHUNKS - 1
    keeps, nears, pairs, fars, owns = [], [], [], [], []

    def activate(chunk, after):
        far = lax.optimization_barrier((fars[chunk], *after))[0] if after else fars[chunk]
        total = keeps[chunk][1].astype(f32) + nears[chunk][1].astype(f32) + far.astype(f32)
        owns.append((jax.nn.silu(total[0]) * total[1]).astype(bf16))

    nears.append(beside(products(None, 0)[0]))
    for chunk in range(CHUNKS):
        after = [keeps[-1]] if chunk else []
        if chunk >= 2:
            after.extend([fars[chunk - 2], pairs[chunk - 1]])
        if chunk < last:
            keep, send = products(chunk, chunk + 1, after)
            nears.append(beside(send))
        else:
            (keep,) = products(chunk, None, after)
        keeps.append(keep)
        pairs.append((keep[0].astype(f32) + nears[chunk][0].astype(f32)).astype(bf16))
        fars.append(across(pairs[-1]))
    older, olders = (), []
    for chunk in range(CHUNKS):
        if chunk >= len(owns):
            after = [pairs[last]]
            if chunk >= 2:
                after.append(olders[chunk - 2][2])
            activate(chunk, after)
        own = owns[chunk]
        other = across(own)
        pieces = (own, other, beside(own), beside(other))
        if chunk < last:
            older = down(down_order, place, pieces, down_weight, chunk, older)
        else:
            older = down(down_order, place, pieces[:3], down_weight, chunk, older)
            older = down(
                down_order, place, pieces[3:], down_weight, chunk, older, 3, (dp_count, tensor_count)
            )
        olders.append(older)
    packed, (_, _, square) = older[:parts], older[parts:]
    spread = [shifted(value, *shift) for value, shift in zip(packed, shifts)]

    total_slots, total_tokens = E * slots, dp_count * tok_rows
    hot, turned_hot, gates = single(
        functools.partial(route_kernel, dp_count, tensor_count),
        [
            jax.ShapeDtypeStruct((total_slots, total_tokens), bf16),
            jax.ShapeDtypeStruct((total_tokens, total_slots), bf16),
            jax.ShapeDtypeStruct((total_slots, 2), f32),
        ],
        [scalars(), scalars(), whole(), pl.BlockSpec(memory_space=pl.ANY)],
        24,
        "route",
        [pltpu.VMEM((total_slots, total_tokens), f32)],
    )(kept_experts, place, infos, square)
    is_kept = jnp.any(kept_experts == own_expert).astype(f32).reshape(1)
    field = jax.ShapeDtypeStruct((total_tokens, lanes), f32)
    everyone = parts * lax.axis_size("col")
    base, zero, one, sums = single(
        functools.partial(solve_kernel, ridge, slots),
        [field, field, field, jax.ShapeDtypeStruct((everyone, 1, 128), f32)],
        [scalars()] + [whole()] * (4 + E),
        40,
        "solve",
    )(is_kept, hot, turned_hot, gates, square, *spread)
    sums = lax.all_to_all(sums, ("dp", "tensor", "col"), split_axis=0, concat_axis=0, tiled=True)

    home = single(
        functools.partial(finish_kernel, ridge, dp_count, tensor_count),
        jax.ShapeDtypeStruct((parts, lanes, tok_rows), bf16),
        [scalars()] + [whole()] * 4,
        16,
        "finish",
    )(place, base, zero, one, sums)
    home = lax.all_to_all(home, ("dp", "tensor"), split_axis=0, concat_axis=0, tiled=True)
    return single(
        join_kernel,
        jax.ShapeDtypeStruct((tok_rows, columns), f32),
        [whole()],
        16,
        "join",
    )(home)


def spread_copies(values, experts, held_count, copies):
    old_shape = values.shape
    grouped = values.reshape((experts // held_count, 1, held_count) + old_shape[1:])
    widened = jnp.broadcast_to(grouped, (experts // held_count, copies, held_count) + old_shape[1:])
    return widened.reshape((experts // held_count * copies, held_count) + old_shape[1:])


def expert_major(returned, experts, held_count, copies):
    old_shape = returned.shape
    grouped = returned.reshape((experts // held_count, copies, held_count) + old_shape[2:])
    merged = jnp.sum(grouped, axis=1)
    return merged.reshape((experts * old_shape[2],) + old_shape[3:])


def exact_product(left, right, contract):
    return lax.dot_general(
        left, right, contract, precision=top_precision, preferred_element_type=jnp.float32
    )


def general(tokens, routes, route_logits, kept_experts, gate_weight, up_weight, down_weight):
    dp_count = lax.axis_size("dp")
    tensor_count = lax.axis_size("tensor")
    held_count = max(1, E // dp_count)
    copies = max(1, dp_count // E)
    tok_rows = tokens.shape[0]
    piece_rows = gate_weight.shape[0]
    FF = piece_rows * dp_count * tensor_count // E
    slot_total = E * CAP
    device_rank = lax.axis_index("dp") * tensor_count + lax.axis_index("tensor")
    own_expert = device_rank * piece_rows // FF
    own_group = own_expert % held_count
    expert_ids = jnp.arange(E, dtype=jnp.int32)
    kept_table = jnp.any(kept_experts[:, None] == expert_ids[None, :], axis=0).astype(jnp.float32)
    own_kept = jnp.sum(jnp.where(expert_ids == own_expert, kept_table, 0.0))
    route_experts = routes.reshape(-1)
    route_onehot = (route_experts[:, None] == expert_ids[None, :]).astype(jnp.int32)
    route_rank = jnp.sum((jnp.cumsum(route_onehot, axis=0) - route_onehot) * route_onehot, axis=1)
    route_slot = route_experts * CAP + route_rank
    gate_probs = jax.nn.softmax(route_logits, axis=-1).reshape(-1)
    route_kept = jnp.sum(route_onehot.astype(jnp.float32) * kept_table[None, :], axis=1)
    slot_match = (jnp.arange(slot_total, dtype=jnp.int32)[:, None] == route_slot[None, :]).astype(
        jnp.float32
    )
    pick_tokens = slot_match.reshape(slot_total, tok_rows, 2).sum(axis=2)
    kept_weights = (
        (slot_match * (gate_probs * route_kept)[None, :])
        .reshape(slot_total, tok_rows, 2)
        .sum(axis=2)
    )
    dropped_weights = (
        (slot_match * (gate_probs * (1.0 - route_kept))[None, :])
        .reshape(slot_total, tok_rows, 2)
        .sum(axis=2)
    )
    by_expert = jnp.dot(
        pick_tokens.astype(jnp.bfloat16), tokens, preferred_element_type=jnp.float32
    ).astype(jnp.bfloat16)
    outgoing = spread_copies(by_expert.reshape(E, CAP, -1), E, held_count, copies)
    chosen = lax.dynamic_index_in_dim(
        lax.all_to_all(outgoing, "dp", split_axis=0, concat_axis=0, tiled=True),
        own_group,
        1,
        keepdims=False,
    )
    contract = (((2,), (1,)), ((), ()))
    gate_part = lax.dot_general(chosen, gate_weight, contract, preferred_element_type=jnp.float32)
    up_part = lax.dot_general(chosen, up_weight, contract, preferred_element_type=jnp.float32)
    gate_part, up_part = (gate_part, up_part)
    gate_sum, up_sum = (
        lax.psum(gate_part.astype(jnp.bfloat16), "col").astype(jnp.float32),
        lax.psum(up_part.astype(jnp.bfloat16), "col").astype(jnp.float32),
    )
    hidden = (jax.nn.silu(gate_sum) * up_sum).astype(jnp.bfloat16)
    expert_out = lax.dot_general(
        hidden, down_weight, (((2,), (0,)), ((), ())), preferred_element_type=jnp.float32
    ).astype(jnp.bfloat16)
    hidden_wide = hidden.astype(jnp.float32)
    group_mask = (jnp.arange(held_count) == own_group)[None, :, None, None]
    placed = jnp.where(group_mask, expert_out[:, None], jnp.zeros((), jnp.bfloat16))
    returned = lax.all_to_all(placed, "dp", split_axis=0, concat_axis=0, tiled=True)
    slot_values = expert_major(returned.astype(jnp.float32), E, held_count, copies)
    dropped_part = jnp.dot(dropped_weights.T, slot_values, precision=top_precision)
    dropped = lax.psum(dropped_part, "tensor")
    ridge_weight = ridge_share * 2.0 * tok_rows * dp_count / E

    def apply_backward(image_tokens):
        slot_image = jnp.dot(kept_weights, image_tokens, precision=top_precision)
        outgoing_image = spread_copies(slot_image.reshape(E, CAP, -1), E, held_count, copies)
        arrived = lax.all_to_all(outgoing_image, "dp", split_axis=0, concat_axis=0, tiled=True)
        chosen = lax.dynamic_index_in_dim(arrived, own_group, 1, keepdims=False)
        return exact_product(hidden_wide, chosen, (((0, 1), (0, 1)), ((), ())))

    def total_norm(values):
        return lax.psum(jnp.sum(values * values), ("dp", "tensor", "col"))

    base_down = down_weight.astype(jnp.float32)
    residual = apply_backward(dropped) - ridge_weight * own_kept * base_down
    res_norm = total_norm(residual)
    direction = residual
    leftover = dropped
    for turn_index in range(ITERS):
        slot_part = exact_product(hidden_wide, direction, (((2,), (0,)), ((), ())))
        placed_part = jnp.where(group_mask, slot_part[:, None], 0.0)
        came_back = lax.all_to_all(placed_part, "dp", split_axis=0, concat_axis=0, tiled=True)
        image_part = jnp.dot(
            kept_weights.T, expert_major(came_back, E, held_count, copies), precision=top_precision
        )
        image_tokens = lax.psum(image_part, "tensor")
        first_copy = (lax.axis_index("tensor") == 0).astype(jnp.float32)
        local_term = first_copy * jnp.sum(image_tokens * image_tokens) + ridge_weight * jnp.sum(
            direction * direction
        )
        curvature = lax.psum(local_term, ("dp", "tensor", "col"))
        step_size = res_norm / curvature
        leftover = leftover - step_size * image_tokens
        if turn_index + 1 < ITERS:
            curved = apply_backward(image_tokens) + ridge_weight * direction
            residual = residual - step_size * curved
            next_norm = total_norm(residual)
            direction = residual + next_norm / res_norm * direction
            res_norm = next_norm
    return leftover


def shards(*arrays):
    sizes = [lax.axis_size(axis) for axis in ("dp", "tensor", "col")]
    if sizes[0] * sizes[1] == E and sizes[2] == 4 and ITERS == 2:
        return one_expert_each(*arrays)
    return general(*arrays)


def solution(mesh):
    placed = (
        P("dp", "col"),
        P("dp", None),
        P("dp", None),
        P(),
        P(("dp", "tensor"), "col"),
        P(("dp", "tensor"), "col"),
        P(("dp", "tensor"), "col"),
    )
    return jax.shard_map(
        shards, mesh=mesh, in_specs=placed, out_specs=P("dp", "col"), check_vma=False
    )
```

```python
import functools

import jax
import jax.numpy as jnp
from jax import lax
from jax.experimental import pallas as pl
from jax.experimental.pallas import tpu as pltpu
from jax.sharding import PartitionSpec as P

E = 8
ITERS = 2
CAP = 40
CHUNKS = 4


ridge_share = 0.25
top_precision = lax.Precision.HIGHEST
MIB = 1024 * 1024
LIGHT = pl.CostEstimate(flops=1, bytes_accessed=1, transcendentals=0)
f32 = jnp.float32
bf16 = jnp.bfloat16
NT = (((1,), (1,)), ((), ()))
NN = (((1,), (0,)), ((), ()))
TN = (((0,), (0,)), ((), ()))


def whole():
    return pl.BlockSpec(memory_space=pltpu.VMEM)


def scalars():
    return pl.BlockSpec(memory_space=pltpu.SMEM)


def mm(left, right, contract=NN):
    return lax.dot_general(left, right, contract, preferred_element_type=f32)


def split_wide(values):
    high = values.astype(bf16)
    low = (values - high.astype(f32)).astype(bf16)
    return jnp.concatenate([high, low], axis=1)


def mm_wide(left, right, contract=NN):
    lanes = right.shape[1]
    both = mm(left, split_wide(right), contract)
    return both[:, :lanes] + both[:, lanes:]


def params(mib):
    return pltpu.CompilerParams(vmem_limit_bytes=mib * MIB)


def block_slots(first, second):
    count = first.shape[1]
    expert_rows = lax.broadcasted_iota(jnp.int32, (E, count), 0).astype(f32)
    hot_first = (expert_rows == first).astype(f32)
    hot_second = (expert_rows == second).astype(f32)
    before = (
        lax.broadcasted_iota(jnp.int32, (count, count), 0)
        < lax.broadcasted_iota(jnp.int32, (count, count), 1)
    ).astype(bf16)
    place = mm((hot_first + hot_second).astype(bf16), before)
    ranked_first = jnp.sum(hot_first * place, axis=0, keepdims=True)
    ranked_second = jnp.sum(hot_second * place, axis=0, keepdims=True)
    return ranked_first, ranked_second


def pick_kernel(parts, tensor_count, place_ref, info_ref, tokens_ref, *out_refs):
    first, second = info_ref[0:1, :], info_ref[1:2, :]
    rank_first, rank_second = block_slots(first, second)
    count = first.shape[1]
    rows = lax.broadcasted_iota(jnp.int32, (CAP, count), 0).astype(f32)
    values = tokens_ref[...]
    logits = info_ref[2:4, :]
    high = logits.astype(bf16).astype(f32)
    middle = (logits - high).astype(bf16).astype(f32)
    extra = jnp.concatenate([info_ref[0:2, :], high, middle, logits - high - middle], axis=0)
    extra = jnp.concatenate([extra, jnp.zeros((8, values.shape[1] - count), f32)], axis=1)
    for shift, out_ref in enumerate(out_refs):
        expert = (lax.rem(place_ref[0] + shift, parts) * tensor_count + place_ref[1]).astype(f32)
        hit = ((first == expert) & (rank_first == rows)) | ((second == expert) & (rank_second == rows))
        rows_picked = mm(hit.astype(f32).astype(bf16), values)
        out_ref[...] = jnp.concatenate([rows_picked, extra], axis=0).astype(bf16)


def stack_kernel(*refs):
    pieces, (rows_ref, info_ref) = refs[:-2], refs[-2:]
    wide = [ref[...].astype(f32) for ref in pieces]
    rows_ref[...] = jnp.concatenate([value[:CAP] for value in wide], axis=0).astype(bf16)
    for index, value in enumerate(wide):
        extra = value[CAP : CAP + 8, : info_ref.shape[2]]
        info_ref[index, 0:2, :] = extra[0:2]
        info_ref[index, 2:4, :] = extra[2:4] + extra[4:6] + extra[6:8]


def gate_up_kernel(has_keep, order_ref, inputs_ref, gate_ref, up_ref, *rest):
    values = inputs_ref[...]
    gate = mm(values, gate_ref[...], NT).astype(bf16)
    up = mm(values, up_ref[...], NT).astype(bf16)
    step = pl.program_id(0)
    outs = rest[-(1 + (has_keep == 2)) :]
    for index, ref in enumerate(outs):

        @pl.when(step // 2 == index)
        def _(ref=ref):
            ref[0, 0] = gate
            ref[0, 1] = up


def gate_up(order, inputs, gate_weight, up_weight, width, keep, send, after):
    slots, depth = inputs.shape
    quarter = gate_weight.shape[0] // 4
    gate_weight = gate_weight.reshape(4, quarter, depth)
    up_weight = up_weight.reshape(4, quarter, depth)
    base = 0 if keep is not None else 2
    chunks = [chunk for chunk in (keep, send) if chunk is not None]
    count = len(chunks)

    def place(s, order):
        return (order[base + s], chunks[0] if count == 1 else jnp.where(s < 2, chunks[0], chunks[1]), 0)

    weight_spec = pl.BlockSpec((None, width, depth), place)
    out_specs = [
        pl.BlockSpec(
            (1, 2, slots, width),
            lambda s, order, index=index: (jnp.clip(s - 2 * index, 0, 1), 0, 0, 0),
        )
        for index in range(count)
    ]
    return pl.pallas_call(
        functools.partial(gate_up_kernel, count),
        grid_spec=pltpu.PrefetchScalarGridSpec(
            num_scalar_prefetch=1,
            grid=(2 * count,),
            in_specs=[
                pl.BlockSpec((slots, depth), lambda s, order: (0, 0)),
                weight_spec,
                weight_spec,
            ]
            + [pl.BlockSpec(memory_space=pl.ANY)] * len(after),
            out_specs=out_specs,
        ),
        out_shape=[jax.ShapeDtypeStruct((2, 2, slots, width), bf16)] * count,
        compiler_params=params(41),
        cost_estimate=pl.CostEstimate(
            flops=32 * count * slots * depth * width,
            bytes_accessed=32 * count * width * depth,
            transcendentals=0,
        ),
        name=f"gate_up_{chunks[-1] + (send is None)}",
    )(order, inputs, gate_weight, up_weight, *after)


def down_kernel(count, pack, has_old, order_ref, place_ref, *refs):
    pieces, down_ref, rest = refs[:count], refs[count], refs[count + 1 :]
    old, new = rest[:3] if has_old else (), rest[3 * has_old :]
    packed_refs = ()
    if pack:
        packed_refs, new = new[:-3], new[-3:]
    step = pl.program_id(0)

    @pl.when(step == 0)
    def _():
        for index, ref in enumerate(new):
            ref[...] = old[index][...] if old else jnp.zeros_like(ref)

    out_ref, gram_ref, square_ref = new
    weight = down_ref[...]
    wide = weight.astype(f32)
    square_ref[...] += jnp.sum((wide * wide).reshape(-1, 8, wide.shape[1]), axis=0)
    for index, ref in enumerate(pieces):

        @pl.when(step == index)
        def _(ref=ref, index=index):
            values = ref[...]
            out_ref[...] += mm(values, weight)
            gram_ref[...] += mm(values, values, NT)
            if pack and index == len(pieces) - 1:
                dp_count, tensor_count = pack
                columns = out_ref.shape[1]
                lanes = columns // (dp_count * tensor_count)
                group = columns // dp_count
                gram = gram_ref[...]
                rolled = pltpu.roll(out_ref[...], lax.rem(columns - place_ref[0] * group, columns), 1)
                for ahead in range(dp_count):
                    parts = [
                        rolled[:, ahead * group + part * lanes : ahead * group + (part + 1) * lanes]
                        for part in range(tensor_count)
                    ]
                    for aside in range(tensor_count):
                        target = lax.rem(place_ref[1] + aside, tensor_count)
                        piece = parts[0]
                        for part in range(1, tensor_count):
                            piece = jnp.where(target == part, parts[part], piece)
                        packed_refs[ahead * tensor_count + aside][...] = jnp.concatenate(
                            [gram, piece], axis=1
                        ).astype(bf16)


def down(order, place, pieces, down_weight, chunk, older, first=0, pack=None):
    slots, width = pieces[0].shape
    columns = down_weight.shape[1]
    down_weight = down_weight.reshape(4, -1, columns)

    def fixed(shape):
        return pl.BlockSpec(shape, lambda s, order, place: (0,) * len(shape))

    shapes = [(slots, columns), (slots, slots), (8, columns)]
    out_shape = [jax.ShapeDtypeStruct(shape, f32) for shape in shapes]
    if pack:
        parts = pack[0] * pack[1]
        packed = (slots, slots + columns // parts)
        out_shape = [jax.ShapeDtypeStruct(packed, bf16)] * parts + out_shape
    return pl.pallas_call(
        functools.partial(down_kernel, len(pieces), pack, bool(older)),
        grid_spec=pltpu.PrefetchScalarGridSpec(
            num_scalar_prefetch=2,
            grid=(len(pieces),),
            in_specs=[fixed((slots, width))] * len(pieces)
            + [pl.BlockSpec((None, width, columns), lambda s, order, place: (order[first + s], chunk, 0))]
            + [fixed(value.shape) for value in older],
            out_specs=[fixed(value.shape) for value in out_shape],
        ),
        out_shape=out_shape,
        compiler_params=params(20),
        cost_estimate=LIGHT,
        name=f"down_{chunk}_{first}",
    )(order, place, *pieces, down_weight, *older)


def route_kernel(blocks, tensor_count, kept_ref, place_ref, *refs):
    infos = [refs[0][block] for block in range(blocks)]
    hot_ref, turned_ref, gates_ref, wide_ref = refs[-4:]
    count = infos[0].shape[1]
    slots = blocks * CAP
    zero = jnp.zeros((CAP, count), f32)
    rows = lax.broadcasted_iota(jnp.int32, (CAP, count), 0).astype(f32)
    routed = []
    for block in range(blocks):
        first, second = infos[block][0:1, :], infos[block][1:2, :]
        delta = infos[block][3:4, :] - infos[block][2:3, :]
        share_first = 1.0 / (1.0 + jnp.exp(delta))
        share_second = 1.0 / (1.0 + jnp.exp(-delta))
        routed.append((first, second, share_first, share_second) + block_slots(first, second))
    for back in range(blocks):
        for aside in range(tensor_count):
            expert = lax.rem(place_ref[0] + blocks - back, blocks) * tensor_count
            expert = expert + lax.rem(place_ref[1] + tensor_count - aside, tensor_count)
            kept = jnp.zeros((), jnp.int32)
            for index in range(kept_ref.shape[0]):
                kept = kept | (kept_ref[index] == expert).astype(jnp.int32)
            kept, expert = kept.astype(f32), expert.astype(f32)
            for shift in range(blocks):
                block = (back + shift) % blocks
                first, second, share_first, share_second, rank_first, rank_second = routed[block]
                hit_first = (first == expert) & (rank_first == rows)
                hit_second = (second == expert) & (rank_second == rows)
                gate = jnp.sum(
                    jnp.where(hit_first, share_first, zero) + jnp.where(hit_second, share_second, zero),
                    axis=1,
                    keepdims=True,
                )
                row = (back * tensor_count + aside) * slots + shift * CAP
                for other in range(blocks):
                    wide_ref[row : row + CAP, other * count : (other + 1) * count] = (
                        (hit_first | hit_second).astype(f32) if other == block else zero
                    )
                gates_ref[row : row + CAP, 0:1] = gate * kept
                gates_ref[row : row + CAP, 1:2] = gate * (1.0 - kept)
    hot_ref[...] = wide_ref[...].astype(bf16)
    turned_ref[...] = wide_ref[...].T.astype(bf16)


def solve_kernel(ridge, slots, own_ref, hot_ref, turned_ref, gates_ref, square_ref, *refs):
    packed_refs, (base_ref, zero_ref, one_ref, sums_ref) = refs[:E], refs[E:]
    hot, turned = hot_ref[...], turned_ref[...]
    kept, dropped = gates_ref[:, 0:1], gates_ref[:, 1:2]
    values = jnp.concatenate([packed_refs[e][:, slots:].astype(f32) for e in range(E)], axis=0)
    base = mm_wide(turned, dropped * values)
    output = mm_wide(turned, kept * values)

    def apply(field):
        spread = kept * mm_wide(hot, field)
        mixed = jnp.concatenate(
            [
                mm_wide(packed_refs[e][:, :slots], spread[e * slots : (e + 1) * slots])
                for e in range(E)
            ],
            axis=0,
        )
        return mm_wide(turned, kept * mixed)

    curved = apply(base)
    zero = curved - ridge * output
    one = apply(zero)
    base_ref[...] = base
    zero_ref[...] = zero
    one_ref[...] = one
    norm = jnp.sum(base * (curved - 2.0 * ridge * output))
    square = jnp.sum(square_ref[...]) * own_ref[0]
    lane = lax.broadcasted_iota(jnp.int32, sums_ref.shape[1:], 1)
    sums = jnp.where(lane == 0, norm + ridge * ridge * square, 0.0)
    for index, value in enumerate((jnp.sum(zero * zero), jnp.sum(zero * one), jnp.sum(one * one))):
        sums = jnp.where(lane == index + 1, value, sums)
    for part in range(sums_ref.shape[0]):
        sums_ref[part] = sums


def finish_kernel(ridge, blocks, copies, place_ref, base_ref, zero_ref, one_ref, sums_ref, out_ref):
    sums = jnp.sum(sums_ref[...], axis=0)[0:1, :]
    norm, zero_zero = sums[:, 0:1], sums[:, 1:2]
    zero_one, one_one = sums[:, 2:3], sums[:, 3:4]
    step = norm / (zero_zero + ridge * norm)
    left = 1.0 - step * ridge
    new = left * left * norm - 2.0 * left * step * zero_zero + step * step * zero_one
    ratio = new / norm
    grown = left + ratio
    image = grown * grown * zero_zero - 2.0 * grown * step * zero_one + step * step * one_one
    later = new / (image + ridge * (new + ratio * ratio * norm))
    field = base_ref[...] - (step + later * grown) * zero_ref[...] + (later * step) * one_ref[...]
    rows = field.shape[0] // blocks
    sideways = field.T.astype(bf16)
    for back in range(blocks):
        target = lax.rem(place_ref[0] + blocks - back, blocks) * copies
        for copy in range(copies):
            out_ref[target + copy] = sideways[:, back * rows : (back + 1) * rows]


def join_kernel(pieces_ref, out_ref):
    rows = jnp.concatenate([pieces_ref[part].astype(f32) for part in range(pieces_ref.shape[0])], axis=0)
    out_ref[...] = rows.T


def single(kernel, out_shape, in_specs, mib, name, scratch=()):
    many = isinstance(out_shape, list)
    return pl.pallas_call(
        kernel,
        out_shape=out_shape,
        in_specs=in_specs,
        out_specs=[whole()] * len(out_shape) if many else whole(),
        scratch_shapes=list(scratch),
        compiler_params=params(mib),
        cost_estimate=LIGHT,
        name=name,
    )


def one_expert_each(tokens, routes, route_logits, kept_experts, gate_weight, up_weight, down_weight):
    dp_count = lax.axis_size("dp")
    tensor_count = lax.axis_size("tensor")
    parts = dp_count * tensor_count
    tok_rows, depth = tokens.shape
    units, columns = down_weight.shape
    slots = dp_count * CAP
    lanes = columns // parts
    width = units // 4 // CHUNKS
    ridge = ridge_share * 2.0 * tok_rows * dp_count / E
    dp_index = lax.axis_index("dp")
    tensor_index = lax.axis_index("tensor")
    col_index = lax.axis_index("col")
    own_expert = dp_index * tensor_count + tensor_index
    place = jnp.stack([dp_index, tensor_index])

    def beside(values):
        return lax.ppermute(values, "col", [(k, k ^ 1) for k in range(4)])

    def across(values):
        return lax.ppermute(values, "col", [(k, k ^ 2) for k in range(4)])

    def shifted(values, ahead, aside=0):
        if ahead == 0 and aside == 0:
            return values
        pairs = [
            (i * tensor_count + j, (i + ahead) % dp_count * tensor_count + (j + aside) % tensor_count)
            for i in range(dp_count)
            for j in range(tensor_count)
        ]
        return lax.ppermute(values, ("dp", "tensor"), pairs)

    shifts = [(ahead, aside) for ahead in range(dp_count) for aside in range(tensor_count)]
    upper = lax.pad(routes.T, jnp.int32(0), ((0, 2, 0), (0, 0, 0))).astype(f32)
    info = upper + lax.pad(route_logits.T, f32(0), ((2, 0, 0), (0, 0, 0)))
    picked = single(
        functools.partial(pick_kernel, dp_count, tensor_count),
        [jax.ShapeDtypeStruct((CAP + 8, depth), bf16)] * dp_count,
        [scalars(), whole(), whole()],
        16,
        "pick",
    )(place, info, tokens)
    arrived = [shifted(value, ahead) for ahead, value in enumerate(picked)]
    inputs, infos = single(
        stack_kernel,
        [jax.ShapeDtypeStruct((slots, depth), bf16), jax.ShapeDtypeStruct((dp_count, 4, tok_rows), f32)],
        [whole()] * dp_count,
        16,
        "stack",
    )(*arrived)

    gate_order = col_index ^ jnp.array([2, 0, 3, 1], jnp.int32)
    down_order = col_index ^ jnp.array([0, 2, 1, 3], jnp.int32)

    def products(keep, send, after=()):
        return gate_up(gate_order, inputs, gate_weight, up_weight, width, keep, send, after)

    last = CHUNKS - 1
    keeps, nears, pairs, fars, owns = [], [], [], [], []

    def activate(chunk, after):
        far = lax.optimization_barrier((fars[chunk], *after))[0] if after else fars[chunk]
        total = keeps[chunk][1].astype(f32) + nears[chunk][1].astype(f32) + far.astype(f32)
        owns.append((jax.nn.silu(total[0]) * total[1]).astype(bf16))

    nears.append(beside(products(None, 0)[0]))
    for chunk in range(CHUNKS):
        after = [keeps[-1]] if chunk else []
        if chunk >= 2:
            activate(chunk - 2, [pairs[chunk - 1]])
            after.extend([pairs[chunk - 1], owns[chunk - 2]])
        if chunk < last:
            keep, send = products(chunk, chunk + 1, after)
            nears.append(beside(send))
        else:
            (keep,) = products(chunk, None, after)
        keeps.append(keep)
        pairs.append((keep[0].astype(f32) + nears[chunk][0].astype(f32)).astype(bf16))
        fars.append(across(pairs[-1]))
    older, olders = (), []
    for chunk in range(CHUNKS):
        if chunk >= len(owns):
            after = [pairs[last]]
            if chunk >= 2:
                after.append(olders[chunk - 2][2])
            activate(chunk, after)
        own = owns[chunk]
        other = across(own)
        if chunk + 2 <= last:
            own, other = lax.optimization_barrier((own, other, pairs[last]))[:2]
        pieces = (own, other, beside(own), beside(other))
        if chunk < last:
            older = down(down_order, place, pieces, down_weight, chunk, older)
        else:
            older = down(down_order, place, pieces[:3], down_weight, chunk, older)
            older = down(
                down_order, place, pieces[3:], down_weight, chunk, older, 3, (dp_count, tensor_count)
            )
        olders.append(older)
    packed, (_, _, square) = older[:parts], older[parts:]
    spread = [shifted(value, *shift) for value, shift in zip(packed, shifts)]

    total_slots, total_tokens = E * slots, dp_count * tok_rows
    hot, turned_hot, gates = single(
        functools.partial(route_kernel, dp_count, tensor_count),
        [
            jax.ShapeDtypeStruct((total_slots, total_tokens), bf16),
            jax.ShapeDtypeStruct((total_tokens, total_slots), bf16),
            jax.ShapeDtypeStruct((total_slots, 2), f32),
        ],
        [scalars(), scalars(), whole(), pl.BlockSpec(memory_space=pl.ANY)],
        24,
        "route",
        [pltpu.VMEM((total_slots, total_tokens), f32)],
    )(kept_experts, place, infos, square)
    is_kept = jnp.any(kept_experts == own_expert).astype(f32).reshape(1)
    field = jax.ShapeDtypeStruct((total_tokens, lanes), f32)
    everyone = parts * lax.axis_size("col")
    base, zero, one, sums = single(
        functools.partial(solve_kernel, ridge, slots),
        [field, field, field, jax.ShapeDtypeStruct((everyone, 1, 128), f32)],
        [scalars()] + [whole()] * (4 + E),
        40,
        "solve",
    )(is_kept, hot, turned_hot, gates, square, *spread)
    sums = lax.all_to_all(sums, ("dp", "tensor", "col"), split_axis=0, concat_axis=0, tiled=True)

    home = single(
        functools.partial(finish_kernel, ridge, dp_count, tensor_count),
        jax.ShapeDtypeStruct((parts, lanes, tok_rows), bf16),
        [scalars()] + [whole()] * 4,
        16,
        "finish",
    )(place, base, zero, one, sums)
    home = lax.all_to_all(home, ("dp", "tensor"), split_axis=0, concat_axis=0, tiled=True)
    return single(
        join_kernel,
        jax.ShapeDtypeStruct((tok_rows, columns), f32),
        [whole()],
        16,
        "join",
    )(home)


def spread_copies(values, experts, held_count, copies):
    old_shape = values.shape
    grouped = values.reshape((experts // held_count, 1, held_count) + old_shape[1:])
    widened = jnp.broadcast_to(grouped, (experts // held_count, copies, held_count) + old_shape[1:])
    return widened.reshape((experts // held_count * copies, held_count) + old_shape[1:])


def expert_major(returned, experts, held_count, copies):
    old_shape = returned.shape
    grouped = returned.reshape((experts // held_count, copies, held_count) + old_shape[2:])
    merged = jnp.sum(grouped, axis=1)
    return merged.reshape((experts * old_shape[2],) + old_shape[3:])


def exact_product(left, right, contract):
    return lax.dot_general(
        left, right, contract, precision=top_precision, preferred_element_type=jnp.float32
    )


def general(tokens, routes, route_logits, kept_experts, gate_weight, up_weight, down_weight):
    dp_count = lax.axis_size("dp")
    tensor_count = lax.axis_size("tensor")
    held_count = max(1, E // dp_count)
    copies = max(1, dp_count // E)
    tok_rows = tokens.shape[0]
    piece_rows = gate_weight.shape[0]
    FF = piece_rows * dp_count * tensor_count // E
    slot_total = E * CAP
    device_rank = lax.axis_index("dp") * tensor_count + lax.axis_index("tensor")
    own_expert = device_rank * piece_rows // FF
    own_group = own_expert % held_count
    expert_ids = jnp.arange(E, dtype=jnp.int32)
    kept_table = jnp.any(kept_experts[:, None] == expert_ids[None, :], axis=0).astype(jnp.float32)
    own_kept = jnp.sum(jnp.where(expert_ids == own_expert, kept_table, 0.0))
    route_experts = routes.reshape(-1)
    route_onehot = (route_experts[:, None] == expert_ids[None, :]).astype(jnp.int32)
    route_rank = jnp.sum((jnp.cumsum(route_onehot, axis=0) - route_onehot) * route_onehot, axis=1)
    route_slot = route_experts * CAP + route_rank
    gate_probs = jax.nn.softmax(route_logits, axis=-1).reshape(-1)
    route_kept = jnp.sum(route_onehot.astype(jnp.float32) * kept_table[None, :], axis=1)
    slot_match = (jnp.arange(slot_total, dtype=jnp.int32)[:, None] == route_slot[None, :]).astype(
        jnp.float32
    )
    pick_tokens = slot_match.reshape(slot_total, tok_rows, 2).sum(axis=2)
    kept_weights = (
        (slot_match * (gate_probs * route_kept)[None, :])
        .reshape(slot_total, tok_rows, 2)
        .sum(axis=2)
    )
    dropped_weights = (
        (slot_match * (gate_probs * (1.0 - route_kept))[None, :])
        .reshape(slot_total, tok_rows, 2)
        .sum(axis=2)
    )
    by_expert = jnp.dot(
        pick_tokens.astype(jnp.bfloat16), tokens, preferred_element_type=jnp.float32
    ).astype(jnp.bfloat16)
    outgoing = spread_copies(by_expert.reshape(E, CAP, -1), E, held_count, copies)
    chosen = lax.dynamic_index_in_dim(
        lax.all_to_all(outgoing, "dp", split_axis=0, concat_axis=0, tiled=True),
        own_group,
        1,
        keepdims=False,
    )
    contract = (((2,), (1,)), ((), ()))
    gate_part = lax.dot_general(chosen, gate_weight, contract, preferred_element_type=jnp.float32)
    up_part = lax.dot_general(chosen, up_weight, contract, preferred_element_type=jnp.float32)
    gate_part, up_part = (gate_part, up_part)
    gate_sum, up_sum = (
        lax.psum(gate_part.astype(jnp.bfloat16), "col").astype(jnp.float32),
        lax.psum(up_part.astype(jnp.bfloat16), "col").astype(jnp.float32),
    )
    hidden = (jax.nn.silu(gate_sum) * up_sum).astype(jnp.bfloat16)
    expert_out = lax.dot_general(
        hidden, down_weight, (((2,), (0,)), ((), ())), preferred_element_type=jnp.float32
    ).astype(jnp.bfloat16)
    hidden_wide = hidden.astype(jnp.float32)
    group_mask = (jnp.arange(held_count) == own_group)[None, :, None, None]
    placed = jnp.where(group_mask, expert_out[:, None], jnp.zeros((), jnp.bfloat16))
    returned = lax.all_to_all(placed, "dp", split_axis=0, concat_axis=0, tiled=True)
    slot_values = expert_major(returned.astype(jnp.float32), E, held_count, copies)
    dropped_part = jnp.dot(dropped_weights.T, slot_values, precision=top_precision)
    dropped = lax.psum(dropped_part, "tensor")
    ridge_weight = ridge_share * 2.0 * tok_rows * dp_count / E

    def apply_backward(image_tokens):
        slot_image = jnp.dot(kept_weights, image_tokens, precision=top_precision)
        outgoing_image = spread_copies(slot_image.reshape(E, CAP, -1), E, held_count, copies)
        arrived = lax.all_to_all(outgoing_image, "dp", split_axis=0, concat_axis=0, tiled=True)
        chosen = lax.dynamic_index_in_dim(arrived, own_group, 1, keepdims=False)
        return exact_product(hidden_wide, chosen, (((0, 1), (0, 1)), ((), ())))

    def total_norm(values):
        return lax.psum(jnp.sum(values * values), ("dp", "tensor", "col"))

    base_down = down_weight.astype(jnp.float32)
    residual = apply_backward(dropped) - ridge_weight * own_kept * base_down
    res_norm = total_norm(residual)
    direction = residual
    leftover = dropped
    for turn_index in range(ITERS):
        slot_part = exact_product(hidden_wide, direction, (((2,), (0,)), ((), ())))
        placed_part = jnp.where(group_mask, slot_part[:, None], 0.0)
        came_back = lax.all_to_all(placed_part, "dp", split_axis=0, concat_axis=0, tiled=True)
        image_part = jnp.dot(
            kept_weights.T, expert_major(came_back, E, held_count, copies), precision=top_precision
        )
        image_tokens = lax.psum(image_part, "tensor")
        first_copy = (lax.axis_index("tensor") == 0).astype(jnp.float32)
        local_term = first_copy * jnp.sum(image_tokens * image_tokens) + ridge_weight * jnp.sum(
            direction * direction
        )
        curvature = lax.psum(local_term, ("dp", "tensor", "col"))
        step_size = res_norm / curvature
        leftover = leftover - step_size * image_tokens
        if turn_index + 1 < ITERS:
            curved = apply_backward(image_tokens) + ridge_weight * direction
            residual = residual - step_size * curved
            next_norm = total_norm(residual)
            direction = residual + next_norm / res_norm * direction
            res_norm = next_norm
    return leftover


def shards(*arrays):
    sizes = [lax.axis_size(axis) for axis in ("dp", "tensor", "col")]
    if sizes[0] * sizes[1] == E and sizes[2] == 4 and ITERS == 2:
        return one_expert_each(*arrays)
    return general(*arrays)


def solution(mesh):
    placed = (
        P("dp", "col"),
        P("dp", None),
        P("dp", None),
        P(),
        P(("dp", "tensor"), "col"),
        P(("dp", "tensor"), "col"),
        P(("dp", "tensor"), "col"),
    )
    return jax.shard_map(
        shards, mesh=mesh, in_specs=placed, out_specs=P("dp", "col"), check_vma=False
    )
```

```python
import functools

import jax
import jax.numpy as jnp
from jax import lax
from jax.experimental import pallas as pl
from jax.experimental.pallas import tpu as pltpu
from jax.sharding import PartitionSpec as P

E = 8
ITERS = 2
CAP = 40
CHUNKS = 4


ridge_share = 0.25
top_precision = lax.Precision.HIGHEST
MIB = 1024 * 1024
LIGHT = pl.CostEstimate(flops=1, bytes_accessed=1, transcendentals=0)
f32 = jnp.float32
bf16 = jnp.bfloat16
NT = (((1,), (1,)), ((), ()))
NN = (((1,), (0,)), ((), ()))
TN = (((0,), (0,)), ((), ()))


def whole():
    return pl.BlockSpec(memory_space=pltpu.VMEM)


def scalars():
    return pl.BlockSpec(memory_space=pltpu.SMEM)


def mm(left, right, contract=NN):
    return lax.dot_general(left, right, contract, preferred_element_type=f32)


def split_wide(values):
    high = values.astype(bf16)
    low = (values - high.astype(f32)).astype(bf16)
    return jnp.concatenate([high, low], axis=1)


def mm_wide(left, right, contract=NN):
    lanes = right.shape[1]
    both = mm(left, split_wide(right), contract)
    return both[:, :lanes] + both[:, lanes:]


def params(mib):
    return pltpu.CompilerParams(vmem_limit_bytes=mib * MIB)


def block_slots(first, second):
    count = first.shape[1]
    expert_rows = lax.broadcasted_iota(jnp.int32, (E, count), 0).astype(f32)
    hot_first = (expert_rows == first).astype(f32)
    hot_second = (expert_rows == second).astype(f32)
    before = (
        lax.broadcasted_iota(jnp.int32, (count, count), 0)
        < lax.broadcasted_iota(jnp.int32, (count, count), 1)
    ).astype(bf16)
    place = mm((hot_first + hot_second).astype(bf16), before)
    ranked_first = jnp.sum(hot_first * place, axis=0, keepdims=True)
    ranked_second = jnp.sum(hot_second * place, axis=0, keepdims=True)
    return ranked_first, ranked_second


def pick_kernel(parts, tensor_count, place_ref, info_ref, tokens_ref, *out_refs):
    first, second = info_ref[0:1, :], info_ref[1:2, :]
    rank_first, rank_second = block_slots(first, second)
    count = first.shape[1]
    rows = lax.broadcasted_iota(jnp.int32, (CAP, count), 0).astype(f32)
    values = tokens_ref[...]
    logits = info_ref[2:4, :]
    high = logits.astype(bf16).astype(f32)
    middle = (logits - high).astype(bf16).astype(f32)
    extra = jnp.concatenate([info_ref[0:2, :], high, middle, logits - high - middle], axis=0)
    extra = jnp.concatenate([extra, jnp.zeros((8, values.shape[1] - count), f32)], axis=1)
    for shift, out_ref in enumerate(out_refs):
        expert = (lax.rem(place_ref[0] + shift, parts) * tensor_count + place_ref[1]).astype(f32)
        hit = ((first == expert) & (rank_first == rows)) | ((second == expert) & (rank_second == rows))
        rows_picked = mm(hit.astype(f32).astype(bf16), values)
        out_ref[...] = jnp.concatenate([rows_picked, extra], axis=0).astype(bf16)


def stack_kernel(*refs):
    pieces, (rows_ref, info_ref) = refs[:-2], refs[-2:]
    wide = [ref[...].astype(f32) for ref in pieces]
    rows_ref[...] = jnp.concatenate([value[:CAP] for value in wide], axis=0).astype(bf16)
    for index, value in enumerate(wide):
        extra = value[CAP : CAP + 8, : info_ref.shape[2]]
        info_ref[index, 0:2, :] = extra[0:2]
        info_ref[index, 2:4, :] = extra[2:4] + extra[4:6] + extra[6:8]


def gate_up_kernel(has_keep, order_ref, inputs_ref, gate_ref, up_ref, *rest):
    values = inputs_ref[...]
    gate = mm(values, gate_ref[...], NT).astype(bf16)
    up = mm(values, up_ref[...], NT).astype(bf16)
    step = pl.program_id(0)
    outs = rest[-(1 + (has_keep == 2)) :]
    for index, ref in enumerate(outs):

        @pl.when(step // 2 == index)
        def _(ref=ref):
            ref[0, 0] = gate
            ref[0, 1] = up


def gate_up(order, inputs, gate_weight, up_weight, width, keep, send, after):
    slots, depth = inputs.shape
    quarter = gate_weight.shape[0] // 4
    gate_weight = gate_weight.reshape(4, quarter, depth)
    up_weight = up_weight.reshape(4, quarter, depth)
    base = 0 if keep is not None else 2
    chunks = [chunk for chunk in (keep, send) if chunk is not None]
    count = len(chunks)

    def place(s, order):
        return (order[base + s], chunks[0] if count == 1 else jnp.where(s < 2, chunks[0], chunks[1]), 0)

    weight_spec = pl.BlockSpec((None, width, depth), place)
    out_specs = [
        pl.BlockSpec(
            (1, 2, slots, width),
            lambda s, order, index=index: (jnp.clip(s - 2 * index, 0, 1), 0, 0, 0),
        )
        for index in range(count)
    ]
    return pl.pallas_call(
        functools.partial(gate_up_kernel, count),
        grid_spec=pltpu.PrefetchScalarGridSpec(
            num_scalar_prefetch=1,
            grid=(2 * count,),
            in_specs=[
                pl.BlockSpec((slots, depth), lambda s, order: (0, 0)),
                weight_spec,
                weight_spec,
            ]
            + [pl.BlockSpec(memory_space=pl.ANY)] * len(after),
            out_specs=out_specs,
        ),
        out_shape=[jax.ShapeDtypeStruct((2, 2, slots, width), bf16)] * count,
        compiler_params=params(41),
        cost_estimate=pl.CostEstimate(
            flops=32 * count * slots * depth * width,
            bytes_accessed=32 * count * width * depth,
            transcendentals=0,
        ),
        name=f"gate_up_{chunks[-1] + (send is None)}",
    )(order, inputs, gate_weight, up_weight, *after)


def down_kernel(count, pack, has_old, order_ref, place_ref, *refs):
    pieces, down_ref, rest = refs[:count], refs[count], refs[count + 1 :]
    old, new = rest[:3] if has_old else (), rest[3 * has_old :]
    packed_refs = ()
    if pack:
        packed_refs, new = new[:-3], new[-3:]
    step = pl.program_id(0)

    @pl.when(step == 0)
    def _():
        for index, ref in enumerate(new):
            ref[...] = old[index][...] if old else jnp.zeros_like(ref)

    out_ref, gram_ref, square_ref = new
    weight = down_ref[...]
    wide = weight.astype(f32)
    square_ref[...] += jnp.sum((wide * wide).reshape(-1, 8, wide.shape[1]), axis=0)
    for index, ref in enumerate(pieces):

        @pl.when(step == index)
        def _(ref=ref, index=index):
            values = ref[...]
            out_ref[...] += mm(values, weight)
            gram_ref[...] += mm(values, values, NT)
            if pack and index == len(pieces) - 1:
                dp_count, tensor_count = pack
                columns = out_ref.shape[1]
                lanes = columns // (dp_count * tensor_count)
                group = columns // dp_count
                gram = gram_ref[...]
                rolled = pltpu.roll(out_ref[...], lax.rem(columns - place_ref[0] * group, columns), 1)
                for ahead in range(dp_count):
                    parts = [
                        rolled[:, ahead * group + part * lanes : ahead * group + (part + 1) * lanes]
                        for part in range(tensor_count)
                    ]
                    for aside in range(tensor_count):
                        target = lax.rem(place_ref[1] + aside, tensor_count)
                        piece = parts[0]
                        for part in range(1, tensor_count):
                            piece = jnp.where(target == part, parts[part], piece)
                        packed_refs[ahead * tensor_count + aside][...] = jnp.concatenate(
                            [gram, piece], axis=1
                        ).astype(bf16)


def down(order, place, pieces, down_weight, first, older, pack=None):
    slots, width = pieces[0].shape
    columns = down_weight.shape[1]
    down_weight = down_weight.reshape(-1, width, columns)

    def fixed(shape):
        return pl.BlockSpec(shape, lambda s, order, place: (0,) * len(shape))

    shapes = [(slots, columns), (slots, slots), (8, columns)]
    out_shape = [jax.ShapeDtypeStruct(shape, f32) for shape in shapes]
    if pack:
        parts = pack[0] * pack[1]
        packed = (slots, slots + columns // parts)
        out_shape = [jax.ShapeDtypeStruct(packed, bf16)] * parts + out_shape
    return pl.pallas_call(
        functools.partial(down_kernel, len(pieces), pack, bool(older)),
        grid_spec=pltpu.PrefetchScalarGridSpec(
            num_scalar_prefetch=2,
            grid=(len(pieces),),
            in_specs=[fixed((slots, width))] * len(pieces)
            + [pl.BlockSpec((None, width, columns), lambda s, order, place: (order[first + s], 0, 0))]
            + [fixed(value.shape) for value in older],
            out_specs=[fixed(value.shape) for value in out_shape],
        ),
        out_shape=out_shape,
        compiler_params=params(20),
        cost_estimate=pl.CostEstimate(
            flops=8 * len(pieces) * slots * width * columns,
            bytes_accessed=8 * len(pieces) * width * columns,
            transcendentals=0,
        ),
        name=f"down_{first}",
    )(order, place, *pieces, down_weight, *older)


def route_kernel(blocks, tensor_count, kept_ref, place_ref, *refs):
    infos = [refs[0][block] for block in range(blocks)]
    hot_ref, turned_ref, gates_ref, wide_ref = refs[-4:]
    count = infos[0].shape[1]
    slots = blocks * CAP
    zero = jnp.zeros((CAP, count), f32)
    rows = lax.broadcasted_iota(jnp.int32, (CAP, count), 0).astype(f32)
    routed = []
    for block in range(blocks):
        first, second = infos[block][0:1, :], infos[block][1:2, :]
        delta = infos[block][3:4, :] - infos[block][2:3, :]
        share_first = 1.0 / (1.0 + jnp.exp(delta))
        share_second = 1.0 / (1.0 + jnp.exp(-delta))
        routed.append((first, second, share_first, share_second) + block_slots(first, second))
    for back in range(blocks):
        for aside in range(tensor_count):
            expert = lax.rem(place_ref[0] + blocks - back, blocks) * tensor_count
            expert = expert + lax.rem(place_ref[1] + tensor_count - aside, tensor_count)
            kept = jnp.zeros((), jnp.int32)
            for index in range(kept_ref.shape[0]):
                kept = kept | (kept_ref[index] == expert).astype(jnp.int32)
            kept, expert = kept.astype(f32), expert.astype(f32)
            for shift in range(blocks):
                block = (back + shift) % blocks
                first, second, share_first, share_second, rank_first, rank_second = routed[block]
                hit_first = (first == expert) & (rank_first == rows)
                hit_second = (second == expert) & (rank_second == rows)
                gate = jnp.sum(
                    jnp.where(hit_first, share_first, zero) + jnp.where(hit_second, share_second, zero),
                    axis=1,
                    keepdims=True,
                )
                row = (back * tensor_count + aside) * slots + shift * CAP
                for other in range(blocks):
                    wide_ref[row : row + CAP, other * count : (other + 1) * count] = (
                        (hit_first | hit_second).astype(f32) if other == block else zero
                    )
                gates_ref[row : row + CAP, 0:1] = gate * kept
                gates_ref[row : row + CAP, 1:2] = gate * (1.0 - kept)
    hot_ref[...] = wide_ref[...].astype(bf16)
    turned_ref[...] = wide_ref[...].T.astype(bf16)


def solve_kernel(ridge, slots, own_ref, hot_ref, turned_ref, gates_ref, square_ref, *refs):
    packed_refs, (base_ref, zero_ref, one_ref, sums_ref) = refs[:E], refs[E:]
    hot, turned = hot_ref[...], turned_ref[...]
    kept, dropped = gates_ref[:, 0:1], gates_ref[:, 1:2]
    values = jnp.concatenate([packed_refs[e][:, slots:].astype(f32) for e in range(E)], axis=0)
    base = mm_wide(turned, dropped * values)
    output = mm_wide(turned, kept * values)

    def apply(field):
        spread = kept * mm_wide(hot, field)
        mixed = jnp.concatenate(
            [
                mm_wide(packed_refs[e][:, :slots], spread[e * slots : (e + 1) * slots])
                for e in range(E)
            ],
            axis=0,
        )
        return mm_wide(turned, kept * mixed)

    curved = apply(base)
    zero = curved - ridge * output
    one = apply(zero)
    base_ref[...] = base
    zero_ref[...] = zero
    one_ref[...] = one
    norm = jnp.sum(base * (curved - 2.0 * ridge * output))
    square = jnp.sum(square_ref[...]) * own_ref[0]
    lane = lax.broadcasted_iota(jnp.int32, sums_ref.shape[1:], 1)
    sums = jnp.where(lane == 0, norm + ridge * ridge * square, 0.0)
    for index, value in enumerate((jnp.sum(zero * zero), jnp.sum(zero * one), jnp.sum(one * one))):
        sums = jnp.where(lane == index + 1, value, sums)
    for part in range(sums_ref.shape[0]):
        sums_ref[part] = sums


def finish_kernel(ridge, blocks, copies, place_ref, base_ref, zero_ref, one_ref, sums_ref, out_ref):
    sums = jnp.sum(sums_ref[...], axis=0)[0:1, :]
    norm, zero_zero = sums[:, 0:1], sums[:, 1:2]
    zero_one, one_one = sums[:, 2:3], sums[:, 3:4]
    step = norm / (zero_zero + ridge * norm)
    left = 1.0 - step * ridge
    new = left * left * norm - 2.0 * left * step * zero_zero + step * step * zero_one
    ratio = new / norm
    grown = left + ratio
    image = grown * grown * zero_zero - 2.0 * grown * step * zero_one + step * step * one_one
    later = new / (image + ridge * (new + ratio * ratio * norm))
    field = base_ref[...] - (step + later * grown) * zero_ref[...] + (later * step) * one_ref[...]
    rows = field.shape[0] // blocks
    sideways = field.T.astype(bf16)
    for back in range(blocks):
        target = lax.rem(place_ref[0] + blocks - back, blocks) * copies
        for copy in range(copies):
            out_ref[target + copy] = sideways[:, back * rows : (back + 1) * rows]


def join_kernel(pieces_ref, out_ref):
    rows = jnp.concatenate([pieces_ref[part].astype(f32) for part in range(pieces_ref.shape[0])], axis=0)
    out_ref[...] = rows.T


def single(kernel, out_shape, in_specs, mib, name, scratch=()):
    many = isinstance(out_shape, list)
    return pl.pallas_call(
        kernel,
        out_shape=out_shape,
        in_specs=in_specs,
        out_specs=[whole()] * len(out_shape) if many else whole(),
        scratch_shapes=list(scratch),
        compiler_params=params(mib),
        cost_estimate=LIGHT,
        name=name,
    )


def one_expert_each(tokens, routes, route_logits, kept_experts, gate_weight, up_weight, down_weight):
    dp_count = lax.axis_size("dp")
    tensor_count = lax.axis_size("tensor")
    parts = dp_count * tensor_count
    tok_rows, depth = tokens.shape
    units, columns = down_weight.shape
    slots = dp_count * CAP
    lanes = columns // parts
    width = units // 4 // CHUNKS
    ridge = ridge_share * 2.0 * tok_rows * dp_count / E
    dp_index = lax.axis_index("dp")
    tensor_index = lax.axis_index("tensor")
    col_index = lax.axis_index("col")
    own_expert = dp_index * tensor_count + tensor_index
    place = jnp.stack([dp_index, tensor_index])

    def beside(values):
        return lax.ppermute(values, "col", [(k, k ^ 1) for k in range(4)])

    def across(values):
        return lax.ppermute(values, "col", [(k, k ^ 2) for k in range(4)])

    def shifted(values, ahead, aside=0):
        if ahead == 0 and aside == 0:
            return values
        pairs = [
            (i * tensor_count + j, (i + ahead) % dp_count * tensor_count + (j + aside) % tensor_count)
            for i in range(dp_count)
            for j in range(tensor_count)
        ]
        return lax.ppermute(values, ("dp", "tensor"), pairs)

    shifts = [(ahead, aside) for ahead in range(dp_count) for aside in range(tensor_count)]
    upper = lax.pad(routes.T, jnp.int32(0), ((0, 2, 0), (0, 0, 0))).astype(f32)
    info = upper + lax.pad(route_logits.T, f32(0), ((2, 0, 0), (0, 0, 0)))
    picked = single(
        functools.partial(pick_kernel, dp_count, tensor_count),
        [jax.ShapeDtypeStruct((CAP + 8, depth), bf16)] * dp_count,
        [scalars(), whole(), whole()],
        16,
        "pick",
    )(place, info, tokens)
    arrived = [shifted(value, ahead) for ahead, value in enumerate(picked)]
    inputs, infos = single(
        stack_kernel,
        [jax.ShapeDtypeStruct((slots, depth), bf16), jax.ShapeDtypeStruct((dp_count, 4, tok_rows), f32)],
        [whole()] * dp_count,
        16,
        "stack",
    )(*arrived)

    gate_order = col_index ^ jnp.array([2, 0, 3, 1], jnp.int32)
    near_first = jnp.array([0, 2, 1, 3] * CHUNKS, jnp.int32)
    down_order = (col_index ^ near_first) * CHUNKS + jnp.arange(4 * CHUNKS, dtype=jnp.int32) // 4

    def products(keep, send, after=()):
        return gate_up(gate_order, inputs, gate_weight, up_weight, width, keep, send, after)

    last = CHUNKS - 1
    keeps, nears, pairs, fars, owns = [], [], [], [], []

    def activate(chunk, after):
        far = lax.optimization_barrier((fars[chunk], *after))[0] if after else fars[chunk]
        total = keeps[chunk][1].astype(f32) + nears[chunk][1].astype(f32) + far.astype(f32)
        owns.append((jax.nn.silu(total[0]) * total[1]).astype(bf16))

    nears.append(beside(products(None, 0)[0]))
    for chunk in range(CHUNKS):
        after = [keeps[-1]] if chunk else []
        if chunk >= 2:
            activate(chunk - 2, [pairs[chunk - 1]])
            after.extend([pairs[chunk - 1], owns[chunk - 2]])
        if chunk < last:
            keep, send = products(chunk, chunk + 1, after)
            nears.append(beside(send))
        else:
            (keep,) = products(chunk, None, after)
        keeps.append(keep)
        pairs.append((keep[0].astype(f32) + nears[chunk][0].astype(f32)).astype(bf16))
        fars.append(across(pairs[-1]))
    older, olders, queue, counts = (), [], [], []
    for chunk in range(CHUNKS):
        if chunk >= len(owns):
            after = [pairs[last]]
            if chunk >= 2:
                after.append(olders[chunk - 2][2])
            activate(chunk, after)
        own = owns[chunk]
        other = across(own)
        if chunk + 2 <= last:
            own, other = lax.optimization_barrier((own, other, pairs[last]))[:2]
        queue.extend((own, other, beside(own), beside(other)))
        done = sum(counts)
        if chunk < last - 1:
            counts.append(4)
        elif chunk == last - 1:
            counts.append(3)
        else:
            counts.extend([4, 1])
        for count in counts[len(olders) :]:
            pack = (dp_count, tensor_count) if done + count == 4 * CHUNKS else None
            older = down(down_order, place, queue[done : done + count], down_weight, done, older, pack)
            olders.append(older)
            done += count
    packed, (_, _, square) = older[:parts], older[parts:]
    spread = [shifted(value, *shift) for value, shift in zip(packed, shifts)]

    total_slots, total_tokens = E * slots, dp_count * tok_rows
    hot, turned_hot, gates = single(
        functools.partial(route_kernel, dp_count, tensor_count),
        [
            jax.ShapeDtypeStruct((total_slots, total_tokens), bf16),
            jax.ShapeDtypeStruct((total_tokens, total_slots), bf16),
            jax.ShapeDtypeStruct((total_slots, 2), f32),
        ],
        [scalars(), scalars(), whole(), pl.BlockSpec(memory_space=pl.ANY)],
        24,
        "route",
        [pltpu.VMEM((total_slots, total_tokens), f32)],
    )(kept_experts, place, infos, square)
    is_kept = jnp.any(kept_experts == own_expert).astype(f32).reshape(1)
    field = jax.ShapeDtypeStruct((total_tokens, lanes), f32)
    everyone = parts * lax.axis_size("col")
    base, zero, one, sums = single(
        functools.partial(solve_kernel, ridge, slots),
        [field, field, field, jax.ShapeDtypeStruct((everyone, 1, 128), f32)],
        [scalars()] + [whole()] * (4 + E),
        40,
        "solve",
    )(is_kept, hot, turned_hot, gates, square, *spread)
    sums = lax.all_to_all(sums, ("dp", "tensor", "col"), split_axis=0, concat_axis=0, tiled=True)

    home = single(
        functools.partial(finish_kernel, ridge, dp_count, tensor_count),
        jax.ShapeDtypeStruct((parts, lanes, tok_rows), bf16),
        [scalars()] + [whole()] * 4,
        16,
        "finish",
    )(place, base, zero, one, sums)
    home = lax.all_to_all(home, ("dp", "tensor"), split_axis=0, concat_axis=0, tiled=True)
    return single(
        join_kernel,
        jax.ShapeDtypeStruct((tok_rows, columns), f32),
        [whole()],
        16,
        "join",
    )(home)


def spread_copies(values, experts, held_count, copies):
    old_shape = values.shape
    grouped = values.reshape((experts // held_count, 1, held_count) + old_shape[1:])
    widened = jnp.broadcast_to(grouped, (experts // held_count, copies, held_count) + old_shape[1:])
    return widened.reshape((experts // held_count * copies, held_count) + old_shape[1:])


def expert_major(returned, experts, held_count, copies):
    old_shape = returned.shape
    grouped = returned.reshape((experts // held_count, copies, held_count) + old_shape[2:])
    merged = jnp.sum(grouped, axis=1)
    return merged.reshape((experts * old_shape[2],) + old_shape[3:])


def exact_product(left, right, contract):
    return lax.dot_general(
        left, right, contract, precision=top_precision, preferred_element_type=jnp.float32
    )


def general(tokens, routes, route_logits, kept_experts, gate_weight, up_weight, down_weight):
    dp_count = lax.axis_size("dp")
    tensor_count = lax.axis_size("tensor")
    held_count = max(1, E // dp_count)
    copies = max(1, dp_count // E)
    tok_rows = tokens.shape[0]
    piece_rows = gate_weight.shape[0]
    FF = piece_rows * dp_count * tensor_count // E
    slot_total = E * CAP
    device_rank = lax.axis_index("dp") * tensor_count + lax.axis_index("tensor")
    own_expert = device_rank * piece_rows // FF
    own_group = own_expert % held_count
    expert_ids = jnp.arange(E, dtype=jnp.int32)
    kept_table = jnp.any(kept_experts[:, None] == expert_ids[None, :], axis=0).astype(jnp.float32)
    own_kept = jnp.sum(jnp.where(expert_ids == own_expert, kept_table, 0.0))
    route_experts = routes.reshape(-1)
    route_onehot = (route_experts[:, None] == expert_ids[None, :]).astype(jnp.int32)
    route_rank = jnp.sum((jnp.cumsum(route_onehot, axis=0) - route_onehot) * route_onehot, axis=1)
    route_slot = route_experts * CAP + route_rank
    gate_probs = jax.nn.softmax(route_logits, axis=-1).reshape(-1)
    route_kept = jnp.sum(route_onehot.astype(jnp.float32) * kept_table[None, :], axis=1)
    slot_match = (jnp.arange(slot_total, dtype=jnp.int32)[:, None] == route_slot[None, :]).astype(
        jnp.float32
    )
    pick_tokens = slot_match.reshape(slot_total, tok_rows, 2).sum(axis=2)
    kept_weights = (
        (slot_match * (gate_probs * route_kept)[None, :])
        .reshape(slot_total, tok_rows, 2)
        .sum(axis=2)
    )
    dropped_weights = (
        (slot_match * (gate_probs * (1.0 - route_kept))[None, :])
        .reshape(slot_total, tok_rows, 2)
        .sum(axis=2)
    )
    by_expert = jnp.dot(
        pick_tokens.astype(jnp.bfloat16), tokens, preferred_element_type=jnp.float32
    ).astype(jnp.bfloat16)
    outgoing = spread_copies(by_expert.reshape(E, CAP, -1), E, held_count, copies)
    chosen = lax.dynamic_index_in_dim(
        lax.all_to_all(outgoing, "dp", split_axis=0, concat_axis=0, tiled=True),
        own_group,
        1,
        keepdims=False,
    )
    contract = (((2,), (1,)), ((), ()))
    gate_part = lax.dot_general(chosen, gate_weight, contract, preferred_element_type=jnp.float32)
    up_part = lax.dot_general(chosen, up_weight, contract, preferred_element_type=jnp.float32)
    gate_part, up_part = (gate_part, up_part)
    gate_sum, up_sum = (
        lax.psum(gate_part.astype(jnp.bfloat16), "col").astype(jnp.float32),
        lax.psum(up_part.astype(jnp.bfloat16), "col").astype(jnp.float32),
    )
    hidden = (jax.nn.silu(gate_sum) * up_sum).astype(jnp.bfloat16)
    expert_out = lax.dot_general(
        hidden, down_weight, (((2,), (0,)), ((), ())), preferred_element_type=jnp.float32
    ).astype(jnp.bfloat16)
    hidden_wide = hidden.astype(jnp.float32)
    group_mask = (jnp.arange(held_count) == own_group)[None, :, None, None]
    placed = jnp.where(group_mask, expert_out[:, None], jnp.zeros((), jnp.bfloat16))
    returned = lax.all_to_all(placed, "dp", split_axis=0, concat_axis=0, tiled=True)
    slot_values = expert_major(returned.astype(jnp.float32), E, held_count, copies)
    dropped_part = jnp.dot(dropped_weights.T, slot_values, precision=top_precision)
    dropped = lax.psum(dropped_part, "tensor")
    ridge_weight = ridge_share * 2.0 * tok_rows * dp_count / E

    def apply_backward(image_tokens):
        slot_image = jnp.dot(kept_weights, image_tokens, precision=top_precision)
        outgoing_image = spread_copies(slot_image.reshape(E, CAP, -1), E, held_count, copies)
        arrived = lax.all_to_all(outgoing_image, "dp", split_axis=0, concat_axis=0, tiled=True)
        chosen = lax.dynamic_index_in_dim(arrived, own_group, 1, keepdims=False)
        return exact_product(hidden_wide, chosen, (((0, 1), (0, 1)), ((), ())))

    def total_norm(values):
        return lax.psum(jnp.sum(values * values), ("dp", "tensor", "col"))

    base_down = down_weight.astype(jnp.float32)
    residual = apply_backward(dropped) - ridge_weight * own_kept * base_down
    res_norm = total_norm(residual)
    direction = residual
    leftover = dropped
    for turn_index in range(ITERS):
        slot_part = exact_product(hidden_wide, direction, (((2,), (0,)), ((), ())))
        placed_part = jnp.where(group_mask, slot_part[:, None], 0.0)
        came_back = lax.all_to_all(placed_part, "dp", split_axis=0, concat_axis=0, tiled=True)
        image_part = jnp.dot(
            kept_weights.T, expert_major(came_back, E, held_count, copies), precision=top_precision
        )
        image_tokens = lax.psum(image_part, "tensor")
        first_copy = (lax.axis_index("tensor") == 0).astype(jnp.float32)
        local_term = first_copy * jnp.sum(image_tokens * image_tokens) + ridge_weight * jnp.sum(
            direction * direction
        )
        curvature = lax.psum(local_term, ("dp", "tensor", "col"))
        step_size = res_norm / curvature
        leftover = leftover - step_size * image_tokens
        if turn_index + 1 < ITERS:
            curved = apply_backward(image_tokens) + ridge_weight * direction
            residual = residual - step_size * curved
            next_norm = total_norm(residual)
            direction = residual + next_norm / res_norm * direction
            res_norm = next_norm
    return leftover


def shards(*arrays):
    sizes = [lax.axis_size(axis) for axis in ("dp", "tensor", "col")]
    if sizes[0] * sizes[1] == E and sizes[2] == 4 and ITERS == 2:
        return one_expert_each(*arrays)
    return general(*arrays)


def solution(mesh):
    placed = (
        P("dp", "col"),
        P("dp", None),
        P("dp", None),
        P(),
        P(("dp", "tensor"), "col"),
        P(("dp", "tensor"), "col"),
        P(("dp", "tensor"), "col"),
    )
    return jax.shard_map(
        shards, mesh=mesh, in_specs=placed, out_specs=P("dp", "col"), check_vma=False
    )
```

```python
import functools

import jax
import jax.numpy as jnp
from jax import lax
from jax.experimental import pallas as pl
from jax.experimental.pallas import tpu as pltpu
from jax.sharding import PartitionSpec as P

E = 8
ITERS = 2
CAP = 40
CHUNKS = 4


ridge_share = 0.25
top_precision = lax.Precision.HIGHEST
MIB = 1024 * 1024
LIGHT = pl.CostEstimate(flops=1, bytes_accessed=1, transcendentals=0)
f32 = jnp.float32
bf16 = jnp.bfloat16
NT = (((1,), (1,)), ((), ()))
NN = (((1,), (0,)), ((), ()))
TN = (((0,), (0,)), ((), ()))


def whole():
    return pl.BlockSpec(memory_space=pltpu.VMEM)


def scalars():
    return pl.BlockSpec(memory_space=pltpu.SMEM)


def mm(left, right, contract=NN):
    return lax.dot_general(left, right, contract, preferred_element_type=f32)


def split_wide(values):
    high = values.astype(bf16)
    low = (values - high.astype(f32)).astype(bf16)
    return jnp.concatenate([high, low], axis=1)


def mm_wide(left, right, contract=NN):
    lanes = right.shape[1]
    both = mm(left, split_wide(right), contract)
    return both[:, :lanes] + both[:, lanes:]


def params(mib):
    return pltpu.CompilerParams(vmem_limit_bytes=mib * MIB)


def block_slots(first, second):
    count = first.shape[1]
    expert_rows = lax.broadcasted_iota(jnp.int32, (E, count), 0).astype(f32)
    hot_first = (expert_rows == first).astype(f32)
    hot_second = (expert_rows == second).astype(f32)
    before = (
        lax.broadcasted_iota(jnp.int32, (count, count), 0)
        < lax.broadcasted_iota(jnp.int32, (count, count), 1)
    ).astype(bf16)
    place = mm((hot_first + hot_second).astype(bf16), before)
    ranked_first = jnp.sum(hot_first * place, axis=0, keepdims=True)
    ranked_second = jnp.sum(hot_second * place, axis=0, keepdims=True)
    return ranked_first, ranked_second


def pick_kernel(parts, tensor_count, place_ref, info_ref, tokens_ref, *out_refs):
    first, second = info_ref[0:1, :], info_ref[1:2, :]
    rank_first, rank_second = block_slots(first, second)
    count = first.shape[1]
    rows = lax.broadcasted_iota(jnp.int32, (CAP, count), 0).astype(f32)
    values = tokens_ref[...]
    logits = info_ref[2:4, :]
    high = logits.astype(bf16).astype(f32)
    middle = (logits - high).astype(bf16).astype(f32)
    extra = jnp.concatenate([info_ref[0:2, :], high, middle, logits - high - middle], axis=0)
    extra = jnp.concatenate([extra, jnp.zeros((8, values.shape[1] - count), f32)], axis=1)
    for shift, out_ref in enumerate(out_refs):
        expert = (lax.rem(place_ref[0] + shift, parts) * tensor_count + place_ref[1]).astype(f32)
        hit = ((first == expert) & (rank_first == rows)) | ((second == expert) & (rank_second == rows))
        rows_picked = mm(hit.astype(f32).astype(bf16), values)
        out_ref[...] = jnp.concatenate([rows_picked, extra], axis=0).astype(bf16)


def stack_kernel(*refs):
    pieces, (rows_ref, info_ref) = refs[:-2], refs[-2:]
    wide = [ref[...].astype(f32) for ref in pieces]
    rows_ref[...] = jnp.concatenate([value[:CAP] for value in wide], axis=0).astype(bf16)
    for index, value in enumerate(wide):
        extra = value[CAP : CAP + 8, : info_ref.shape[2]]
        info_ref[index, 0:2, :] = extra[0:2]
        info_ref[index, 2:4, :] = extra[2:4] + extra[4:6] + extra[6:8]


def gate_up_kernel(has_keep, order_ref, inputs_ref, gate_ref, up_ref, *rest):
    values = inputs_ref[...]
    gate = mm(values, gate_ref[...], NT).astype(bf16)
    up = mm(values, up_ref[...], NT).astype(bf16)
    step = pl.program_id(0)
    outs = rest[-(1 + (has_keep == 2)) :]
    for index, ref in enumerate(outs):

        @pl.when(step // 2 == index)
        def _(ref=ref):
            ref[0, 0] = gate
            ref[0, 1] = up


def gate_up(order, inputs, gate_weight, up_weight, width, keep, send, after):
    slots, depth = inputs.shape
    quarter = gate_weight.shape[0] // 4
    gate_weight = gate_weight.reshape(4, quarter, depth)
    up_weight = up_weight.reshape(4, quarter, depth)
    base = 0 if keep is not None else 2
    chunks = [chunk for chunk in (keep, send) if chunk is not None]
    count = len(chunks)

    def place(s, order):
        return (order[base + s], chunks[0] if count == 1 else jnp.where(s < 2, chunks[0], chunks[1]), 0)

    weight_spec = pl.BlockSpec((None, width, depth), place)
    out_specs = [
        pl.BlockSpec(
            (1, 2, slots, width),
            lambda s, order, index=index: (jnp.clip(s - 2 * index, 0, 1), 0, 0, 0),
        )
        for index in range(count)
    ]
    return pl.pallas_call(
        functools.partial(gate_up_kernel, count),
        grid_spec=pltpu.PrefetchScalarGridSpec(
            num_scalar_prefetch=1,
            grid=(2 * count,),
            in_specs=[
                pl.BlockSpec((slots, depth), lambda s, order: (0, 0)),
                weight_spec,
                weight_spec,
            ]
            + [pl.BlockSpec(memory_space=pl.ANY)] * len(after),
            out_specs=out_specs,
        ),
        out_shape=[jax.ShapeDtypeStruct((2, 2, slots, width), bf16)] * count,
        compiler_params=params(41),
        cost_estimate=pl.CostEstimate(
            flops=32 * count * slots * depth * width,
            bytes_accessed=32 * count * width * depth,
            transcendentals=0,
        ),
        name=f"gate_up_{chunks[-1] + (send is None)}",
    )(order, inputs, gate_weight, up_weight, *after)


def down_kernel(count, pack, has_old, order_ref, place_ref, *refs):
    pieces, down_ref, rest = refs[:count], refs[count], refs[count + 1 :]
    old, new = rest[:3] if has_old else (), rest[3 * has_old :]
    packed_refs = ()
    if pack:
        packed_refs, new = new[:-3], new[-3:]
    step = pl.program_id(0)

    @pl.when(step == 0)
    def _():
        for index, ref in enumerate(new):
            ref[...] = old[index][...] if old else jnp.zeros_like(ref)

    out_ref, gram_ref, square_ref = new
    weight = down_ref[...]
    wide = weight.astype(f32)
    square_ref[...] += jnp.sum((wide * wide).reshape(-1, 8, wide.shape[1]), axis=0)
    for index, ref in enumerate(pieces):

        @pl.when(step == index)
        def _(ref=ref, index=index):
            values = ref[...]
            out_ref[...] += mm(values, weight)
            gram_ref[...] += mm(values, values, NT)
            if pack and index == len(pieces) - 1:
                dp_count, tensor_count = pack
                columns = out_ref.shape[1]
                lanes = columns // (dp_count * tensor_count)
                group = columns // dp_count
                gram = gram_ref[...]
                rolled = pltpu.roll(out_ref[...], lax.rem(columns - place_ref[0] * group, columns), 1)
                for ahead in range(dp_count):
                    parts = [
                        rolled[:, ahead * group + part * lanes : ahead * group + (part + 1) * lanes]
                        for part in range(tensor_count)
                    ]
                    for aside in range(tensor_count):
                        target = lax.rem(place_ref[1] + aside, tensor_count)
                        piece = parts[0]
                        for part in range(1, tensor_count):
                            piece = jnp.where(target == part, parts[part], piece)
                        packed_refs[ahead * tensor_count + aside][...] = jnp.concatenate(
                            [gram, piece], axis=1
                        ).astype(bf16)


def down(order, place, pieces, down_weight, first, older, pack=None):
    slots, width = pieces[0].shape
    columns = down_weight.shape[1]
    down_weight = down_weight.reshape(-1, width, columns)

    def fixed(shape):
        return pl.BlockSpec(shape, lambda s, order, place: (0,) * len(shape))

    shapes = [(slots, columns), (slots, slots), (8, columns)]
    out_shape = [jax.ShapeDtypeStruct(shape, f32) for shape in shapes]
    if pack:
        parts = pack[0] * pack[1]
        packed = (slots, slots + columns // parts)
        out_shape = [jax.ShapeDtypeStruct(packed, bf16)] * parts + out_shape
    return pl.pallas_call(
        functools.partial(down_kernel, len(pieces), pack, bool(older)),
        grid_spec=pltpu.PrefetchScalarGridSpec(
            num_scalar_prefetch=2,
            grid=(len(pieces),),
            in_specs=[fixed((slots, width))] * len(pieces)
            + [pl.BlockSpec((None, width, columns), lambda s, order, place: (order[first + s], 0, 0))]
            + [fixed(value.shape) for value in older],
            out_specs=[fixed(value.shape) for value in out_shape],
        ),
        out_shape=out_shape,
        compiler_params=params(20),
        cost_estimate=pl.CostEstimate(
            flops=8 * len(pieces) * slots * width * columns,
            bytes_accessed=8 * len(pieces) * width * columns,
            transcendentals=0,
        ),
        name=f"down_{first}",
    )(order, place, *pieces, down_weight, *older)


def route_kernel(blocks, tensor_count, kept_ref, place_ref, *refs):
    infos = [refs[0][block] for block in range(blocks)]
    hot_ref, turned_ref, gates_ref, wide_ref = refs[-4:]
    count = infos[0].shape[1]
    slots = blocks * CAP
    zero = jnp.zeros((CAP, count), f32)
    rows = lax.broadcasted_iota(jnp.int32, (CAP, count), 0).astype(f32)
    routed = []
    for block in range(blocks):
        first, second = infos[block][0:1, :], infos[block][1:2, :]
        delta = infos[block][3:4, :] - infos[block][2:3, :]
        share_first = 1.0 / (1.0 + jnp.exp(delta))
        share_second = 1.0 / (1.0 + jnp.exp(-delta))
        routed.append((first, second, share_first, share_second) + block_slots(first, second))
    for back in range(blocks):
        for aside in range(tensor_count):
            expert = lax.rem(place_ref[0] + blocks - back, blocks) * tensor_count
            expert = expert + lax.rem(place_ref[1] + tensor_count - aside, tensor_count)
            kept = jnp.zeros((), jnp.int32)
            for index in range(kept_ref.shape[0]):
                kept = kept | (kept_ref[index] == expert).astype(jnp.int32)
            kept, expert = kept.astype(f32), expert.astype(f32)
            for shift in range(blocks):
                block = (back + shift) % blocks
                first, second, share_first, share_second, rank_first, rank_second = routed[block]
                hit_first = (first == expert) & (rank_first == rows)
                hit_second = (second == expert) & (rank_second == rows)
                gate = jnp.sum(
                    jnp.where(hit_first, share_first, zero) + jnp.where(hit_second, share_second, zero),
                    axis=1,
                    keepdims=True,
                )
                row = (back * tensor_count + aside) * slots + shift * CAP
                for other in range(blocks):
                    wide_ref[row : row + CAP, other * count : (other + 1) * count] = (
                        (hit_first | hit_second).astype(f32) if other == block else zero
                    )
                gates_ref[row : row + CAP, 0:1] = gate * kept
                gates_ref[row : row + CAP, 1:2] = gate * (1.0 - kept)
    hot_ref[...] = wide_ref[...].astype(bf16)
    turned_ref[...] = wide_ref[...].T.astype(bf16)


def solve_kernel(ridge, slots, own_ref, hot_ref, turned_ref, gates_ref, square_ref, *refs):
    packed_refs, (base_ref, zero_ref, one_ref, sums_ref) = refs[:E], refs[E:]
    hot, turned = hot_ref[...], turned_ref[...]
    kept, dropped = gates_ref[:, 0:1], gates_ref[:, 1:2]
    values = jnp.concatenate([packed_refs[e][:, slots:].astype(f32) for e in range(E)], axis=0)
    lanes = values.shape[1]
    both = mm_wide(turned, jnp.concatenate([dropped * values, kept * values], axis=1))
    base, output = both[:, :lanes], both[:, lanes:]

    def apply(field):
        spread = kept * mm_wide(hot, field)
        mixed = jnp.concatenate(
            [
                mm_wide(packed_refs[e][:, :slots], spread[e * slots : (e + 1) * slots])
                for e in range(E)
            ],
            axis=0,
        )
        return mm_wide(turned, kept * mixed)

    curved = apply(base)
    zero = curved - ridge * output
    one = apply(zero)
    base_ref[...] = base
    zero_ref[...] = zero
    one_ref[...] = one
    norm = jnp.sum(base * (curved - 2.0 * ridge * output))
    square = jnp.sum(square_ref[...]) * own_ref[0]
    lane = lax.broadcasted_iota(jnp.int32, sums_ref.shape[1:], 1)
    sums = jnp.where(lane == 0, norm + ridge * ridge * square, 0.0)
    for index, value in enumerate((jnp.sum(zero * zero), jnp.sum(zero * one), jnp.sum(one * one))):
        sums = jnp.where(lane == index + 1, value, sums)
    for part in range(sums_ref.shape[0]):
        sums_ref[part] = sums


def finish_kernel(ridge, blocks, copies, place_ref, base_ref, zero_ref, one_ref, sums_ref, out_ref):
    sums = jnp.sum(sums_ref[...], axis=0)[0:1, :]
    norm, zero_zero = sums[:, 0:1], sums[:, 1:2]
    zero_one, one_one = sums[:, 2:3], sums[:, 3:4]
    step = norm / (zero_zero + ridge * norm)
    left = 1.0 - step * ridge
    new = left * left * norm - 2.0 * left * step * zero_zero + step * step * zero_one
    ratio = new / norm
    grown = left + ratio
    image = grown * grown * zero_zero - 2.0 * grown * step * zero_one + step * step * one_one
    later = new / (image + ridge * (new + ratio * ratio * norm))
    field = base_ref[...] - (step + later * grown) * zero_ref[...] + (later * step) * one_ref[...]
    rows = field.shape[0] // blocks
    sideways = field.T.astype(bf16)
    for back in range(blocks):
        target = lax.rem(place_ref[0] + blocks - back, blocks) * copies
        for copy in range(copies):
            out_ref[target + copy] = sideways[:, back * rows : (back + 1) * rows]


def join_kernel(pieces_ref, out_ref):
    rows = jnp.concatenate([pieces_ref[part].astype(f32) for part in range(pieces_ref.shape[0])], axis=0)
    out_ref[...] = rows.T


def single(kernel, out_shape, in_specs, mib, name, scratch=()):
    many = isinstance(out_shape, list)
    return pl.pallas_call(
        kernel,
        out_shape=out_shape,
        in_specs=in_specs,
        out_specs=[whole()] * len(out_shape) if many else whole(),
        scratch_shapes=list(scratch),
        compiler_params=params(mib),
        cost_estimate=LIGHT,
        name=name,
    )


def one_expert_each(tokens, routes, route_logits, kept_experts, gate_weight, up_weight, down_weight):
    dp_count = lax.axis_size("dp")
    tensor_count = lax.axis_size("tensor")
    parts = dp_count * tensor_count
    tok_rows, depth = tokens.shape
    units, columns = down_weight.shape
    slots = dp_count * CAP
    lanes = columns // parts
    width = units // 4 // CHUNKS
    ridge = ridge_share * 2.0 * tok_rows * dp_count / E
    dp_index = lax.axis_index("dp")
    tensor_index = lax.axis_index("tensor")
    col_index = lax.axis_index("col")
    own_expert = dp_index * tensor_count + tensor_index
    place = jnp.stack([dp_index, tensor_index])

    def beside(values):
        return lax.ppermute(values, "col", [(k, k ^ 1) for k in range(4)])

    def across(values):
        return lax.ppermute(values, "col", [(k, k ^ 2) for k in range(4)])

    def shifted(values, ahead, aside=0):
        if ahead == 0 and aside == 0:
            return values
        pairs = [
            (i * tensor_count + j, (i + ahead) % dp_count * tensor_count + (j + aside) % tensor_count)
            for i in range(dp_count)
            for j in range(tensor_count)
        ]
        return lax.ppermute(values, ("dp", "tensor"), pairs)

    shifts = [(ahead, aside) for ahead in range(dp_count) for aside in range(tensor_count)]
    upper = lax.pad(routes.T, jnp.int32(0), ((0, 2, 0), (0, 0, 0))).astype(f32)
    info = upper + lax.pad(route_logits.T, f32(0), ((2, 0, 0), (0, 0, 0)))
    picked = single(
        functools.partial(pick_kernel, dp_count, tensor_count),
        [jax.ShapeDtypeStruct((CAP + 8, depth), bf16)] * dp_count,
        [scalars(), whole(), whole()],
        16,
        "pick",
    )(place, info, tokens)
    arrived = [shifted(value, ahead) for ahead, value in enumerate(picked)]
    inputs, infos = single(
        stack_kernel,
        [jax.ShapeDtypeStruct((slots, depth), bf16), jax.ShapeDtypeStruct((dp_count, 4, tok_rows), f32)],
        [whole()] * dp_count,
        16,
        "stack",
    )(*arrived)

    gate_order = col_index ^ jnp.array([2, 0, 3, 1], jnp.int32)
    near_first = jnp.array([0, 2, 1, 3] * CHUNKS, jnp.int32)
    down_order = (col_index ^ near_first) * CHUNKS + jnp.arange(4 * CHUNKS, dtype=jnp.int32) // 4

    def products(keep, send, after=()):
        return gate_up(gate_order, inputs, gate_weight, up_weight, width, keep, send, after)

    last = CHUNKS - 1
    keeps, nears, pairs, fars, owns = [], [], [], [], []

    def activate(chunk, after):
        far = lax.optimization_barrier((fars[chunk], *after))[0] if after else fars[chunk]
        total = keeps[chunk][1].astype(f32) + nears[chunk][1].astype(f32) + far.astype(f32)
        owns.append((jax.nn.silu(total[0]) * total[1]).astype(bf16))

    nears.append(beside(products(None, 0)[0]))
    for chunk in range(CHUNKS):
        after = [keeps[-1]] if chunk else []
        if chunk >= 2:
            activate(chunk - 2, [pairs[chunk - 1]])
            after.extend([pairs[chunk - 1], owns[chunk - 2]])
        if chunk < last:
            keep, send = products(chunk, chunk + 1, after)
            nears.append(beside(send))
        else:
            (keep,) = products(chunk, None, after)
        keeps.append(keep)
        pairs.append((keep[0].astype(f32) + nears[chunk][0].astype(f32)).astype(bf16))
        fars.append(across(pairs[-1]))
    older, olders, queue, counts = (), [], [], []
    for chunk in range(CHUNKS):
        if chunk >= len(owns):
            after = [pairs[last]]
            if chunk >= 2:
                after.append(olders[chunk - 2][2])
            activate(chunk, after)
        own = owns[chunk]
        other = across(own)
        if chunk + 2 <= last:
            own, other = lax.optimization_barrier((own, other, pairs[last]))[:2]
        queue.extend((own, other, beside(own), beside(other)))
        done = sum(counts)
        if chunk < last - 1:
            counts.append(4)
        elif chunk == last - 1:
            counts.append(3)
        else:
            counts.extend([4, 1])
        for count in counts[len(olders) :]:
            pack = (dp_count, tensor_count) if done + count == 4 * CHUNKS else None
            older = down(down_order, place, queue[done : done + count], down_weight, done, older, pack)
            olders.append(older)
            done += count
    packed, (_, _, square) = older[:parts], older[parts:]
    spread = [shifted(value, *shift) for value, shift in zip(packed, shifts)]

    total_slots, total_tokens = E * slots, dp_count * tok_rows
    hot, turned_hot, gates = single(
        functools.partial(route_kernel, dp_count, tensor_count),
        [
            jax.ShapeDtypeStruct((total_slots, total_tokens), bf16),
            jax.ShapeDtypeStruct((total_tokens, total_slots), bf16),
            jax.ShapeDtypeStruct((total_slots, 2), f32),
        ],
        [scalars(), scalars(), whole(), pl.BlockSpec(memory_space=pl.ANY)],
        24,
        "route",
        [pltpu.VMEM((total_slots, total_tokens), f32)],
    )(kept_experts, place, infos, square)
    is_kept = jnp.any(kept_experts == own_expert).astype(f32).reshape(1)
    field = jax.ShapeDtypeStruct((total_tokens, lanes), f32)
    everyone = parts * lax.axis_size("col")
    base, zero, one, sums = single(
        functools.partial(solve_kernel, ridge, slots),
        [field, field, field, jax.ShapeDtypeStruct((everyone, 1, 128), f32)],
        [scalars()] + [whole()] * (4 + E),
        40,
        "solve",
    )(is_kept, hot, turned_hot, gates, square, *spread)
    sums = lax.all_to_all(sums, ("dp", "tensor", "col"), split_axis=0, concat_axis=0, tiled=True)

    home = single(
        functools.partial(finish_kernel, ridge, dp_count, tensor_count),
        jax.ShapeDtypeStruct((parts, lanes, tok_rows), bf16),
        [scalars()] + [whole()] * 4,
        16,
        "finish",
    )(place, base, zero, one, sums)
    home = lax.all_to_all(home, ("dp", "tensor"), split_axis=0, concat_axis=0, tiled=True)
    return single(
        join_kernel,
        jax.ShapeDtypeStruct((tok_rows, columns), f32),
        [whole()],
        16,
        "join",
    )(home)


def spread_copies(values, experts, held_count, copies):
    old_shape = values.shape
    grouped = values.reshape((experts // held_count, 1, held_count) + old_shape[1:])
    widened = jnp.broadcast_to(grouped, (experts // held_count, copies, held_count) + old_shape[1:])
    return widened.reshape((experts // held_count * copies, held_count) + old_shape[1:])


def expert_major(returned, experts, held_count, copies):
    old_shape = returned.shape
    grouped = returned.reshape((experts // held_count, copies, held_count) + old_shape[2:])
    merged = jnp.sum(grouped, axis=1)
    return merged.reshape((experts * old_shape[2],) + old_shape[3:])


def exact_product(left, right, contract):
    return lax.dot_general(
        left, right, contract, precision=top_precision, preferred_element_type=jnp.float32
    )


def general(tokens, routes, route_logits, kept_experts, gate_weight, up_weight, down_weight):
    dp_count = lax.axis_size("dp")
    tensor_count = lax.axis_size("tensor")
    held_count = max(1, E // dp_count)
    copies = max(1, dp_count // E)
    tok_rows = tokens.shape[0]
    piece_rows = gate_weight.shape[0]
    FF = piece_rows * dp_count * tensor_count // E
    slot_total = E * CAP
    device_rank = lax.axis_index("dp") * tensor_count + lax.axis_index("tensor")
    own_expert = device_rank * piece_rows // FF
    own_group = own_expert % held_count
    expert_ids = jnp.arange(E, dtype=jnp.int32)
    kept_table = jnp.any(kept_experts[:, None] == expert_ids[None, :], axis=0).astype(jnp.float32)
    own_kept = jnp.sum(jnp.where(expert_ids == own_expert, kept_table, 0.0))
    route_experts = routes.reshape(-1)
    route_onehot = (route_experts[:, None] == expert_ids[None, :]).astype(jnp.int32)
    route_rank = jnp.sum((jnp.cumsum(route_onehot, axis=0) - route_onehot) * route_onehot, axis=1)
    route_slot = route_experts * CAP + route_rank
    gate_probs = jax.nn.softmax(route_logits, axis=-1).reshape(-1)
    route_kept = jnp.sum(route_onehot.astype(jnp.float32) * kept_table[None, :], axis=1)
    slot_match = (jnp.arange(slot_total, dtype=jnp.int32)[:, None] == route_slot[None, :]).astype(
        jnp.float32
    )
    pick_tokens = slot_match.reshape(slot_total, tok_rows, 2).sum(axis=2)
    kept_weights = (
        (slot_match * (gate_probs * route_kept)[None, :])
        .reshape(slot_total, tok_rows, 2)
        .sum(axis=2)
    )
    dropped_weights = (
        (slot_match * (gate_probs * (1.0 - route_kept))[None, :])
        .reshape(slot_total, tok_rows, 2)
        .sum(axis=2)
    )
    by_expert = jnp.dot(
        pick_tokens.astype(jnp.bfloat16), tokens, preferred_element_type=jnp.float32
    ).astype(jnp.bfloat16)
    outgoing = spread_copies(by_expert.reshape(E, CAP, -1), E, held_count, copies)
    chosen = lax.dynamic_index_in_dim(
        lax.all_to_all(outgoing, "dp", split_axis=0, concat_axis=0, tiled=True),
        own_group,
        1,
        keepdims=False,
    )
    contract = (((2,), (1,)), ((), ()))
    gate_part = lax.dot_general(chosen, gate_weight, contract, preferred_element_type=jnp.float32)
    up_part = lax.dot_general(chosen, up_weight, contract, preferred_element_type=jnp.float32)
    gate_part, up_part = (gate_part, up_part)
    gate_sum, up_sum = (
        lax.psum(gate_part.astype(jnp.bfloat16), "col").astype(jnp.float32),
        lax.psum(up_part.astype(jnp.bfloat16), "col").astype(jnp.float32),
    )
    hidden = (jax.nn.silu(gate_sum) * up_sum).astype(jnp.bfloat16)
    expert_out = lax.dot_general(
        hidden, down_weight, (((2,), (0,)), ((), ())), preferred_element_type=jnp.float32
    ).astype(jnp.bfloat16)
    hidden_wide = hidden.astype(jnp.float32)
    group_mask = (jnp.arange(held_count) == own_group)[None, :, None, None]
    placed = jnp.where(group_mask, expert_out[:, None], jnp.zeros((), jnp.bfloat16))
    returned = lax.all_to_all(placed, "dp", split_axis=0, concat_axis=0, tiled=True)
    slot_values = expert_major(returned.astype(jnp.float32), E, held_count, copies)
    dropped_part = jnp.dot(dropped_weights.T, slot_values, precision=top_precision)
    dropped = lax.psum(dropped_part, "tensor")
    ridge_weight = ridge_share * 2.0 * tok_rows * dp_count / E

    def apply_backward(image_tokens):
        slot_image = jnp.dot(kept_weights, image_tokens, precision=top_precision)
        outgoing_image = spread_copies(slot_image.reshape(E, CAP, -1), E, held_count, copies)
        arrived = lax.all_to_all(outgoing_image, "dp", split_axis=0, concat_axis=0, tiled=True)
        chosen = lax.dynamic_index_in_dim(arrived, own_group, 1, keepdims=False)
        return exact_product(hidden_wide, chosen, (((0, 1), (0, 1)), ((), ())))

    def total_norm(values):
        return lax.psum(jnp.sum(values * values), ("dp", "tensor", "col"))

    base_down = down_weight.astype(jnp.float32)
    residual = apply_backward(dropped) - ridge_weight * own_kept * base_down
    res_norm = total_norm(residual)
    direction = residual
    leftover = dropped
    for turn_index in range(ITERS):
        slot_part = exact_product(hidden_wide, direction, (((2,), (0,)), ((), ())))
        placed_part = jnp.where(group_mask, slot_part[:, None], 0.0)
        came_back = lax.all_to_all(placed_part, "dp", split_axis=0, concat_axis=0, tiled=True)
        image_part = jnp.dot(
            kept_weights.T, expert_major(came_back, E, held_count, copies), precision=top_precision
        )
        image_tokens = lax.psum(image_part, "tensor")
        first_copy = (lax.axis_index("tensor") == 0).astype(jnp.float32)
        local_term = first_copy * jnp.sum(image_tokens * image_tokens) + ridge_weight * jnp.sum(
            direction * direction
        )
        curvature = lax.psum(local_term, ("dp", "tensor", "col"))
        step_size = res_norm / curvature
        leftover = leftover - step_size * image_tokens
        if turn_index + 1 < ITERS:
            curved = apply_backward(image_tokens) + ridge_weight * direction
            residual = residual - step_size * curved
            next_norm = total_norm(residual)
            direction = residual + next_norm / res_norm * direction
            res_norm = next_norm
    return leftover


def shards(*arrays):
    sizes = [lax.axis_size(axis) for axis in ("dp", "tensor", "col")]
    if sizes[0] * sizes[1] == E and sizes[2] == 4 and ITERS == 2:
        return one_expert_each(*arrays)
    return general(*arrays)


def solution(mesh):
    placed = (
        P("dp", "col"),
        P("dp", None),
        P("dp", None),
        P(),
        P(("dp", "tensor"), "col"),
        P(("dp", "tensor"), "col"),
        P(("dp", "tensor"), "col"),
    )
    return jax.shard_map(
        shards, mesh=mesh, in_specs=placed, out_specs=P("dp", "col"), check_vma=False
    )
```
